32 devices in a mesh: row: 8 (over y, x, core), col: 4 (over z).
Axes of the slice: x: 2, y: 2, z: 4, core: 2. Of those that a mesh axis runs over, the one named last changes fastest.
Arguments:
- streams: bfloat16 [4, 8192, 2048], P(None, 'row', 'col')
- segments: int32 [8, 1024], P('row'), may hold values from 0 to 7, never falling along the last dimension, each value on 1 to 512 neighbouring positions
- attention_in: float32 [3, 2048, 2048], P(None, 'row', 'col'), may hold values from -0.125 to 0.125
- attention_out: float32 [2048, 2048], P('col', 'row'), may hold values from -0.75 to 0.75
- gate_up: float32 [2, 2048, 8192], P(None, 'row', 'col'), may hold values from -0.125 to 0.125
- down_weights: float32 [8192, 2048], P('col', 'row'), may hold values from -0.0625 to 0.0625
- hyper_mix: float32 [2, 4, 6], replicated
- moment_attention_in: float32 [3, 2048, 2048], P(None, 'row', 'col'), may hold values from -160 to 160
- moment_attention_out: float32 [2048, 2048], P('col', 'row'), may hold values from -160 to 160
- moment_gate_up: float32 [2, 2048, 8192], P(None, 'row', 'col'), may hold values from -160 to 160
- moment_down_weights: float32 [8192, 2048], P('col', 'row'), may hold values from -160 to 160
- moment_hyper_mix: float32 [2, 4, 6], replicated, may hold values from -12288 to 12288
- average_attention_in: float32 [3, 2048, 2048], P(None, 'row', 'col'), may hold values from -0.125 to 0.125
- average_attention_out: float32 [2048, 2048], P('col', 'row'), may hold values from -0.75 to 0.75
- average_gate_up: float32 [2, 2048, 8192], P(None, 'row', 'col'), may hold values from -0.125 to 0.125
- average_down_weights: float32 [8192, 2048], P('col', 'row'), may hold values from -0.0625 to 0.0625
- average_hyper_mix: float32 [2, 4, 6], replicated, may hold values from -3 to 3
- cotangent: bfloat16 [4, 8192, 2048], P(None, 'row', 'col')
Outputs:
- out_streams: bfloat16 [4, 8192, 2048], P(None, 'row', 'col')
- grad_streams: float32 [4, 8192, 2048], P(None, 'row', 'col')
- new_attention_in: float32 [3, 2048, 2048], P(None, 'row', 'col')
- new_moment_attention_in: float32 [3, 2048, 2048], P(None, 'row', 'col')
- new_average_attention_in: float32 [3, 2048, 2048], P(None, 'row', 'col')
- new_attention_out: float32 [2048, 2048], P('col', 'row')
- new_moment_attention_out: float32 [2048, 2048], P('col', 'row')
- new_average_attention_out: float32 [2048, 2048], P('col', 'row')
- new_gate_up: float32 [2, 2048, 8192], P(None, 'row', 'col')
- new_moment_gate_up: float32 [2, 2048, 8192], P(None, 'row', 'col')
- new_average_gate_up: float32 [2, 2048, 8192], P(None, 'row', 'col')
- new_down_weights: float32 [8192, 2048], P('col', 'row')
- new_moment_down_weights: float32 [8192, 2048], P('col', 'row')
- new_average_down_weights: float32 [8192, 2048], P('col', 'row')
- new_hyper_mix: float32 [2, 4, 6], replicated
- new_moment_hyper_mix: float32 [2, 4, 6], replicated
- new_average_hyper_mix: float32 [2, 4, 6], replicated
The draws below stay inside these ranges and needn't reach their ends.
Inputs may be any that keep to these rules, and one draw needn't show every extreme that they name: `segments`: row s holds the document numbers of sequence s: 8 documents numbered 0 to 7 in order, each 1 to 512 tokens long, one of them exactly 512.
All inputs are finite; a program needn't handle non-finite values.
Results may differ from the reference program's by a relative error of at most 0.019.
Values may be sent and summed in bfloat16 or wider, within the bound.
A program may use at most 208 MiB of HBM per device.

```python
import math
import jax
import jax.numpy as jnp
import numpy as np
from jax import lax

D = 2048
HEADS = 16
HEAD_DIM = 128
FF = 8192
STREAMS = 4
DOCS = 8
STEP = 8
TOK_DEV = 1024
SEQ = 1024
SEQS = 8
TOKENS = 8192
N_ROW = 8


def draw_streams(key, part):
    key = jax.random.fold_in(key, 11)
    shape = (STREAMS, TOKENS, D)
    place = jnp.arange(D, dtype=jnp.float32) / (D - 1)
    base = jax.random.normal(key, shape, jnp.float32)
    scale = 0.5 + place
    return (base * scale).astype(jnp.bfloat16)


def draw_cotangent(key, part):
    key = jax.random.fold_in(key, 23)
    shape = (STREAMS, TOKENS, D)
    place = jnp.arange(D, dtype=jnp.float32) / (D - 1)
    token_place = (jnp.arange(TOKENS, dtype=jnp.float32) / (TOKENS - 1))[:, None]
    base = jax.random.normal(key, shape, jnp.float32)
    scale = (0.5 + token_place) * (0.5 + place)
    return (base * scale).astype(jnp.bfloat16)


def draw_hyper_mix(key, part):
    key = jax.random.fold_in(key, 37)
    shape = (2, STREAMS, STREAMS + 2)
    first, second, third = jax.random.split(key, 3)
    column = jnp.arange(STREAMS + 2)[None, None, :]
    stream_index = jnp.arange(STREAMS)[None, :, None]
    entry_in = jax.random.uniform(first, shape, jnp.float32, 0.2, 0.8)
    outward = jax.random.uniform(third, shape, jnp.float32, 0.5, 1.5)
    noise = 0.25 * jax.random.normal(second, shape, jnp.float32)
    across = (column - 1 == stream_index).astype(jnp.float32) + noise
    return jnp.where(column == 0, entry_in, jnp.where(column == STREAMS + 1, outward, across))


def block_levels(rng, extent, cuts, smallest, largest):
    gain = 1.0
    for axis_at, shards_of in cuts:
        steps = jax.random.uniform(jax.random.fold_in(jax.random.fold_in(rng, 6), axis_at), (shards_of,), jnp.float32, smallest / len(cuts), largest / len(cuts))
        gain = gain * jnp.repeat(jnp.exp(steps), extent[axis_at] // shards_of).reshape((-1,) + (1,) * (len(extent) - 1 - axis_at))
    return gain


def length_profile(amount, total, most, skew):
    loads = [(1 << 20) // math.isqrt(grade ** skew) + 1 for grade in range(2, amount + 1)]
    surplus, holding = total - most - (amount - 1), [1] * (amount - 1)
    while surplus > 0:
        candidates = [i for i in range(amount - 1) if holding[i] < most]
        whole, left = sum([loads[i] for i in candidates]), surplus
        for i in candidates:
            more = min(most - holding[i], max(1, left * loads[i] // whole), surplus)
            holding[i] = holding[i] + more
            surplus = surplus - more
    return np.array([most] + holding)


def ragged_sizes(own_key, amount, total, limit, skew):
    if amount == 2:
        one = jax.random.randint(own_key, (), max(1, total - limit), min(limit, total - 1) + 1)
        return jnp.stack([one, total - one])
    tallies = jnp.asarray(length_profile(amount, total, limit, skew), jnp.int32)
    twos = (amount - 1) // 2
    donor, taker = tallies[1:1 + 2 * twos:2], tallies[2:2 + 2 * twos:2]
    margin = jnp.minimum(donor - 1, limit - taker)
    shifted = jax.random.randint(jax.random.fold_in(own_key, 1), (twos,), 0, 1 << 20) % (margin + 1)
    tallies = tallies.at[1:1 + 2 * twos:2].set(donor - shifted).at[2:2 + 2 * twos:2].set(taker + shifted)
    return tallies[jax.random.permutation(jax.random.fold_in(own_key, 2), amount)]


def centred(key, extent, width, reach, cuts=(), kind=jnp.bfloat16):
    values = jax.random.normal(key, extent, jnp.float32) * width
    if len(cuts) > 0:
        values = block_levels(key, extent, cuts, -0.22, 0.18) * values
    return jnp.clip(values, min=-reach, max=reach).astype(kind)


def setup_inputs(seed: int = 0) -> dict:
    key_of = jax.random.split(jax.random.key(seed), 19)
    return {
        "streams": draw_streams(jax.random.fold_in(key_of[18], 71), 0),
        "segments": jax.vmap(lambda own: jnp.searchsorted(jnp.cumsum(ragged_sizes(own, DOCS, SEQ, SEQ // 2, 2)), jnp.arange(SEQ), side="right"))(jax.random.split(key_of[1], SEQS)).reshape((SEQS, SEQ)).astype(jnp.int32),
        "attention_in": centred(key_of[2], (3, D, D), D ** -0.5, 0.125, ((1, 8), (2, 4)), jnp.float32),
        "attention_out": centred(key_of[3], (D, D), (D // 32) ** -0.5, 0.75, ((0, 4), (1, 8)), jnp.float32),
        "gate_up": centred(key_of[4], (2, D, FF), D ** -0.5, 0.125, ((1, 8), (2, 4)), jnp.float32),
        "down_weights": centred(key_of[5], (FF, D), FF ** -0.5, 0.0625, ((0, 4), (1, 8)), jnp.float32),
        "hyper_mix": draw_hyper_mix(jax.random.fold_in(key_of[18], 71), 0),
        "moment_attention_in": centred(key_of[7], (3, D, D), (0.3 * (TOK_DEV * N_ROW) ** 0.5), 160.0, ((1, 8), (2, 4)), jnp.float32),
        "moment_attention_out": centred(key_of[8], (D, D), (0.3 * (TOK_DEV * N_ROW) ** 0.5), 160.0, ((0, 4), (1, 8)), jnp.float32),
        "moment_gate_up": centred(key_of[9], (2, D, FF), (0.3 * (TOK_DEV * N_ROW) ** 0.5), 160.0, ((1, 8), (2, 4)), jnp.float32),
        "moment_down_weights": centred(key_of[10], (FF, D), (0.3 * (TOK_DEV * N_ROW) ** 0.5), 160.0, ((0, 4), (1, 8)), jnp.float32),
        "moment_hyper_mix": centred(key_of[11], (2, STREAMS, STREAMS + 2), (0.5 * (TOK_DEV * N_ROW * D) ** 0.5), 12288.0, (), jnp.float32),
        "average_attention_in": centred(key_of[12], (3, D, D), D ** -0.5, 0.125, ((1, 8), (2, 4)), jnp.float32),
        "average_attention_out": centred(key_of[13], (D, D), (D // 32) ** -0.5, 0.75, ((0, 4), (1, 8)), jnp.float32),
        "average_gate_up": centred(key_of[14], (2, D, FF), D ** -0.5, 0.125, ((1, 8), (2, 4)), jnp.float32),
        "average_down_weights": centred(key_of[15], (FF, D), FF ** -0.5, 0.0625, ((0, 4), (1, 8)), jnp.float32),
        "average_hyper_mix": centred(key_of[16], (2, STREAMS, STREAMS + 2), 0.5, 3.0, (), jnp.float32),
        "cotangent": draw_cotangent(jax.random.fold_in(key_of[18], 71), 0),
    }


HIGH = lax.Precision.HIGHEST
EPSILON = 1e-05
MASKED = -1e+30
MOMENTUM = 0.9
DECAY = 0.01

@jax.custom_vjp
def low(v):
    return lax.optimization_barrier(v.astype(jnp.bfloat16)).astype(jnp.float32)

@jax.custom_vjp
def low_back(v):
    return v

def low_keep(v):
    return (low(v), None)

def low_pass(kept, grad):
    return (grad,)

def back_keep(v):
    return (v, None)

def back_low(kept, grad):
    return (low(grad),)
low.defvjp(low_keep, low_pass)
low_back.defvjp(back_keep, back_low)

def matmul(left, right):
    return jnp.dot(left, right, precision=HIGH, preferred_element_type=jnp.float32)

def normalize(values):
    center = values - lax.optimization_barrier(jnp.mean(values, -1, keepdims=True))
    spread = lax.optimization_barrier(jnp.mean(center * center, -1, keepdims=True))
    return center * lax.rsqrt(spread + EPSILON)

def rope_tables(segments):
    length = segments.shape[-1]
    index = jnp.arange(length, dtype=jnp.int32)
    before = jnp.concatenate([jnp.full(segments.shape[:-1] + (1,), -1, jnp.int32), segments[..., :-1]], -1)
    starts = jnp.where(segments != before, index, 0).astype(jnp.int32)
    places = index - lax.cummax(starts, axis=segments.ndim - 1)
    rates = 10000.0 ** (-2.0 * jnp.arange(HEAD_DIM // 2).astype(jnp.float32) / HEAD_DIM)
    angle = places[..., None].astype(jnp.float32) * rates
    angle = jnp.concatenate([angle, angle], -1)[..., None, :]
    return (jnp.cos(angle), jnp.sin(angle))

def rotate(values, cosine, sine):
    half = values.shape[-1] // 2
    turned = jnp.concatenate([-values[..., half:], values[..., :half]], -1)
    return values * cosine + turned * sine

def attend(packed):
    queries, key_heads, value_heads, segment_row = packed
    index = jnp.arange(segment_row.shape[0])
    raw = jnp.einsum('qhe,khe->hqk', queries, key_heads, precision=HIGH) * HEAD_DIM ** (-0.5)
    raw = low_back(raw)
    allowed = (segment_row[:, None] == segment_row[None, :]) & (index[None, :] <= index[:, None])
    scores = jnp.where(allowed[None], raw, MASKED)
    weights = jax.nn.softmax(scores, axis=-1)
    return jnp.einsum('hqk,khe->qhe', low(weights), value_heads, precision=HIGH)

def mix_in(streams, coeffs):
    return jnp.einsum('s,std->td', coeffs, streams, precision=HIGH)

def mix_out(streams, coeffs, branch):
    mixed = jnp.einsum('ij,itd->jtd', coeffs[:, 1:1 + STREAMS], streams, precision=HIGH)
    return mixed + coeffs[:, 1 + STREAMS][:, None, None] * branch[None]

def forward(streams, projections, output_rows, gate_rows, down_rows, mixings, cosine, sine, segments):
    projections = low(projections)
    output_rows = low(output_rows)
    gate_rows = low(gate_rows)
    down_rows = low(down_rows)
    first = low(normalize(mix_in(streams, mixings[0, :, 0])))
    shape = (SEQS, SEQ, HEADS, HEAD_DIM)
    queries = low(rotate(low_back(matmul(first, projections[0])).reshape(shape), cosine, sine))
    key_heads = low(rotate(low_back(matmul(first, projections[1])).reshape(shape), cosine, sine))
    value_heads = low(low_back(matmul(first, projections[2])).reshape(shape))
    attended = lax.map(jax.checkpoint(attend), (queries, key_heads, value_heads, segments))
    attended = low(low_back(attended.reshape(SEQS * SEQ, D)))
    branch = low_back(matmul(attended, output_rows))
    middle = mix_out(streams, mixings[0], branch)
    second = low(normalize(mix_in(middle, mixings[1, :, 0])))
    gate = low_back(matmul(second, gate_rows[0]))
    upper = low_back(matmul(second, gate_rows[1]))
    active = low(jax.nn.silu(gate) * upper)
    branch_two = low_back(matmul(active, down_rows))
    return mix_out(middle, mixings[1], branch_two)

def update(weight, grad, moment, average, rate):
    step_grad = grad + DECAY * weight
    moment_new = MOMENTUM * moment + step_grad
    weight_new = weight - rate * (step_grad + MOMENTUM * moment_new)
    return (weight_new, moment_new, average + (weight_new - average) / (STEP + 1))

def reference(streams, segments, attention_in, attention_out, gate_up, down_weights, hyper_mix, moment_attention_in, moment_attention_out, moment_gate_up, moment_down_weights, moment_hyper_mix, average_attention_in, average_attention_out, average_gate_up, average_down_weights, average_hyper_mix, cotangent):
    cosine, sine = rope_tables(segments)

    def layer(inputs, projections, output_rows, gate_rows, down_rows, mixings):
        return forward(inputs, projections, output_rows, gate_rows, down_rows, mixings, cosine, sine, segments)
    result, pullback = jax.vjp(layer, streams.astype(jnp.float32), attention_in, attention_out, gate_up, down_weights, hyper_mix)
    grads = pullback(cotangent.astype(jnp.float32))
    token_scale = TOKENS ** (-0.5)
    model_rate = D ** (-0.5) * token_scale
    first = update(attention_in, grads[1], moment_attention_in, average_attention_in, model_rate)
    second = update(attention_out, grads[2], moment_attention_out, average_attention_out, model_rate)
    third = update(gate_up, grads[3], moment_gate_up, average_gate_up, model_rate)
    fourth = update(down_weights, grads[4], moment_down_weights, average_down_weights, FF ** (-0.5) * token_scale)
    fifth = update(hyper_mix, grads[5], moment_hyper_mix, average_hyper_mix, 0.05 * (TOKENS * D) ** (-0.5))
    return (result.astype(jnp.bfloat16), grads[0], first[0], first[1], first[2], second[0], second[1], second[2], third[0], third[1], third[2], fourth[0], fourth[1], fourth[2], fifth[0], fifth[1], fifth[2])
```

```python
import jax
import jax.numpy as jnp
from jax import lax
from jax.sharding import PartitionSpec as P

D = 2048
HEAD_DIM = 128
FF = 8192
STEP = 8


EPSILON = 1e-05
MASKED = -1e30
MOMENTUM = 0.9
DECAY = 0.01


def rope_tables(segments):
    length = segments.shape[-1]
    index = jnp.arange(length, dtype=jnp.int32)
    before = jnp.concatenate(
        [jnp.full(segments.shape[:-1] + (1,), -1, jnp.int32), segments[..., :-1]], -1
    )
    starts = jnp.where(segments != before, index, 0)
    places = index - lax.cummax(starts, axis=segments.ndim - 1)
    rates = 10000.0 ** (-2.0 * jnp.arange(HEAD_DIM // 2).astype(jnp.float32) / HEAD_DIM)
    angle = places[..., None].astype(jnp.float32) * rates
    angle = jnp.concatenate([angle, angle], -1)[..., None, :]
    return (jnp.cos(angle), jnp.sin(angle))


def rotate(values, cosine, sine):
    half = values.shape[-1] // 2
    turned = jnp.concatenate([-values[..., half:], values[..., :half]], -1)
    return values * cosine + turned * sine


def unrotate(values, cosine, sine):
    scaled = values * sine
    half = values.shape[-1] // 2
    return values * cosine + jnp.concatenate([scaled[..., half:], -scaled[..., :half]], -1)


def weighted(coeffs, streams):
    total = coeffs[0] * streams[0]
    for index in range(1, len(streams)):
        total = total + coeffs[index] * streams[index]
    return total


def mix_out(streams, coeffs, branch):
    count = coeffs.shape[0]
    return [
        weighted(coeffs[:, 1 + j], streams) + coeffs[j, 1 + count] * branch for j in range(count)
    ]


def mix_back(coeffs, grad_after, grad_mixed):
    count = coeffs.shape[0]
    return [
        weighted(coeffs[i, 1 : 1 + count], grad_after) + coeffs[i, 0] * grad_mixed
        for i in range(count)
    ]


def mixing_grads(before, grad_mixed, grad_after, branch):
    rows = []
    for i, own in enumerate(before):
        row = [jnp.sum(own * grad_mixed)]
        row = row + [jnp.sum(own * after) for after in grad_after]
        row.append(jnp.sum(grad_after[i] * branch))
        rows.append(jnp.stack(row))
    return jnp.stack(rows)


def gather_columns(values):
    return lax.all_gather(values.astype(jnp.bfloat16), "col", axis=1, tiled=True)


def normalize_gather(mixed):
    sums, squares = lax.psum((jnp.sum(mixed, -1), jnp.sum(mixed * mixed, -1)), "col")
    center = sums / D
    spread = squares / D - center * center
    scale = lax.rsqrt(spread + EPSILON)
    normal = (mixed - center[:, None]) * scale[:, None]
    return (normal, scale, gather_columns(normal))


def norm_backward(grad_normal, normal, scale):
    sums, products = lax.psum((jnp.sum(grad_normal, -1), jnp.sum(grad_normal * normal, -1)), "col")
    inner = grad_normal - sums[:, None] / D - normal * (products[:, None] / D)
    return scale[:, None] * inner


def project_in(whole, weights):
    return jnp.einsum("tn,knw->ktw", whole, weights, preferred_element_type=jnp.float32)


def scatter_columns(partial_value):
    return lax.psum_scatter(
        partial_value.astype(jnp.bfloat16), "col", scatter_dimension=1, tiled=True
    ).astype(jnp.float32)


def project_out(active, weights):
    return scatter_columns(jnp.dot(active, weights, preferred_element_type=jnp.float32))


def back_out(whole, active, weights):
    weight_grad = lax.psum_scatter(
        jnp.einsum("tw,td->wd", active, whole, preferred_element_type=jnp.float32).astype(
            jnp.bfloat16
        ),
        "row",
        scatter_dimension=1,
        tiled=True,
    ).astype(jnp.float32)
    grad_active = jnp.einsum("tn,wn->tw", whole, weights, preferred_element_type=jnp.float32)
    return (grad_active, weight_grad)


def back_in(grads, whole, weights):
    weight_grad = lax.psum_scatter(
        jnp.einsum("td,ktw->kdw", whole, grads, preferred_element_type=jnp.float32).astype(
            jnp.bfloat16
        ),
        "row",
        scatter_dimension=1,
        tiled=True,
    ).astype(jnp.float32)
    partial_value = jnp.einsum("ktw,knw->tn", grads, weights, preferred_element_type=jnp.float32)
    return (scatter_columns(partial_value), weight_grad)


def block_scores(queries, key_heads, segment_row, start, block):
    length = key_heads.shape[0]
    index = jnp.arange(length)
    rows = lax.dynamic_slice_in_dim(index, start, block)
    own_docs = lax.dynamic_slice_in_dim(segment_row, start, block)
    allowed = (own_docs[:, None] == segment_row[None, :]) & (index[None, :] <= rows[:, None])
    part = lax.dynamic_slice_in_dim(queries, start, block, 0)
    raw = jnp.einsum("qhe,khe->hqk", part, key_heads, preferred_element_type=jnp.float32)
    raw = raw * queries.shape[-1] ** (-0.5)
    return (jnp.where(allowed[None], raw, MASKED), part)


def attend_forward(queries, key_heads, value_heads, segment_row):
    length = queries.shape[0]
    block = min(512, length)
    starts = jnp.arange(length // block) * block

    def one_block(start):
        scores, part = block_scores(queries, key_heads, segment_row, start, block)
        top = jnp.max(scores, -1, keepdims=True)
        expo = jnp.exp(scores - top)
        total = jnp.sum(expo, -1, keepdims=True)
        probs = (expo / total).astype(jnp.bfloat16)
        result = jnp.einsum("hqk,khe->qhe", probs, value_heads, preferred_element_type=jnp.float32)
        return (result, (top + jnp.log(total))[..., 0])

    results, log_totals = lax.map(one_block, starts)
    return (results.reshape(length, -1), log_totals)


def attend_back(queries, key_heads, value_heads, segment_row, log_totals, grad_result):
    length = queries.shape[0]
    block = min(512, length)
    starts = jnp.arange(length // block) * block
    factor = queries.shape[-1] ** (-0.5)

    def one_block(carry, packed):
        start, log_total = packed
        scores, part = block_scores(queries, key_heads, segment_row, start, block)
        probs = jnp.exp(scores - log_total[..., None])
        grad_part = lax.dynamic_slice_in_dim(grad_result, start, block, 0)
        grad_probs = jnp.einsum(
            "qhe,khe->hqk", grad_part, value_heads, preferred_element_type=jnp.float32
        )
        row_sum = jnp.sum(probs * grad_probs, -1, keepdims=True)
        grad_scores = (probs * (grad_probs - row_sum)).astype(jnp.bfloat16)
        grad_query = (
            jnp.einsum("hqk,khe->qhe", grad_scores, key_heads, preferred_element_type=jnp.float32)
            * factor
        )
        grad_keys = (
            carry[0]
            + jnp.einsum("hqk,qhe->khe", grad_scores, part, preferred_element_type=jnp.float32)
            * factor
        )
        grad_values = carry[1] + jnp.einsum(
            "hqk,qhe->khe",
            probs.astype(jnp.bfloat16),
            grad_part,
            preferred_element_type=jnp.float32,
        )
        return ((grad_keys, grad_values), grad_query)

    zeros = jnp.zeros(key_heads.shape, jnp.float32)
    (grad_keys, grad_values), grad_queries = lax.scan(
        one_block, (zeros, zeros), (starts, log_totals)
    )
    return (grad_queries.reshape(queries.shape), grad_keys, grad_values)


def forward(stream_values, hyper_mix, lowered, cosine, sine, segment_row):
    projections, output_rows, gate_rows, down_rows = lowered
    normal_one, scale_one, whole_one = normalize_gather(weighted(hyper_mix[0, :, 0], stream_values))
    projected = project_in(whole_one, projections)
    length = stream_values[0].shape[0]
    shape = (length, projected.shape[2] // HEAD_DIM, HEAD_DIM)
    queries = rotate(projected[0].reshape(shape), cosine, sine).astype(jnp.bfloat16)
    key_heads = rotate(projected[1].reshape(shape), cosine, sine).astype(jnp.bfloat16)
    value_heads = projected[2].reshape(shape).astype(jnp.bfloat16)
    attended, log_totals = attend_forward(queries, key_heads, value_heads, segment_row)
    attended = attended.astype(jnp.bfloat16)
    branch = project_out(attended, output_rows)
    middle = mix_out(stream_values, hyper_mix[0], branch)
    normal_two, scale_two, whole_two = normalize_gather(weighted(hyper_mix[1, :, 0], middle))
    gated = project_in(whole_two, gate_rows)
    active = (jax.nn.silu(gated[0]) * gated[1]).astype(jnp.bfloat16)
    branch_two = project_out(active, down_rows)
    final = mix_out(middle, hyper_mix[1], branch_two)
    kept = {
        "normal_one": normal_one,
        "scale_one": scale_one,
        "whole_one": whole_one,
        "queries": queries,
        "key_heads": key_heads,
        "value_heads": value_heads,
        "log_totals": log_totals,
        "attended": attended,
        "branch": branch,
        "middle": middle,
        "normal_two": normal_two,
        "scale_two": scale_two,
        "whole_two": whole_two,
        "gated": gated,
        "active": active,
        "branch_two": branch_two,
    }
    return (final, kept)


def update(weight, grad, moment, average, rate):
    step_grad = grad + DECAY * weight
    moment_new = MOMENTUM * moment + step_grad
    weight_new = weight - rate * (step_grad + MOMENTUM * moment_new)
    return (weight_new, moment_new, average + (weight_new - average) / (STEP + 1))


def per_device(
    streams,
    segments,
    attention_in,
    attention_out,
    gate_up,
    down_weights,
    hyper_mix,
    moment_attention_in,
    moment_attention_out,
    moment_gate_up,
    moment_down_weights,
    moment_hyper_mix,
    average_attention_in,
    average_attention_out,
    average_gate_up,
    average_down_weights,
    average_hyper_mix,
    cotangent,
):
    stream_values = [streams[i].astype(jnp.float32) for i in range(streams.shape[0])]
    cosine, sine = rope_tables(segments)
    cosine = cosine[0]
    sine = sine[0]
    segment_row = segments[0]
    lowered = tuple(
        lax.all_gather(weights.astype(jnp.bfloat16), "row", axis=1, tiled=True)
        for weights in (attention_in, attention_out, gate_up, down_weights)
    )
    projections, output_rows, gate_rows, down_rows = lowered
    final, kept = forward(stream_values, hyper_mix, lowered, cosine, sine, segment_row)
    count = hyper_mix.shape[1]
    mix_one = hyper_mix[0]
    mix_two = hyper_mix[1]
    grad_final = [cotangent[j].astype(jnp.float32) for j in range(count)]
    grad_branch_two = gather_columns(weighted(mix_two[:, 1 + count], grad_final))
    grad_active, grad_down = back_out(grad_branch_two, kept["active"], down_rows)
    gate = kept["gated"][0]
    upper = kept["gated"][1]
    sigma = jax.nn.sigmoid(gate)
    grad_gate = grad_active * upper * sigma * (1.0 + gate * (1.0 - sigma))
    grad_upper = grad_active * gate * sigma
    grad_normal_two, grad_gate_up = back_in(
        jnp.stack([grad_gate, grad_upper]).astype(jnp.bfloat16), kept["whole_two"], gate_rows
    )
    grad_mixed_two = norm_backward(grad_normal_two, kept["normal_two"], kept["scale_two"])
    grad_middle = mix_back(mix_two, grad_final, grad_mixed_two)
    hyper_two = mixing_grads(kept["middle"], grad_mixed_two, grad_final, kept["branch_two"])
    grad_branch = gather_columns(weighted(mix_one[:, 1 + count], grad_middle))
    grad_attended, grad_output = back_out(grad_branch, kept["attended"], output_rows)
    shape = kept["queries"].shape
    length = shape[0]
    grad_attended = grad_attended.astype(jnp.bfloat16).reshape(shape)
    grad_queries, grad_keys, grad_values = attend_back(
        kept["queries"],
        kept["key_heads"],
        kept["value_heads"],
        segment_row,
        kept["log_totals"],
        grad_attended,
    )
    grad_heads = jnp.stack(
        [
            unrotate(grad_queries, cosine, sine).reshape(length, -1),
            unrotate(grad_keys, cosine, sine).reshape(length, -1),
            grad_values.reshape(length, -1),
        ]
    ).astype(jnp.bfloat16)
    grad_normal_one, grad_projections = back_in(grad_heads, kept["whole_one"], projections)
    grad_mixed_one = norm_backward(grad_normal_one, kept["normal_one"], kept["scale_one"])
    grad_streams = mix_back(mix_one, grad_middle, grad_mixed_one)
    hyper_one = mixing_grads(stream_values, grad_mixed_one, grad_middle, kept["branch"])
    grad_hyper = lax.psum(jnp.stack([hyper_one, hyper_two]), ("row", "col"))
    tokens_all = streams.shape[1] * lax.axis_size("row")
    token_scale = tokens_all ** (-0.5)
    model_rate = D ** (-0.5) * token_scale
    first = update(
        attention_in, grad_projections, moment_attention_in, average_attention_in, model_rate
    )
    second = update(
        attention_out, grad_output, moment_attention_out, average_attention_out, model_rate
    )
    third = update(gate_up, grad_gate_up, moment_gate_up, average_gate_up, model_rate)
    fourth = update(
        down_weights,
        grad_down,
        moment_down_weights,
        average_down_weights,
        FF ** (-0.5) * token_scale,
    )
    fifth = update(
        hyper_mix,
        grad_hyper,
        moment_hyper_mix,
        average_hyper_mix,
        0.05 * (tokens_all * D) ** (-0.5),
    )
    return (
        jnp.stack(final).astype(jnp.bfloat16),
        jnp.stack(grad_streams),
        first[0],
        first[1],
        first[2],
        second[0],
        second[1],
        second[2],
        third[0],
        third[1],
        third[2],
        fourth[0],
        fourth[1],
        fourth[2],
        fifth[0],
        fifth[1],
        fifth[2],
    )


def solution(mesh):
    in_specs = (
        P(None, "row", "col"),
        P("row", None),
        P(None, "row", "col"),
        P("col", "row"),
        P(None, "row", "col"),
        P("col", "row"),
        P(),
        P(None, "row", "col"),
        P("col", "row"),
        P(None, "row", "col"),
        P("col", "row"),
        P(),
        P(None, "row", "col"),
        P("col", "row"),
        P(None, "row", "col"),
        P("col", "row"),
        P(),
        P(None, "row", "col"),
    )
    out_specs = (
        P(None, "row", "col"),
        P(None, "row", "col"),
        P(None, "row", "col"),
        P(None, "row", "col"),
        P(None, "row", "col"),
        P("col", "row"),
        P("col", "row"),
        P("col", "row"),
        P(None, "row", "col"),
        P(None, "row", "col"),
        P(None, "row", "col"),
        P("col", "row"),
        P("col", "row"),
        P("col", "row"),
        P(),
        P(),
        P(),
    )
    return jax.shard_map(
        per_device, mesh=mesh, in_specs=in_specs, out_specs=out_specs, check_vma=False
    )
```

```python
import functools

import jax
import jax.numpy as jnp
from jax import lax
from jax.experimental import pallas as pl
from jax.experimental.pallas import tpu as pltpu
from jax.sharding import PartitionSpec as P

D = 2048
HEAD_DIM = 128
FF = 8192
STEP = 8


EPSILON = 1e-05
MASKED = -1e30
MOMENTUM = 0.9
DECAY = 0.01
GROUP = 128
MESH = pl.DeviceIdType.MESH
VM, SM = pltpu.VMEM, pltpu.SMEM
f32 = jnp.float32
LANES = (((1,), (1,)), ((), ()))
ROWS = (((0,), (0,)), ((), ()))


def rope_tables(segments):
    segments = segments[0]
    length = segments.shape[0]
    index = jnp.arange(length, dtype=jnp.int32)
    before = jnp.concatenate([jnp.full((1,), -1, jnp.int32), segments[:-1]])
    starts = jnp.where(segments != before, index, 0)
    places = index - lax.cummax(starts)
    rates = 10000.0 ** (-2.0 * jnp.arange(HEAD_DIM // 2).astype(jnp.float32) / HEAD_DIM)
    angle = places[:, None].astype(jnp.float32) * rates
    cosine, sine = jnp.cos(angle), jnp.sin(angle)
    return (jnp.concatenate([cosine, cosine], 1), jnp.concatenate([-sine, sine], 1))


def exchange(
    size, tokens, width, chunk, hop, scatter, gather, prepare, finish, scratch, during=None, rows_too=0
):
    send, recv, blocks, facts, own_facts, sums_sent, sums_got, blocks_sent, blocks_got, facts_sent, facts_got = scratch
    me = lax.axis_index("col")
    chunks = tokens // chunk
    per_group = GROUP // chunk
    edge = size - 1

    def far(place):
        return jnp.maximum(place, edge - place) * hop if scatter is not None else place * 0

    def remote(source, target, sent, got, device):
        return pltpu.make_async_remote_copy(
            src_ref=source,
            dst_ref=target,
            send_sem=sent,
            recv_sem=got,
            device_id={"col": device},
            device_id_type=MESH,
        )

    def rows(index):
        return pl.ds(pl.multiple_of(index * chunk, chunk), chunk)

    def sum_copy(shard, slot, index, device):
        return remote(
            send.at[shard, rows(index)],
            recv.at[slot, rows(index)],
            sums_sent.at[shard, index],
            sums_got.at[slot, index],
            device,
        )

    def block_copy(place, index, way, device):
        return remote(
            blocks.at[place, rows(index)],
            blocks.at[place, rows(index)],
            blocks_sent.at[way, place, index],
            blocks_got.at[place, index],
            device,
        )

    def fact_copy(place, group, device):
        return remote(
            facts.at[group, pl.ds(pl.multiple_of(place * 8, 8), 8)],
            facts.at[group, pl.ds(pl.multiple_of(place * 8, 8), 8)],
            facts_sent.at[device, group],
            facts_got.at[place, group],
            device,
        )

    right = jnp.minimum(me + 1, edge)
    left = jnp.maximum(me - 1, 0)
    other = jnp.where(me == edge, left, right)

    def inside(index):
        return (index >= 0) & (index < chunks)

    def relay_sums(step):
        index = step - me * hop

        @pl.when(inside(index))
        def _():
            for shard in range(size - 1, 0, -1):

                @pl.when(shard > me)
                def _():
                    mine = scatter[rows(index), shard * width : (shard + 1) * width]

                    @pl.when(me > 0)
                    def _():
                        sum_copy(shard, shard, index, other).wait_recv()
                        total = mine.astype(jnp.float32) + recv[shard, rows(index)].astype(
                            jnp.float32
                        )
                        send[shard, rows(index)] = total.astype(jnp.bfloat16)

                    @pl.when(me == 0)
                    def _():
                        send[shard, rows(index)] = mine

                    slot = jnp.where(me + 1 == shard, size, shard)
                    sum_copy(shard, slot, index, right).start()

        back = step - (edge - me) * hop

        @pl.when(inside(back))
        def _():
            for shard in range(size - 1):

                @pl.when(shard < me)
                def _():
                    mine = scatter[rows(back), shard * width : (shard + 1) * width]

                    @pl.when(me < edge)
                    def _():
                        sum_copy(shard, shard, back, other).wait_recv()
                        total = mine.astype(jnp.float32) + recv[shard, rows(back)].astype(
                            jnp.float32
                        )
                        send[shard, rows(back)] = total.astype(jnp.bfloat16)

                    @pl.when(me == edge)
                    def _():
                        send[shard, rows(back)] = mine

                    sum_copy(shard, shard, back, left).start()

    def ready(step):
        index = step - far(me)

        @pl.when(inside(index))
        def _():
            if scatter is not None:

                @pl.when(me > 0)
                def _():
                    sum_copy(0, size, index, other).wait_recv()

                @pl.when(me < edge)
                def _():
                    sum_copy(0, me, index, other).wait_recv()

                start = pl.multiple_of(me * width, width)
                total = scatter[rows(index), pl.ds(start, width)].astype(jnp.float32)
                total = total + jnp.where(me > 0, recv[size, rows(index)].astype(jnp.float32), 0.0)
                total = total + jnp.where(
                    me < edge, recv[me, rows(index)].astype(jnp.float32), 0.0
                )
            else:
                total = None
            columns, block = prepare(rows(index), total)
            lane = lax.broadcasted_iota(jnp.int32, (chunk, 128), 1)
            packed = jnp.zeros((chunk, 128), jnp.float32)
            for place, column in enumerate(columns):
                packed = jnp.where(lane == place, column, packed)
            within = lax.rem(index, per_group)
            own_facts[pl.ds(pl.multiple_of(within * chunk, chunk), chunk), :] = packed
            if gather:
                blocks[me, rows(index)] = block

                @pl.when(me < edge)
                def _():
                    block_copy(me, index, 0, right).start()

                @pl.when(me > 0)
                def _():
                    block_copy(me, index, 1, left).start()

            @pl.when(within == per_group - 1)
            def _():
                group = index // per_group
                turned = own_facts[...].T
                facts[group, pl.ds(pl.multiple_of(me * 8, 8), 8), :] = turned[:8]
                for place in range(size):

                    @pl.when(place != me)
                    def _():
                        fact_copy(me, group, place).start()

    def relay_blocks(step):
        for near in range(1, size):
            for way, place in ((0, me - near), (1, me + near)):
                index = step - far(place) - near * hop

                @pl.when((place >= 0) & (place < size) & inside(index))
                def _():
                    block_copy(place, index, way, other).wait_recv()
                    onward = (me < edge) if way == 0 else (me > 0)

                    @pl.when(onward)
                    def _():
                        block_copy(place, index, way, right if way == 0 else left).start()

    longest = 2 * edge * hop if scatter is not None else edge * hop
    if not gather:
        longest = edge * hop

    def conclude(step):
        index = step - longest

        @pl.when(inside(index) & (lax.rem(index, per_group) == per_group - 1))
        def _():
            group = index // per_group
            for place in range(size):

                @pl.when(place != me)
                def _():
                    fact_copy(place, group, other).wait_recv()

            turned = facts[group].T
            finish(group, pl.ds(pl.multiple_of(group * GROUP, GROUP), GROUP), turned)

    barrier = pltpu.get_barrier_semaphore()
    for place in range(size):

        @pl.when(place != me)
        def _():
            pl.semaphore_signal(barrier, inc=1, device_id={"col": place}, device_id_type=MESH)

    line = lax.axis_index("row")
    for place in range(rows_too):

        @pl.when(place != line)
        def _():
            pl.semaphore_signal(barrier, inc=1, device_id={"row": place}, device_id_type=MESH)

    pl.semaphore_wait(barrier, size - 1 + max(rows_too - 1, 0))

    def step_all(step, carry):
        if scatter is not None:
            relay_sums(step)
        ready(step)
        if gather:
            relay_blocks(step)
        conclude(step)
        if during is not None:

            @pl.when(inside(step))
            def _():
                during(rows(step))

        return carry

    lax.fori_loop(0, chunks + longest, step_all, 0)

    def drain(index, carry):
        if scatter is not None:
            for shard in range(size):

                @pl.when(shard != me)
                def _():
                    sum_copy(shard, shard, index, other).wait_send()

        if gather:
            for place in range(size):

                @pl.when((place <= me) & (me < edge))
                def _():
                    block_copy(place, index, 0, other).wait_send()

                @pl.when((place >= me) & (me > 0))
                def _():
                    block_copy(place, index, 1, other).wait_send()

        return carry

    lax.fori_loop(0, chunks, drain, 0)

    def drain_facts(group, carry):
        for place in range(size):

            @pl.when(place != me)
            def _():
                fact_copy(me, group, place).wait_send()

        return carry

    lax.fori_loop(0, tokens // GROUP, drain_facts, 0)


def exchange_scratch(size, tokens, width, chunk, scatter, gather):
    chunks = tokens // chunk
    groups = tokens // GROUP
    dma = pltpu.SemaphoreType.DMA
    tiny = (1, chunk, 128)
    return [
        pltpu.VMEM((size, tokens, width) if scatter else tiny, jnp.bfloat16),
        pltpu.VMEM((size + 1, tokens, width) if scatter else tiny, jnp.bfloat16),
        pltpu.VMEM((size, tokens, width) if gather else tiny, jnp.bfloat16),
        pltpu.VMEM((groups, 128, 128), jnp.float32),
        pltpu.VMEM((GROUP, 128), jnp.float32),
        dma((size, chunks) if scatter else (1, 1)),
        dma((size + 1, chunks) if scatter else (1, 1)),
        dma((2, size, chunks) if gather else (1, 1, 1)),
        dma((size, chunks) if gather else (1, 1)),
        dma((size, groups)),
        dma((size, groups)),
    ]


def call(body, operands, places, outs, scratch, name, ident):
    moved = sum(array.size * array.dtype.itemsize for array in list(operands) + outs)
    return pl.pallas_call(
        body,
        out_shape=outs,
        in_specs=[pl.BlockSpec(memory_space=place) for place in places],
        out_specs=[pl.BlockSpec(memory_space=pltpu.VMEM)] * len(outs),
        scratch_shapes=scratch,
        compiler_params=pltpu.CompilerParams(
            collective_id=ident, has_side_effects=True, vmem_limit_bytes=58 * 2**20
        ),
        cost_estimate=pl.CostEstimate(
            flops=10**11, bytes_accessed=moved, transcendentals=0
        ),
        name=name,
    )(*operands)


def norm_stats(value):
    mean = jnp.sum(value, -1, keepdims=True) * (1.0 / value.shape[-1])
    center = value - mean
    return mean, center, jnp.sum(center * center, -1, keepdims=True)


def norm_whole(size, width, turned):
    means = [turned[:, 8 * z : 8 * z + 1] for z in range(size)]
    squares = [turned[:, 8 * z + 1 : 8 * z + 2] for z in range(size)]
    mean = sum(means[1:], means[0]) * (1.0 / size)
    shifts = [own - mean for own in means]
    spread = sum(squares[1:], squares[0])
    for shift in shifts:
        spread = spread + width * shift * shift
    return shifts, lax.rsqrt(spread * (1.0 / (size * width)) + EPSILON)


def norm_in_kernel(size, chunk, hop, coeffs, streams, whole, scale, *scratch):
    count, tokens, width = streams.shape
    blocks = scratch[2]

    def prepare(rows, total):
        mixed = coeffs[0] * streams[0, rows].astype(f32)
        for k in range(1, count):
            mixed = mixed + coeffs[k] * streams[k, rows].astype(f32)
        mean, center, square = norm_stats(mixed)
        return (mean, square), center.astype(jnp.bfloat16)

    def finish(group, rows, turned):
        shifts, rate = norm_whole(size, width, turned)
        scale[rows, :] = rate
        for z in range(size):
            value = (blocks[z, rows].astype(f32) + shifts[z]) * rate
            whole[rows, z * width : (z + 1) * width] = value.astype(jnp.bfloat16)

    exchange(size, tokens, width, chunk, hop, None, True, prepare, finish, scratch)


def norm_in(size, streams, coeffs, chunk=64, hop=1):
    _, tokens, width = streams.shape
    return call(
        functools.partial(norm_in_kernel, size, chunk, hop),
        (coeffs, streams),
        (SM, VM),
        [
            jax.ShapeDtypeStruct((tokens, size * width), jnp.bfloat16),
            jax.ShapeDtypeStruct((tokens, 1), f32),
        ],
        exchange_scratch(size, tokens, width, chunk, False, True),
        "norm_in",
        1,
    )


def norm_mid_kernel(size, chunk, hop, coeffs, partial, streams, whole, scale, branch, *scratch):
    count, tokens, width = streams.shape
    blocks = scratch[2]

    def prepare(rows, total):
        branch[rows, :] = total
        mixed = coeffs[count] * total
        for k in range(count):
            mixed = mixed + coeffs[k] * streams[k, rows].astype(f32)
        mean, center, square = norm_stats(mixed)
        return (mean, square), center.astype(jnp.bfloat16)

    def finish(group, rows, turned):
        shifts, rate = norm_whole(size, width, turned)
        scale[rows, :] = rate
        for z in range(size):
            value = (blocks[z, rows].astype(f32) + shifts[z]) * rate
            whole[rows, z * width : (z + 1) * width] = value.astype(jnp.bfloat16)

    exchange(size, tokens, width, chunk, hop, partial, True, prepare, finish, scratch)


def norm_mid(size, partial, streams, coeffs, chunk=64, hop=1):
    _, tokens, width = streams.shape
    return call(
        functools.partial(norm_mid_kernel, size, chunk, hop),
        (coeffs, partial, streams),
        (SM, VM, VM),
        [
            jax.ShapeDtypeStruct((tokens, size * width), jnp.bfloat16),
            jax.ShapeDtypeStruct((tokens, 1), f32),
            jax.ShapeDtypeStruct((tokens, width), f32),
        ],
        exchange_scratch(size, tokens, width, chunk, True, True),
        "norm_mid",
        2,
    )


def back_mid_kernel(
    size, chunk, hop, coeffs, partial, grads, whole_normal, scale, whole, inner, *scratch
):
    count, tokens, width = grads.shape
    blocks = scratch[2]
    me = lax.axis_index("col")

    def own_normal(rows):
        return whole_normal[rows, pl.ds(pl.multiple_of(me * width, width), width)].astype(f32)

    def prepare(rows, total):
        inner[rows, :] = total
        normal = own_normal(rows)
        part = 1.0 / width
        first = jnp.sum(total, -1, keepdims=True)
        second = jnp.sum(total * normal, -1, keepdims=True)
        plain = jnp.sum(normal, -1, keepdims=True)
        square = jnp.sum(normal * normal, -1, keepdims=True)
        spread = square - plain * plain * part
        cross = second - first * plain * part
        slope = jnp.where(spread > 1e-3, cross / jnp.maximum(spread, 1e-3), 0.0)
        level = (first - slope * plain) * part
        known = coeffs[0] * grads[0, rows].astype(f32)
        for k in range(1, count):
            known = known + coeffs[k] * grads[k, rows].astype(f32)
        block = known + (coeffs[count] * scale[rows, :]) * (total - level - slope * normal)
        return (first, second, level, slope), block.astype(jnp.bfloat16)

    def finish(group, rows, turned):
        first = turned[:, 0:1]
        second = turned[:, 1:2]
        for z in range(1, size):
            first = first + turned[:, 8 * z : 8 * z + 1]
            second = second + turned[:, 8 * z + 1 : 8 * z + 2]
        first = first * (1.0 / (size * width))
        second = second * (1.0 / (size * width))
        rate = scale[rows, :]
        gain = coeffs[count] * rate
        for z in range(size):
            level = gain * (turned[:, 8 * z + 2 : 8 * z + 3] - first)
            slope = gain * (turned[:, 8 * z + 3 : 8 * z + 4] - second)
            columns = slice(z * width, (z + 1) * width)
            value = blocks[z, rows].astype(f32) + level + slope * whole_normal[rows, columns].astype(f32)
            whole[rows, columns] = value.astype(jnp.bfloat16)
        inner[rows, :] = rate * (inner[rows, :] - first - second * own_normal(rows))

    exchange(size, tokens, width, chunk, hop, partial, True, prepare, finish, scratch)


def back_mid(size, partial, grads, whole_normal, scale, coeffs, chunk=64, hop=1):
    _, tokens, width = grads.shape
    return call(
        functools.partial(back_mid_kernel, size, chunk, hop),
        (coeffs, partial, grads, whole_normal, scale),
        (SM, VM, VM, VM, VM),
        [
            jax.ShapeDtypeStruct((tokens, size * width), jnp.bfloat16),
            jax.ShapeDtypeStruct((tokens, width), f32),
        ],
        exchange_scratch(size, tokens, width, chunk, True, True),
        "back_mid",
        3,
    )


def tile_sum(product):
    height, width = product.shape
    folded = jnp.sum(product.reshape(height // 8, 8, width), 0)
    total = folded[:, :128]
    for start in range(128, width, 128):
        total = total + folded[:, start : start + 128]
    return total


def back_in_kernel(
    size,
    chunk,
    hop,
    coeffs,
    partial,
    whole_normal,
    scale,
    streams,
    grads,
    branch_one,
    branch_two,
    inner_two,
    final,
    grad_streams,
    whole_sums,
    inner,
    sums,
    shares,
    shares_sent,
    shares_got,
    *scratch,
):
    count, tokens, width = streams.shape
    me = lax.axis_index("col")
    square = count * count
    sums[...] = jnp.zeros_like(sums)

    def own_normal(rows):
        return whole_normal[rows, pl.ds(pl.multiple_of(me * width, width), width)].astype(f32)

    def prepare(rows, total):
        inner[rows, :] = total
        first = jnp.sum(total, -1, keepdims=True)
        second = jnp.sum(total * own_normal(rows), -1, keepdims=True)
        return (first, second), None

    def finish(group, rows, turned):
        first = turned[:, 0:1]
        second = turned[:, 1:2]
        for z in range(1, size):
            first = first + turned[:, 8 * z : 8 * z + 1]
            second = second + turned[:, 8 * z + 1 : 8 * z + 2]
        first = first * (1.0 / (size * width))
        second = second * (1.0 / (size * width))
        own = scale[rows, :] * (inner[rows, :] - first - second * own_normal(rows))
        below = inner_two[rows, :]
        for i in range(count):
            value = coeffs[square + i] * below + coeffs[square + 3 * count + i] * own
            for k in range(count):
                value = value + coeffs[i * count + k] * grads[k, rows].astype(f32)
            grad_streams[i, rows] = value
            place = square + 3 * count + 1 + i
            sums[place] = sums[place] + tile_sum(streams[i, rows].astype(f32) * own)

    def during(rows):
        values = [streams[i, rows].astype(f32) for i in range(count)]
        above = [grads[i, rows].astype(f32) for i in range(count)]
        one = branch_one[rows, :]
        two = branch_two[rows, :]
        below = inner_two[rows, :]
        for j in range(count):
            value = coeffs[square + count + j] * one + coeffs[square + 2 * count + j] * two
            for k in range(count):
                value = value + coeffs[k * count + j] * values[k]
            final[j, rows] = value.astype(jnp.bfloat16)
        pairs = [(a, b) for a in values for b in above]
        pairs = pairs + [(a, below) for a in values]
        pairs = pairs + [(one, b) for b in above]
        pairs = pairs + [(a, two) for a in above]
        pairs = pairs + [(one, below)]
        for place, (a, b) in enumerate(pairs):
            sums[place] = sums[place] + tile_sum(a * b)

    count_rows = lax.axis_size("row")
    exchange(
        size,
        tokens,
        width,
        chunk,
        hop,
        partial,
        False,
        prepare,
        finish,
        scratch,
        during,
        count_rows,
    )
    total = jnp.sum(jnp.sum(sums[...], 1), -1, keepdims=True)
    total = jnp.broadcast_to(total, whole_sums.shape)
    for axis, members, base in (("col", size, 0), ("row", count_rows, size)):
        here = lax.axis_index(axis)

        def share_copy(member, target):
            return pltpu.make_async_remote_copy(
                src_ref=shares.at[base + here],
                dst_ref=shares.at[base + here],
                send_sem=shares_sent.at[base + member],
                recv_sem=shares_got.at[base + here],
                device_id={axis: target},
                device_id_type=MESH,
            )

        shares[base + here] = total
        for member in range(members):

            @pl.when(member != here)
            def _():
                share_copy(member, member).start()

        for member in range(members):

            @pl.when(member != here)
            def _():
                pltpu.make_async_remote_copy(
                    src_ref=shares.at[base + member],
                    dst_ref=shares.at[base + member],
                    send_sem=shares_sent.at[base + member],
                    recv_sem=shares_got.at[base + member],
                    device_id={axis: member},
                    device_id_type=MESH,
                ).wait()

        total = shares[base]
        for member in range(1, members):
            total = total + shares[base + member]
    whole_sums[...] = total


def back_in(
    size,
    coeffs,
    partial,
    whole_normal,
    scale,
    streams,
    grads,
    branch_one,
    branch_two,
    inner_two,
    chunk=64,
    hop=1,
):
    count, tokens, width = streams.shape
    products = -(-(count * count + 4 * count + 1) // 8) * 8
    return call(
        functools.partial(back_in_kernel, size, chunk, hop),
        (
            coeffs,
            partial,
            whole_normal,
            scale,
            streams,
            grads,
            branch_one,
            branch_two,
            inner_two,
        ),
        (SM,) + (VM,) * 8,
        [
            jax.ShapeDtypeStruct(streams.shape, jnp.bfloat16),
            jax.ShapeDtypeStruct(streams.shape, f32),
            jax.ShapeDtypeStruct((products, 128), f32),
        ],
        [
            pltpu.VMEM((tokens, width), f32),
            pltpu.VMEM((products, 8, 128), f32),
            pltpu.VMEM((size + lax.axis_size("row"), products, 128), f32),
            pltpu.SemaphoreType.DMA((size + lax.axis_size("row"),)),
            pltpu.SemaphoreType.DMA((size + lax.axis_size("row"),)),
        ]
        + exchange_scratch(size, tokens, width, chunk, True, False),
        "back_in",
        4,
    )


def block_probs(queries, key_heads, rows_docs, columns_docs, start):
    scores = lax.dot_general(queries, key_heads, LANES, preferred_element_type=f32)
    scores = scores * HEAD_DIM ** (-0.5)
    row = lax.broadcasted_iota(jnp.int32, scores.shape, 0) + start
    column = lax.broadcasted_iota(jnp.int32, scores.shape, 1)
    scores = jnp.where((rows_docs == columns_docs) & (column <= row), scores, MASKED)
    expo = jnp.exp(scores - jnp.max(scores, -1, keepdims=True))
    return expo * (1.0 / jnp.sum(expo, -1, keepdims=True))


def attend_forward_kernel(
    block, query, key, value, cosine, sine, column, row, queries, key_heads, value_heads, attended
):
    length = query.shape[0]

    def turn(values):
        return (values * cosine[...] + pltpu.roll(values, HEAD_DIM // 2, 1) * sine[...]).astype(
            jnp.bfloat16
        )

    queries[...] = turn(query[...])
    key_heads[...] = turn(key[...])
    value_heads[...] = value[...].astype(jnp.bfloat16)
    for start in range(0, length, block):
        end = start + block
        probs = block_probs(
            queries[start:end], key_heads[:end], column[start:end], row[:, :end], start
        )
        result = jnp.dot(
            probs.astype(jnp.bfloat16), value_heads[:end], preferred_element_type=f32
        )
        attended[start:end, :] = result.astype(jnp.bfloat16)


def attend_forward(projected, cosine, sine, column, row):
    length, width = projected.shape
    width = width // 3
    heads = width // HEAD_DIM
    block = min(256, length)

    def head(offset):
        return pl.BlockSpec((length, HEAD_DIM), lambda h: (0, h + offset))

    def fixed(array):
        return pl.BlockSpec(array.shape, lambda h: (0, 0))

    return pl.pallas_call(
        functools.partial(attend_forward_kernel, block),
        grid=(heads,),
        out_shape=[jax.ShapeDtypeStruct((length, width), jnp.bfloat16)] * 4,
        in_specs=[head(0), head(heads), head(2 * heads)]
        + [fixed(array) for array in (cosine, sine, column, row)],
        out_specs=[head(0)] * 4,
        compiler_params=pltpu.CompilerParams(vmem_limit_bytes=48 * 2**20),
        name="attend_forward",
    )(projected, projected, projected, cosine, sine, column, row)


def attend_back_kernel(
    block,
    queries,
    key_heads,
    value_heads,
    grad_result,
    cosine,
    sine,
    column,
    row,
    grad_query,
    grad_key,
    grad_value,
    key_sum,
    value_sum,
):
    length = queries.shape[0]
    factor = HEAD_DIM ** (-0.5)

    def turn_back(values, rows):
        values = values * factor
        return (
            values * cosine[rows] - pltpu.roll(values, HEAD_DIM // 2, 1) * sine[rows]
        ).astype(jnp.bfloat16)

    for start in range(length - block, -1, -block):
        end = start + block
        query, grad_part = queries[start:end], grad_result[start:end]
        probs = block_probs(query, key_heads[:end], column[start:end], row[:, :end], start)
        grad_probs = lax.dot_general(
            grad_part, value_heads[:end], LANES, preferred_element_type=f32
        )
        row_sum = jnp.sum(probs * grad_probs, -1, keepdims=True)
        grad_scores = (probs * (grad_probs - row_sum)).astype(jnp.bfloat16)
        grad_part_query = jnp.dot(grad_scores, key_heads[:end], preferred_element_type=f32)
        grad_query[start:end, :] = turn_back(grad_part_query, pl.ds(start, block))
        key_part = lax.dot_general(grad_scores, query, ROWS, preferred_element_type=f32)
        value_part = lax.dot_general(
            probs.astype(jnp.bfloat16), grad_part, ROWS, preferred_element_type=f32
        )
        if end == length:
            key_sum[...] = key_part
            value_sum[...] = value_part
        else:
            key_sum[:end, :] += key_part
            value_sum[:end, :] += value_part
    grad_key[...] = turn_back(key_sum[...], pl.ds(0, length))
    grad_value[...] = value_sum[...].astype(jnp.bfloat16)


def attend_back(queries, key_heads, value_heads, grad_result, cosine, sine, column, row):
    length, width = queries.shape
    heads = width // HEAD_DIM
    block = min(256, length)
    head = pl.BlockSpec((length, HEAD_DIM), lambda h: (0, h))

    def fixed(array):
        return pl.BlockSpec(array.shape, lambda h: (0, 0))

    grads = pl.pallas_call(
        functools.partial(attend_back_kernel, block),
        grid=(heads,),
        out_shape=[jax.ShapeDtypeStruct((length, width), jnp.bfloat16)] * 3,
        in_specs=[head] * 4 + [fixed(array) for array in (cosine, sine, column, row)],
        out_specs=[head] * 3,
        scratch_shapes=[pltpu.VMEM((length, HEAD_DIM), f32)] * 2,
        compiler_params=pltpu.CompilerParams(vmem_limit_bytes=48 * 2**20),
        name="attend_back",
    )(queries, key_heads, value_heads, grad_result, cosine, sine, column, row)
    return jnp.concatenate(grads, 1)


def update(weight, grad, moment, average, rate):
    step_grad = grad + DECAY * weight
    moment_new = MOMENTUM * moment + step_grad
    weight_new = weight - rate * (step_grad + MOMENTUM * moment_new)
    return (weight_new, moment_new, average + (weight_new - average) / (STEP + 1))


def tie(*values):
    return lax.optimization_barrier(values)


def line_ways():
    size = lax.axis_size("col")
    up = [(i, i + 1) for i in range(size - 1)]
    down = [(i + 1, i) for i in range(size - 1)]
    return size, lax.axis_index("col"), up, down


def gather_steps(values):
    size, me, up, down = line_ways()
    width = values.shape[1]
    before, after = [values], [values]
    for _ in range(size - 1):
        step = (lax.ppermute(before[-1], "col", up), lax.ppermute(after[-1], "col", down))
        step = yield step
        before.append(step[0])
        after.append(step[1])
    row = jnp.concatenate(before[:0:-1] + after, 1)
    yield lax.dynamic_slice_in_dim(row, (size - 1 - me) * width, size * width, 1)


def scatter_steps(partial):
    size, me, up, down = line_ways()
    width = partial.shape[1] // size

    def share(place):
        return lax.dynamic_slice_in_dim(partial, place * width, width, 1)

    first = share(jnp.minimum(me + size - 1, size - 1))
    last = share(jnp.maximum(me - size + 1, 0))
    for step in range(1, size):
        if step > 1:
            first = share(jnp.minimum(me + size - step, size - 1)).astype(f32) + first.astype(f32)
            last = share(jnp.maximum(me - size + step, 0)).astype(f32) + last.astype(f32)
            first = first.astype(jnp.bfloat16)
            last = last.astype(jnp.bfloat16)
        first, last = yield (lax.ppermute(first, "col", up), lax.ppermute(last, "col", down))
    yield share(me).astype(f32) + first.astype(f32) + last.astype(f32)


def advance(steps, got, *values):
    moved = next(steps) if got is None else steps.send(got)
    tied = tie(*moved, *values)
    return tied[: len(moved)], tied[len(moved) :]


def finish_line(steps, got):
    moved = steps.send(got)
    while isinstance(moved, tuple):
        moved = steps.send(moved)
    return moved


def weighted(coeffs, streams):
    total = coeffs[0] * streams[0].astype(f32)
    for index in range(1, len(streams)):
        total = total + coeffs[index] * streams[index].astype(f32)
    return total


def small_matmul(left, right):
    return jnp.sum(left[:, :, None] * right[None, :, :], 1)


def matmul(spec, left, right, kind=jnp.float32):
    return jnp.einsum(spec, left, right, preferred_element_type=f32).astype(kind)


def scatter_rows(grad, axis):
    return lax.psum_scatter(grad, "row", scatter_dimension=axis, tiled=True).astype(f32)


def side_by_side(weights):
    return jnp.concatenate([weights[k] for k in range(weights.shape[0])], 1)


def one_by_one(values, count):
    width = values.shape[1] // count
    return jnp.stack([values[:, k * width : (k + 1) * width] for k in range(count)])


def per_device(
    streams,
    segments,
    attention_in,
    attention_out,
    gate_up,
    down_weights,
    hyper_mix,
    moment_attention_in,
    moment_attention_out,
    moment_gate_up,
    moment_down_weights,
    moment_hyper_mix,
    average_attention_in,
    average_attention_out,
    average_gate_up,
    average_down_weights,
    average_hyper_mix,
    cotangent,
):
    size = lax.axis_size("col")
    low = jnp.bfloat16
    count, length, width = streams.shape
    cosine, sine = rope_tables(segments)

    def gather_rows(weights, axis):
        return lax.all_gather(weights.astype(low), "row", axis=axis, tiled=True)

    projections = gather_rows(side_by_side(attention_in), 0)
    output_rows = gather_rows(attention_out, 1)
    gate_rows = gather_rows(side_by_side(gate_up), 0)
    down_rows = gather_rows(down_weights, 1)

    one, two = hyper_mix[0], hyper_mix[1]
    across_one, across_two = one[:, 1 : 1 + count], two[:, 1 : 1 + count]
    through = small_matmul(across_one, across_two)
    in_two = small_matmul(across_one, two[:, :1])[:, 0]
    out_one = small_matmul(one[None, :, 1 + count], across_two)[0]
    turn = jnp.sum(one[:, 1 + count] * two[:, 0])

    whole_one, scale_one = norm_in(size, streams, one[:, 0])
    whole_one, grads_tied = tie(whole_one, cotangent)

    steps = gather_steps(
        weighted(two[:, 1 + count], [grads_tied[i] for i in range(count)]).astype(low)
    )
    got, (projected,) = advance(steps, None, matmul("tn,nw->tw", whole_one, projections))
    queries, key_heads, value_heads, attended = attend_forward(
        projected, cosine, sine, segments.T, segments
    )
    got, (attended,) = advance(steps, got, attended)

    mid_coeffs = jnp.concatenate([in_two, turn[None]])
    whole_two, scale_two, branch_one = norm_mid(
        size, matmul("tw,wd->td", attended, output_rows, low), streams, mid_coeffs
    )
    whole_two, *got = tie(whole_two, *got)

    gated = matmul("tn,nw->tw", whole_two, gate_rows)
    whole_grad_two = finish_line(steps, tuple(got))
    hidden = gated.shape[1] // 2
    gate, upper = gated[:, :hidden], gated[:, hidden:]
    sigma = jax.nn.sigmoid(gate)
    active = (gate * sigma * upper).astype(low)
    partial_two = matmul("tw,wd->td", active, down_rows, low)
    grad_down = matmul("tw,td->wd", active, whole_grad_two, low)
    grad_down, partial_two, whole_grad_two = tie(grad_down, partial_two, whole_grad_two)
    grad_down = scatter_rows(grad_down, 1)

    steps = scatter_steps(partial_two)
    grad_active = matmul("tn,wn->tw", whole_grad_two, down_rows)
    grad_gate = grad_active * upper * sigma * (1.0 + gate * (1.0 - sigma))
    grad_upper = grad_active * gate * sigma
    grad_gated = jnp.concatenate([grad_gate, grad_upper], 1).astype(low)
    got, (grad_gated,) = advance(steps, None, grad_gated)
    grad_gate_up = matmul("td,tw->dw", whole_two, grad_gated, low)
    got, (grad_gate_up, grad_gated) = advance(steps, got, grad_gate_up, grad_gated)
    grad_gate_up, grad_down = tie(grad_gate_up, grad_down)
    grad_gate_up = scatter_rows(grad_gate_up, 0)
    partial_mid = matmul("tw,nw->tn", grad_gated, gate_rows, low)
    branch_two = finish_line(steps, got)
    partial_mid, branch_two = tie(partial_mid, branch_two)
    back_coeffs = jnp.concatenate([out_one, turn[None]])
    whole_grad_one, inner_two = back_mid(
        size, partial_mid, cotangent, whole_two, scale_two, back_coeffs
    )

    grad_output = matmul("tw,td->wd", attended, whole_grad_one, low)
    grad_output, whole_grad_one = tie(grad_output, whole_grad_one)
    grad_output, grad_gate_up = tie(grad_output, grad_gate_up)
    grad_output = scatter_rows(grad_output, 1)
    grad_attended = matmul("tn,wn->tw", whole_grad_one, output_rows, low)
    grad_heads = attend_back(
        queries, key_heads, value_heads, grad_attended, cosine, sine, segments.T, segments
    )
    grad_projections = matmul("td,tw->dw", whole_one, grad_heads, low)
    grad_projections, grad_heads = tie(grad_projections, grad_heads)
    grad_projections, grad_output = tie(grad_projections, grad_output)
    grad_projections = scatter_rows(grad_projections, 0)
    end_coeffs = jnp.concatenate(
        [through.reshape(-1), in_two, out_one, two[:, 1 + count], one[:, 0]]
    )
    final, grad_streams, products = back_in(
        size,
        end_coeffs,
        matmul("tw,nw->tn", grad_heads, projections, low),
        whole_one,
        scale_one,
        streams,
        cotangent,
        branch_one,
        branch_two,
        inner_two,
    )

    products = products[:, 0]
    cuts = [count * count, count, count, count, 1, count]
    parts = []
    start = 0
    for cut in cuts:
        parts.append(products[start : start + cut])
        start = start + cut
    streams_grads, streams_two, branch_grads, grads_branch, branch_inner, streams_one = parts
    streams_grads = streams_grads.reshape(count, count)
    hyper_one = jnp.concatenate(
        [
            streams_one[:, None],
            small_matmul(streams_grads, across_two.T) + streams_two[:, None] * two[None, :, 0],
            small_matmul(across_two, branch_grads[:, None]) + (two[:, 0] * branch_inner)[:, None],
        ],
        1,
    )
    hyper_two = jnp.concatenate(
        [
            small_matmul(across_one.T, streams_two[:, None])
            + (one[:, 1 + count] * branch_inner)[:, None],
            small_matmul(across_one.T, streams_grads)
            + one[:, 1 + count][:, None] * branch_grads[None, :],
            grads_branch[:, None],
        ],
        1,
    )
    grad_hyper = jnp.stack([hyper_one, hyper_two])
    grad_projections = one_by_one(grad_projections, attention_in.shape[0])
    grad_gate_up = one_by_one(grad_gate_up, gate_up.shape[0])
    tokens_all = length * lax.axis_size("row")
    token_scale = tokens_all ** (-0.5)
    model_rate = D ** (-0.5) * token_scale
    first = update(
        attention_in, grad_projections, moment_attention_in, average_attention_in, model_rate
    )
    second = update(
        attention_out, grad_output, moment_attention_out, average_attention_out, model_rate
    )
    third = update(gate_up, grad_gate_up, moment_gate_up, average_gate_up, model_rate)
    fourth = update(
        down_weights,
        grad_down,
        moment_down_weights,
        average_down_weights,
        FF ** (-0.5) * token_scale,
    )
    fifth = update(
        hyper_mix,
        grad_hyper,
        moment_hyper_mix,
        average_hyper_mix,
        0.05 * (tokens_all * D) ** (-0.5),
    )
    return (
        final,
        grad_streams,
        first[0],
        first[1],
        first[2],
        second[0],
        second[1],
        second[2],
        third[0],
        third[1],
        third[2],
        fourth[0],
        fourth[1],
        fourth[2],
        fifth[0],
        fifth[1],
        fifth[2],
    )


def solution(mesh):
    in_specs = (
        P(None, "row", "col"),
        P("row", None),
        P(None, "row", "col"),
        P("col", "row"),
        P(None, "row", "col"),
        P("col", "row"),
        P(),
        P(None, "row", "col"),
        P("col", "row"),
        P(None, "row", "col"),
        P("col", "row"),
        P(),
        P(None, "row", "col"),
        P("col", "row"),
        P(None, "row", "col"),
        P("col", "row"),
        P(),
        P(None, "row", "col"),
    )
    out_specs = (
        P(None, "row", "col"),
        P(None, "row", "col"),
        P(None, "row", "col"),
        P(None, "row", "col"),
        P(None, "row", "col"),
        P("col", "row"),
        P("col", "row"),
        P("col", "row"),
        P(None, "row", "col"),
        P(None, "row", "col"),
        P(None, "row", "col"),
        P("col", "row"),
        P("col", "row"),
        P("col", "row"),
        P(),
        P(),
        P(),
    )
    return jax.shard_map(
        per_device, mesh=mesh, in_specs=in_specs, out_specs=out_specs, check_vma=False
    )
```

```python
import functools

import jax
import jax.numpy as jnp
from jax import lax
from jax.experimental import pallas as pl
from jax.experimental.pallas import tpu as pltpu
from jax.sharding import PartitionSpec as P

D = 2048
HEAD_DIM = 128
FF = 8192
STEP = 8


EPSILON = 1e-05
MASKED = -1e30
MOMENTUM = 0.9
DECAY = 0.01
GROUP = 128
MESH = pl.DeviceIdType.MESH
VM, SM = pltpu.VMEM, pltpu.SMEM
f32 = jnp.float32
LANES = (((1,), (1,)), ((), ()))
ROWS = (((0,), (0,)), ((), ()))


def rope_tables(segments):
    segments = segments[0]
    length = segments.shape[0]
    index = jnp.arange(length, dtype=jnp.int32)
    before = jnp.concatenate([jnp.full((1,), -1, jnp.int32), segments[:-1]])
    starts = jnp.where(segments != before, index, 0)
    places = index - lax.cummax(starts)
    rates = 10000.0 ** (-2.0 * jnp.arange(HEAD_DIM // 2).astype(jnp.float32) / HEAD_DIM)
    angle = places[:, None].astype(jnp.float32) * rates
    cosine, sine = jnp.cos(angle), jnp.sin(angle)
    return (jnp.concatenate([cosine, cosine], 1), jnp.concatenate([-sine, sine], 1))


def line_exchange(
    size, tokens, width, chunk, hop, scatter, gather, produce, prepare, finish, scratch, during=None, rows_too=0
):
    recv, blocks, facts, own_facts, sums_sent, sums_got, blocks_sent, blocks_got, facts_sent, facts_got = scratch
    me = lax.axis_index("col")
    chunks = tokens // chunk
    per_group = GROUP // chunk
    groups = tokens // GROUP
    edge = size - 1

    def far(place):
        return jnp.maximum(place, edge - place) * hop if scatter is not None else place * 0

    def remote(source, target, sent, got, device):
        return pltpu.make_async_remote_copy(
            src_ref=source,
            dst_ref=target,
            send_sem=sent,
            recv_sem=got,
            device_id={"col": device},
            device_id_type=MESH,
        )

    def rows(index):
        return pl.ds(pl.multiple_of(index * chunk, chunk), chunk)

    def group_rows(group):
        return pl.ds(pl.multiple_of(group * GROUP, GROUP), GROUP)

    def sum_copy(shard, slot, index, device):
        return remote(
            scatter.at[rows(index), pl.ds(shard * width, width)],
            recv.at[slot, rows(index)],
            sums_sent.at[shard, index],
            sums_got.at[slot, index],
            device,
        )

    def block_copy(place, index, way, device):
        return remote(
            blocks.at[place, rows(index)],
            blocks.at[place, rows(index)],
            blocks_sent.at[way, place, index],
            blocks_got.at[place, index],
            device,
        )

    def fact_copy(place, group, device):
        return remote(
            facts.at[group, pl.ds(pl.multiple_of(place * 8, 8), 8)],
            facts.at[group, pl.ds(pl.multiple_of(place * 8, 8), 8)],
            facts_sent.at[device, group],
            facts_got.at[place, group],
            device,
        )

    right = jnp.minimum(me + 1, edge)
    left = jnp.maximum(me - 1, 0)
    other = jnp.where(me == edge, left, right)

    def inside(index):
        return (index >= 0) & (index < chunks)

    def relay_sum(shard, slot, index, fresh, target):
        columns = slice(shard * width, (shard + 1) * width)

        @pl.when(jnp.logical_not(fresh))
        def _():
            sum_copy(shard, shard, index, other).wait_recv()
            total = scatter[rows(index), columns].astype(f32) + recv[shard, rows(index)].astype(f32)
            scatter[rows(index), columns] = total.astype(jnp.bfloat16)

        sum_copy(shard, slot, index, target).start()

    def relay_sums(step):
        index = step - me * hop

        @pl.when(inside(index))
        def _():
            for shard in range(size - 1, 0, -1):

                @pl.when(shard > me)
                def _():
                    slot = jnp.where(me + 1 == shard, size, shard)
                    relay_sum(shard, slot, index, me == 0, right)

        back = step - (edge - me) * hop

        @pl.when(inside(back))
        def _():
            for shard in range(size - 1):

                @pl.when(shard < me)
                def _():
                    relay_sum(shard, shard, back, me == edge, left)

    def ready(step):
        index = step - far(me)

        @pl.when(inside(index))
        def _():
            if scatter is not None:

                @pl.when(me > 0)
                def _():
                    sum_copy(0, size, index, other).wait_recv()

                @pl.when(me < edge)
                def _():
                    sum_copy(0, me, index, other).wait_recv()

                start = pl.multiple_of(me * width, width)
                total = scatter[rows(index), pl.ds(start, width)].astype(f32)
                total = total + jnp.where(me > 0, recv[size, rows(index)].astype(f32), 0.0)
                total = total + jnp.where(me < edge, recv[me, rows(index)].astype(f32), 0.0)
            else:
                total = None
            columns, block = prepare(rows(index), total)
            lane = lax.broadcasted_iota(jnp.int32, (chunk, 128), 1)
            packed = jnp.zeros((chunk, 128), f32)
            for place, column in enumerate(columns):
                packed = jnp.where(lane == place, column, packed)
            within = lax.rem(index, per_group)
            own_facts[pl.ds(pl.multiple_of(within * chunk, chunk), chunk), :] = packed
            if gather:
                blocks[me, rows(index)] = block

                @pl.when(me < edge)
                def _():
                    block_copy(me, index, 0, right).start()

                @pl.when(me > 0)
                def _():
                    block_copy(me, index, 1, left).start()

            @pl.when(within == per_group - 1)
            def _():
                group = index // per_group
                turned = own_facts[...].T
                facts[group, pl.ds(pl.multiple_of(me * 8, 8), 8), :] = turned[:8]
                for place in range(size):

                    @pl.when(place != me)
                    def _():
                        fact_copy(me, group, place).start()

    def relay_blocks(step):
        for near in range(1, size):
            for way, place in ((0, me - near), (1, me + near)):
                index = step - far(place) - near * hop

                @pl.when((place >= 0) & (place < size) & inside(index))
                def _():
                    block_copy(place, index, way, other).wait_recv()
                    onward = (me < edge) if way == 0 else (me > 0)

                    @pl.when(onward)
                    def _():
                        block_copy(place, index, way, right if way == 0 else left).start()

    longest = 2 * edge * hop if scatter is not None and gather else edge * hop

    def conclude(step):
        index = step - longest

        @pl.when(inside(index) & (lax.rem(index, per_group) == per_group - 1))
        def _():
            group = index // per_group
            for place in range(size):

                @pl.when(place != me)
                def _():
                    fact_copy(place, group, other).wait_recv()

            finish(group, group_rows(group), facts[group].T)

    barrier = pltpu.get_barrier_semaphore()
    for place in range(size):

        @pl.when(place != me)
        def _():
            pl.semaphore_signal(barrier, inc=1, device_id={"col": place}, device_id_type=MESH)

    line = lax.axis_index("row")
    for place in range(rows_too):

        @pl.when(place != line)
        def _():
            pl.semaphore_signal(barrier, inc=1, device_id={"row": place}, device_id_type=MESH)

    if scatter is not None:
        order = sorted(range(size), key=lambda shard: -max(shard, edge - shard))
        for shard in order:
            produce(group_rows(0), shard, True)
    pl.semaphore_wait(barrier, size - 1 + max(rows_too - 1, 0))

    def step_all(step, carry):
        if scatter is not None:
            relay_sums(step)
        ready(step)
        if gather:
            relay_blocks(step)
        conclude(step)
        if scatter is not None:
            following = step // per_group + 1
            for part in range(per_group):

                @pl.when((following < groups) & (lax.rem(step, per_group) == part))
                def _():
                    for shard in range(part * size // per_group, (part + 1) * size // per_group):
                        produce(group_rows(following), shard, False)

        if during is not None:

            @pl.when(inside(step))
            def _():
                during(rows(step))

        return carry

    lax.fori_loop(0, chunks + longest, step_all, 0)

    def drain(index, carry):
        if scatter is not None:
            for shard in range(size):

                @pl.when(shard != me)
                def _():
                    sum_copy(shard, shard, index, other).wait_send()

        if gather:
            for place in range(size):

                @pl.when((place <= me) & (me < edge))
                def _():
                    block_copy(place, index, 0, other).wait_send()

                @pl.when((place >= me) & (me > 0))
                def _():
                    block_copy(place, index, 1, other).wait_send()

        return carry

    lax.fori_loop(0, chunks, drain, 0)

    def drain_facts(group, carry):
        for place in range(size):

            @pl.when(place != me)
            def _():
                fact_copy(me, group, place).wait_send()

        return carry

    lax.fori_loop(0, groups, drain_facts, 0)


def exchange_scratch(size, tokens, width, chunk, scatter, gather):
    chunks = tokens // chunk
    groups = tokens // GROUP
    dma = pltpu.SemaphoreType.DMA
    tiny = (1, chunk, 128)
    return [
        pltpu.VMEM((size + 1, tokens, width) if scatter else tiny, jnp.bfloat16),
        pltpu.VMEM((size, tokens, width) if gather else tiny, jnp.bfloat16),
        pltpu.VMEM((groups, 128, 128), f32),
        pltpu.VMEM((GROUP, 128), f32),
        dma((size, chunks) if scatter else (1, 1)),
        dma((size + 1, chunks) if scatter else (1, 1)),
        dma((2, size, chunks) if gather else (1, 1, 1)),
        dma((size, chunks) if gather else (1, 1)),
        dma((size, groups)),
        dma((size, groups)),
    ]


def call(body, operands, places, outs, out_places, scratch, name, ident, cost=10**11):
    moved = sum(array.size * array.dtype.itemsize for array in list(operands) + outs)
    return pl.pallas_call(
        body,
        out_shape=outs,
        in_specs=[pl.BlockSpec(memory_space=place) for place in places],
        out_specs=[pl.BlockSpec(memory_space=place) for place in out_places],
        scratch_shapes=scratch,
        compiler_params=pltpu.CompilerParams(
            collective_id=ident, has_side_effects=True, vmem_limit_bytes=60 * 2**20
        ),
        cost_estimate=pl.CostEstimate(flops=cost, bytes_accessed=moved, transcendentals=0),
        name=name,
    )(*operands)


def held(*arrays):
    return [pltpu.VMEM(array.shape, array.dtype) for array in arrays]


def start_loads(pairs, sems):
    copies = [
        pltpu.make_async_copy(source, target, sems.at[place])
        for place, (source, target) in enumerate(pairs)
    ]
    for copy in copies:
        copy.start()
    return copies


def group_store(source, target, sems):
    groups = source.shape[0] // GROUP

    def copy(group):
        rows = pl.ds(pl.multiple_of(group * GROUP, GROUP), GROUP)
        return pltpu.make_async_copy(source.at[rows], target.at[rows], sems.at[group])

    def wait_all():
        def one(group, carry):
            copy(group).wait()
            return carry

        lax.fori_loop(0, groups, one, 0)

    return lambda group: copy(group).start(), wait_all


def norm_stats(value):
    mean = jnp.sum(value, -1, keepdims=True) * (1.0 / value.shape[-1])
    center = value - mean
    return mean, center, jnp.sum(center * center, -1, keepdims=True)


def norm_whole(size, width, turned):
    means = [turned[:, 8 * z : 8 * z + 1] for z in range(size)]
    squares = [turned[:, 8 * z + 1 : 8 * z + 2] for z in range(size)]
    mean = sum(means[1:], means[0]) * (1.0 / size)
    shifts = [own - mean for own in means]
    spread = sum(squares[1:], squares[0])
    for shift in shifts:
        spread = spread + width * shift * shift
    return shifts, lax.rsqrt(spread * (1.0 / (size * width)) + EPSILON)


def norm_finish(size, width, blocks, scale, whole, store):
    def finish(group, rows, turned):
        shifts, rate = norm_whole(size, width, turned)
        scale[rows, :] = rate
        for z in range(size):
            value = (blocks[z, rows].astype(f32) + shifts[z]) * rate
            whole[rows, z * width : (z + 1) * width] = value.astype(jnp.bfloat16)
        store(group)

    return finish


def norm_in_kernel(
    size,
    chunk,
    hop,
    coeffs,
    streams,
    grads_in,
    whole_out,
    scale,
    branch_grad,
    whole,
    grads,
    loads,
    stores,
    *scratch,
):
    count, tokens, width = streams.shape
    waits = start_loads(((grads_in, grads),), loads)
    store, wait_stores = group_store(whole, whole_out, stores)

    def prepare(rows, total):
        mixed = coeffs[0] * streams[0, rows].astype(f32)
        for k in range(1, count):
            mixed = mixed + coeffs[k] * streams[k, rows].astype(f32)
        mean, center, square = norm_stats(mixed)
        return (mean, square), center.astype(jnp.bfloat16)

    def during(rows):
        @pl.when(rows.start == 0)
        def _():
            waits[0].wait()

        value = coeffs[count] * grads[0, rows].astype(f32)
        for k in range(1, count):
            value = value + coeffs[count + k] * grads[k, rows].astype(f32)
        branch_grad[rows, :] = value.astype(jnp.bfloat16)

    finish = norm_finish(size, width, scratch[1], scale, whole, store)
    line_exchange(
        size, tokens, width, chunk, hop, None, True, None, prepare, finish, scratch, during
    )
    wait_stores()


def norm_in(size, streams, grads, coeffs, chunk=64, hop=1):
    _, tokens, width = streams.shape
    whole = jax.ShapeDtypeStruct((tokens, size * width), jnp.bfloat16)
    return call(
        functools.partial(norm_in_kernel, size, chunk, hop),
        (coeffs, streams, grads),
        (SM, VM, pl.ANY),
        [
            whole,
            jax.ShapeDtypeStruct((tokens, 1), f32),
            jax.ShapeDtypeStruct((tokens, width), jnp.bfloat16),
        ],
        (pl.ANY, VM, VM),
        held(whole, grads)
        + [pltpu.SemaphoreType.DMA((1,)), pltpu.SemaphoreType.DMA((tokens // GROUP,))]
        + exchange_scratch(size, tokens, width, chunk, False, True),
        "norm_in",
        1,
    )


def norm_mid_kernel(
    size,
    chunk,
    hop,
    coeffs,
    attended_in,
    rows_in,
    streams_in,
    whole_out,
    scale,
    branch,
    attended,
    weights,
    streams,
    scatter,
    whole,
    loads,
    stores,
    *scratch,
):
    count, tokens, width = streams.shape
    heads = attended.shape[1]
    own_columns = rows_in.at[:, pl.ds(rows_in.shape[1] - heads, heads)]
    waits = start_loads(
        ((attended_in, attended), (own_columns, weights), (streams_in, streams)), loads
    )
    store, wait_stores = group_store(whole, whole_out, stores)
    waits[0].wait()
    waits[1].wait()

    def produce(rows, shard, first):
        columns = slice(shard * width, (shard + 1) * width)
        scatter[rows, columns] = lax.dot_general(
            attended[rows, :], weights[columns, :], LANES, preferred_element_type=f32
        ).astype(jnp.bfloat16)
        if first and shard == size // 2:
            waits[2].wait()

    def prepare(rows, total):
        branch[rows, :] = total
        mixed = coeffs[count] * total
        for k in range(count):
            mixed = mixed + coeffs[k] * streams[k, rows].astype(f32)
        mean, center, square = norm_stats(mixed)
        return (mean, square), center.astype(jnp.bfloat16)

    finish = norm_finish(size, width, scratch[1], scale, whole, store)
    line_exchange(size, tokens, width, chunk, hop, scatter, True, produce, prepare, finish, scratch)
    wait_stores()


def norm_mid(size, attended, rows, streams, coeffs, chunk=64, hop=1):
    _, tokens, width = streams.shape
    weights = jax.ShapeDtypeStruct((size * width, attended.shape[1]), jnp.bfloat16)
    whole = jax.ShapeDtypeStruct((tokens, size * width), jnp.bfloat16)
    return call(
        functools.partial(norm_mid_kernel, size, chunk, hop),
        (coeffs, attended, rows, streams),
        (SM, pl.ANY, pl.ANY, pl.ANY),
        [
            whole,
            jax.ShapeDtypeStruct((tokens, 1), f32),
            jax.ShapeDtypeStruct((tokens, width), f32),
        ],
        (pl.ANY, VM, VM),
        held(attended, weights, streams, whole, whole)
        + [pltpu.SemaphoreType.DMA((3,)), pltpu.SemaphoreType.DMA((tokens // GROUP,))]
        + exchange_scratch(size, tokens, width, chunk, True, True),
        "norm_mid",
        2,
    )


def back_mid_kernel(
    size,
    chunk,
    hop,
    coeffs,
    gated_in,
    rows_in,
    grads_in,
    normal_in,
    scale,
    whole_out,
    inner_out,
    gated,
    weights,
    grads,
    whole_normal,
    scatter,
    inner,
    whole,
    loads,
    stores,
    inner_stores,
    *scratch,
):
    count, tokens, width = grads.shape
    blocks = scratch[1]
    hidden = gated.shape[2]
    me = lax.axis_index("col")
    edge = size - 1
    order = sorted(range(size), key=lambda shard: -max(shard, edge - shard))
    pairs = [(gated_in.at[:, pl.ds(0, GROUP)], gated.at[:, pl.ds(0, GROUP)])]
    for shard in order:
        shard_rows = pl.ds(shard * width, width)
        pairs.append((rows_in.at[shard_rows, pl.ds(0, 2 * hidden)], weights.at[shard_rows]))
    rest = pl.ds(GROUP, tokens - GROUP)
    pairs = pairs + [
        (gated_in.at[:, rest], gated.at[:, rest]),
        (grads_in, grads),
        (normal_in, whole_normal),
    ]
    waits = start_loads(pairs, loads)
    store, wait_stores = group_store(whole, whole_out, stores)
    store_inner, wait_inner = group_store(inner, inner_out, inner_stores)
    waits[0].wait()

    def produce(rows, shard, first):
        if first:
            waits[1 + order.index(shard)].wait()
        shard_rows = slice(shard * width, (shard + 1) * width)
        total = lax.dot_general(
            gated[0, rows], weights[shard_rows, :hidden], LANES, preferred_element_type=f32
        )
        total = total + lax.dot_general(
            gated[1, rows], weights[shard_rows, hidden:], LANES, preferred_element_type=f32
        )
        scatter[rows, shard_rows] = total.astype(jnp.bfloat16)
        if first and shard == order[-1]:
            for wait in waits[1 + size :]:
                wait.wait()

    def own_normal(rows):
        return whole_normal[rows, pl.ds(pl.multiple_of(me * width, width), width)].astype(f32)

    def prepare(rows, total):
        inner[rows, :] = total
        normal = own_normal(rows)
        part = 1.0 / width
        first = jnp.sum(total, -1, keepdims=True)
        second = jnp.sum(total * normal, -1, keepdims=True)
        plain = jnp.sum(normal, -1, keepdims=True)
        square = jnp.sum(normal * normal, -1, keepdims=True)
        spread = square - plain * plain * part
        cross = second - first * plain * part
        slope = jnp.where(spread > 1e-3, cross / jnp.maximum(spread, 1e-3), 0.0)
        level = (first - slope * plain) * part
        known = coeffs[0] * grads[0, rows].astype(f32)
        for k in range(1, count):
            known = known + coeffs[k] * grads[k, rows].astype(f32)
        block = known + (coeffs[count] * scale[rows, :]) * (total - level - slope * normal)
        return (first, second, level, slope), block.astype(jnp.bfloat16)

    def finish(group, rows, turned):
        first, second = whole_sums(size, width, turned)
        rate = scale[rows, :]
        gain = coeffs[count] * rate
        for z in range(size):
            level = gain * (turned[:, 8 * z + 2 : 8 * z + 3] - first)
            slope = gain * (turned[:, 8 * z + 3 : 8 * z + 4] - second)
            columns = slice(z * width, (z + 1) * width)
            value = blocks[z, rows].astype(f32) + level
            value = value + slope * whole_normal[rows, columns].astype(f32)
            whole[rows, columns] = value.astype(jnp.bfloat16)
        store(group)
        inner[rows, :] = rate * (inner[rows, :] - first - second * own_normal(rows))
        store_inner(group)

    line_exchange(size, tokens, width, chunk, hop, scatter, True, produce, prepare, finish, scratch)
    wait_stores()
    wait_inner()


def whole_sums(size, width, turned):
    first = turned[:, 0:1]
    second = turned[:, 1:2]
    for z in range(1, size):
        first = first + turned[:, 8 * z : 8 * z + 1]
        second = second + turned[:, 8 * z + 1 : 8 * z + 2]
    return first * (1.0 / (size * width)), second * (1.0 / (size * width))


def back_mid(size, gated, rows, grads, whole_normal, scale, coeffs, chunk=64, hop=1):
    _, tokens, width = grads.shape
    whole = jax.ShapeDtypeStruct((tokens, size * width), jnp.bfloat16)
    inner = jax.ShapeDtypeStruct((tokens, width), f32)
    groups = tokens // GROUP
    weights = jax.ShapeDtypeStruct((size * width, 2 * gated.shape[2]), jnp.bfloat16)
    return call(
        functools.partial(back_mid_kernel, size, chunk, hop),
        (coeffs, gated, rows, grads, whole_normal, scale),
        (SM,) + (pl.ANY,) * 4 + (VM,),
        [whole, inner],
        (pl.ANY, pl.ANY),
        held(gated, weights, grads, whole_normal, whole, inner, whole)
        + [
            pltpu.SemaphoreType.DMA((size + 4,)),
            pltpu.SemaphoreType.DMA((groups,)),
            pltpu.SemaphoreType.DMA((groups,)),
        ]
        + exchange_scratch(size, tokens, width, chunk, True, True),
        "back_mid",
        3,
        10**9,
    )


def tile_sum(product):
    height, width = product.shape
    folded = jnp.sum(product.reshape(height // 8, 8, width), 0)
    total = folded[:, :128]
    for start in range(128, width, 128):
        total = total + folded[:, start : start + 128]
    return total


def back_in_kernel(
    size,
    chunk,
    hop,
    coeffs,
    heads_in,
    rows_in,
    normal,
    scale,
    streams_in,
    grads_in,
    branch_one_in,
    branch_two_in,
    inner_two_in,
    final_out,
    grad_streams_out,
    whole_products,
    heads,
    weights,
    streams,
    grads,
    branch_one,
    branch_two,
    inner_two,
    final,
    grad_streams,
    scatter,
    inner,
    products,
    shares,
    loads,
    final_stores,
    stores,
    shares_sent,
    shares_got,
    *scratch,
):
    count, tokens, width = streams.shape
    square = count * count
    edge = size - 1
    order = sorted(range(size), key=lambda shard: -max(shard, edge - shard))
    pairs = [(heads_in.at[pl.ds(0, GROUP)], heads.at[pl.ds(0, GROUP)])]
    for shard in order:
        shard_rows = pl.ds(shard * width, width)
        own_columns = pl.ds(0, heads.shape[1])
        pairs.append((rows_in.at[shard_rows, own_columns], weights.at[shard_rows]))
    rest = pl.ds(GROUP, tokens - GROUP)
    pairs = pairs + [
        (heads_in.at[rest], heads.at[rest]),
        (streams_in, streams),
        (grads_in, grads),
        (branch_one_in, branch_one),
        (branch_two_in, branch_two),
        (inner_two_in, inner_two),
    ]
    waits = start_loads(pairs, loads)
    products[...] = jnp.zeros_like(products)
    waits[0].wait()

    def produce(rows, shard, first):
        if first:
            waits[1 + order.index(shard)].wait()
        shard_rows = slice(shard * width, (shard + 1) * width)
        total = lax.dot_general(
            heads[rows, :], weights[shard_rows, :], LANES, preferred_element_type=f32
        )
        scatter[rows, shard_rows] = total.astype(jnp.bfloat16)
        if first and shard == order[-1]:
            for wait in waits[1 + size :]:
                wait.wait()

    def prepare(rows, total):
        inner[rows, :] = total
        first = jnp.sum(total, -1, keepdims=True)
        second = jnp.sum(total * normal[rows, :].astype(f32), -1, keepdims=True)
        return (first, second), None

    def store(stream, group):
        rows = pl.ds(pl.multiple_of(group * GROUP, GROUP), GROUP)
        return pltpu.make_async_copy(
            grad_streams.at[stream, rows], grad_streams_out.at[stream, rows], stores.at[stream, group]
        )

    def finish(group, rows, turned):
        first, second = whole_sums(size, width, turned)
        own = scale[rows, :] * (inner[rows, :] - first - second * normal[rows, :].astype(f32))
        below = inner_two[rows, :]
        for i in range(count):
            value = coeffs[square + i] * below + coeffs[square + 3 * count + i] * own
            for k in range(count):
                value = value + coeffs[i * count + k] * grads[k, rows].astype(f32)
            grad_streams[i, rows] = value
            store(i, group).start()
            place = square + 3 * count + 1 + i
            products[place] = products[place] + tile_sum(streams[i, rows].astype(f32) * own)

    def store_final(rows, index):
        return pltpu.make_async_copy(
            final.at[:, rows], final_out.at[:, rows], final_stores.at[index]
        )

    def during(rows):
        values = [streams[i, rows].astype(f32) for i in range(count)]
        above = [grads[i, rows].astype(f32) for i in range(count)]
        one = branch_one[rows, :]
        two = branch_two[rows, :].astype(f32)
        below = inner_two[rows, :]
        for j in range(count):
            value = coeffs[square + count + j] * one + coeffs[square + 2 * count + j] * two
            for k in range(count):
                value = value + coeffs[k * count + j] * values[k]
            final[j, rows] = value.astype(jnp.bfloat16)
        pairs = [(a, b) for a in values for b in above]
        pairs = pairs + [(a, below) for a in values]
        pairs = pairs + [(one, b) for b in above]
        pairs = pairs + [(a, two) for a in above]
        pairs = pairs + [(one, below)]
        for place, (a, b) in enumerate(pairs):
            products[place] = products[place] + tile_sum(a * b)
        store_final(rows, rows.start // chunk).start()

    count_rows = lax.axis_size("row")
    line_exchange(
        size,
        tokens,
        width,
        chunk,
        hop,
        scatter,
        False,
        produce,
        prepare,
        finish,
        scratch,
        during,
        count_rows,
    )
    total = jnp.sum(jnp.sum(products[...], 1), -1, keepdims=True)
    total = jnp.broadcast_to(total, whole_products.shape)
    for axis, members, base in (("col", size, 0), ("row", count_rows, size)):
        here = lax.axis_index(axis)

        def share_copy(source, member):
            return pltpu.make_async_remote_copy(
                src_ref=shares.at[base + source],
                dst_ref=shares.at[base + source],
                send_sem=shares_sent.at[base + member],
                recv_sem=shares_got.at[base + source],
                device_id={axis: member},
                device_id_type=MESH,
            )

        shares[base + here] = total
        for member in range(members):

            @pl.when(member != here)
            def _():
                share_copy(here, member).start()

        for member in range(members):

            @pl.when(member != here)
            def _():
                share_copy(member, member).wait()

        total = shares[base]
        for member in range(1, members):
            total = total + shares[base + member]
    whole_products[...] = total

    def wait_final(index, carry):
        store_final(pl.ds(pl.multiple_of(index * chunk, chunk), chunk), index).wait()
        return carry

    lax.fori_loop(0, tokens // chunk, wait_final, 0)

    def wait_streams(group, carry):
        for i in range(count):
            store(i, group).wait()
        return carry

    lax.fori_loop(0, tokens // GROUP, wait_streams, 0)


def back_in(
    size,
    coeffs,
    heads,
    rows,
    normal,
    scale,
    streams,
    grads,
    branch_one,
    branch_two,
    inner_two,
    chunk=64,
    hop=2,
):
    count, tokens, width = streams.shape
    products = -(-(count * count + 4 * count + 1) // 8) * 8
    final = jax.ShapeDtypeStruct(streams.shape, jnp.bfloat16)
    grad_streams = jax.ShapeDtypeStruct(streams.shape, f32)
    members = size + lax.axis_size("row")
    dma = pltpu.SemaphoreType.DMA
    return call(
        functools.partial(back_in_kernel, size, chunk, hop),
        (
            coeffs,
            heads,
            rows,
            normal,
            scale,
            streams,
            grads,
            branch_one,
            branch_two,
            inner_two,
        ),
        (SM, pl.ANY, pl.ANY, VM, VM) + (pl.ANY,) * 5,
        [final, grad_streams, jax.ShapeDtypeStruct((products, 128), f32)],
        (pl.ANY, pl.ANY, VM),
        held(
            heads,
            jax.ShapeDtypeStruct((size * width, heads.shape[1]), jnp.bfloat16),
            streams,
            grads,
            branch_one,
            branch_two,
            inner_two,
            final,
            grad_streams,
        )
        + [
            pltpu.VMEM((tokens, size * width), jnp.bfloat16),
            pltpu.VMEM((tokens, width), f32),
            pltpu.VMEM((products, 8, 128), f32),
            pltpu.VMEM((members, products, 128), f32),
            dma((size + 7,)),
            dma((tokens // chunk,)),
            dma((count, tokens // GROUP)),
            dma((members,)),
            dma((members,)),
        ]
        + exchange_scratch(size, tokens, width, chunk, True, False),
        "back_in",
        4,
    )


def tiled(body, grid, operands, specs, outs, out_specs, scratch, flops, name):
    moved = sum(array.size * array.dtype.itemsize for array in list(operands) + (list(outs) if isinstance(outs, list) else [outs]))
    return pl.pallas_call(
        body,
        grid=grid,
        out_shape=outs,
        in_specs=specs,
        out_specs=out_specs,
        scratch_shapes=scratch,
        compiler_params=pltpu.CompilerParams(vmem_limit_bytes=60 * 2**20),
        cost_estimate=pl.CostEstimate(flops=flops, bytes_accessed=moved, transcendentals=0),
        name=name,
    )(*operands)


def gate_kernel(whole, gate_rows, upper_rows, active, by_gate, by_upper):
    gate = jnp.dot(whole[...], gate_rows[...], preferred_element_type=f32)
    upper = jnp.dot(whole[...], upper_rows[...], preferred_element_type=f32)
    sigma = jax.nn.sigmoid(gate)
    silu = gate * sigma
    active[...] = (silu * upper).astype(jnp.bfloat16)
    by_gate[...] = (upper * sigma * (1.0 + gate * (1.0 - sigma))).astype(jnp.bfloat16)
    by_upper[...] = silu.astype(jnp.bfloat16)


def gate_forward(whole, weights, tile=256):
    tokens, features = whole.shape
    hidden = weights.shape[1] // 3
    tile = min(tile, hidden)
    tiles = hidden // tile
    out = pl.BlockSpec((tokens, tile), lambda j: (0, j))
    return tiled(
        gate_kernel,
        (tiles,),
        (whole, weights, weights),
        [
            pl.BlockSpec((tokens, features), lambda j: (0, 0)),
            pl.BlockSpec((features, tile), lambda j: (0, j)),
            pl.BlockSpec((features, tile), lambda j: (0, j + tiles)),
        ],
        [jax.ShapeDtypeStruct((tokens, hidden), jnp.bfloat16)] * 3,
        [out] * 3,
        [],
        4 * tokens * features * hidden,
        "gate_forward",
    )


def gate_back_kernel(whole, rows, by_gate, by_upper, grads):
    grad = jnp.dot(whole[...], rows[...], preferred_element_type=f32)
    grads[0] = (grad * by_gate[...].astype(f32)).astype(jnp.bfloat16)
    grads[1] = (grad * by_upper[...].astype(f32)).astype(jnp.bfloat16)


def gate_back(whole, weights, by_gate, by_upper, tile=512):
    tokens, features = whole.shape
    hidden = weights.shape[1] // 3
    tile = min(tile, hidden)
    tiles = hidden // tile
    part = pl.BlockSpec((tokens, tile), lambda j: (0, j))
    return tiled(
        gate_back_kernel,
        (tiles,),
        (whole, weights, by_gate, by_upper),
        [
            pl.BlockSpec((tokens, features), lambda j: (0, 0)),
            pl.BlockSpec((features, tile), lambda j: (0, 2 * tiles + j)),
            part,
            part,
        ],
        jax.ShapeDtypeStruct((2, tokens, hidden), jnp.bfloat16),
        pl.BlockSpec((2, tokens, tile), lambda j: (0, 0, j)),
        [],
        2 * tokens * features * hidden,
        "gate_back",
    )


def outer_kernel(cut, left, right, other_left, other_right, out, turned):
    step = pl.program_id(0)

    @pl.when(step == 0)
    def _():
        turned[...] = left[...].T

    @pl.when(step == cut)
    def _():
        turned[...] = other_left[...].T

    @pl.when(step < cut)
    def _():
        out[...] = jnp.dot(turned[...], right[...], preferred_element_type=f32).astype(jnp.bfloat16)

    @pl.when(step >= cut)
    def _():
        out[...] = jnp.dot(turned[...], other_right[...], preferred_element_type=f32).astype(
            jnp.bfloat16
        )


def outer(left, right, other_left, other_right, tile=512, name="outer"):
    tokens, rows = left.shape
    tile = min(tile, other_right.shape[1])
    other = other_right.shape[1] // tile
    if right.ndim == 3:
        tiles = right.shape[2] // tile
        cut = right.shape[0] * tiles
        clip = lambda j: jnp.minimum(j, cut - 1)
        spec = pl.BlockSpec((None, tokens, tile), lambda j: (clip(j) // tiles, 0, clip(j) % tiles))
    else:
        cut = right.shape[1] // tile
        spec = pl.BlockSpec((tokens, tile), lambda j: (0, jnp.minimum(j, cut - 1)))
    whole = pl.BlockSpec((tokens, rows), lambda j: (0, 0))
    return tiled(
        functools.partial(outer_kernel, cut),
        (cut + other,),
        (left, right, other_left, other_right),
        [whole, spec, whole, pl.BlockSpec((tokens, tile), lambda j: (0, jnp.maximum(j - cut, 0)))],
        jax.ShapeDtypeStruct((rows, (cut + other) * tile), jnp.bfloat16),
        pl.BlockSpec((rows, tile), lambda j: (0, j)),
        [pltpu.VMEM((rows, tokens), jnp.bfloat16)],
        2 * tokens * rows * (cut + other) * tile,
        name,
    )


def product_kernel(dims, left, right, out):
    total = lax.dot_general(left[...], right[...], dims, preferred_element_type=f32)
    out[...] = total.astype(out.dtype)


def product(left, right, start, columns, kind=jnp.bfloat16, tile=512, name="product"):
    tokens, depth = left.shape
    tile = min(tile, columns)
    first = start // tile
    return tiled(
        functools.partial(product_kernel, (((1,), (0,)), ((), ()))),
        (columns // tile,),
        (left, right),
        [
            pl.BlockSpec((tokens, depth), lambda j: (0, 0)),
            pl.BlockSpec((depth, tile), lambda j: (0, first + j)),
        ],
        jax.ShapeDtypeStruct((tokens, columns), kind),
        pl.BlockSpec((tokens, tile), lambda j: (0, j)),
        [],
        2 * tokens * depth * columns,
        name,
    )


def product_turned(left, right, place, tile=512, name="product_turned"):
    tokens, depth = left.shape
    rows = right.shape[0]
    tile = min(tile, rows)
    return tiled(
        functools.partial(product_kernel, LANES),
        (rows // tile,),
        (left, right),
        [
            pl.BlockSpec((tokens, depth), lambda j: (0, 0)),
            pl.BlockSpec((tile, depth), lambda j: (j, place)),
        ],
        jax.ShapeDtypeStruct((tokens, rows), jnp.bfloat16),
        pl.BlockSpec((tokens, tile), lambda j: (0, j)),
        [],
        2 * tokens * depth * rows,
        name,
    )


def block_probs(queries, key_heads, rows_docs, columns_docs, start):
    scores = lax.dot_general(queries, key_heads, LANES, preferred_element_type=f32)
    scores = scores * HEAD_DIM ** (-0.5)
    row = lax.broadcasted_iota(jnp.int32, scores.shape, 0) + start
    column = lax.broadcasted_iota(jnp.int32, scores.shape, 1)
    scores = jnp.where((rows_docs == columns_docs) & (column <= row), scores, MASKED)
    expo = jnp.exp(scores - jnp.max(scores, -1, keepdims=True))
    return expo * (1.0 / jnp.sum(expo, -1, keepdims=True))


def attend_forward_kernel(
    block, query, key, value, cosine, sine, column, row, queries, key_heads, value_heads, attended
):
    length = query.shape[0]

    def turn(values):
        return (values * cosine[...] + pltpu.roll(values, HEAD_DIM // 2, 1) * sine[...]).astype(
            jnp.bfloat16
        )

    queries[...] = turn(query[...])
    key_heads[...] = turn(key[...])
    value_heads[...] = value[...].astype(jnp.bfloat16)
    for start in range(0, length, block):
        end = start + block
        probs = block_probs(
            queries[start:end], key_heads[:end], column[start:end], row[:, :end], start
        )
        result = jnp.dot(
            probs.astype(jnp.bfloat16), value_heads[:end], preferred_element_type=f32
        )
        attended[start:end, :] = result.astype(jnp.bfloat16)


def attend_forward(projected, cosine, sine, column, row):
    length, width = projected.shape
    width = width // 3
    heads = width // HEAD_DIM
    block = min(256, length)

    def head(offset):
        return pl.BlockSpec((length, HEAD_DIM), lambda h: (0, h + offset))

    def fixed(array):
        return pl.BlockSpec(array.shape, lambda h: (0, 0))

    return pl.pallas_call(
        functools.partial(attend_forward_kernel, block),
        grid=(heads,),
        out_shape=[jax.ShapeDtypeStruct((length, width), jnp.bfloat16)] * 4,
        in_specs=[head(0), head(heads), head(2 * heads)]
        + [fixed(array) for array in (cosine, sine, column, row)],
        out_specs=[head(0)] * 4,
        compiler_params=pltpu.CompilerParams(vmem_limit_bytes=60 * 2**20),
        name="attend_forward",
    )(projected, projected, projected, cosine, sine, column, row)


def attend_back_kernel(
    block,
    queries,
    key_heads,
    value_heads,
    grad_result,
    cosine,
    sine,
    column,
    row,
    grad_query,
    grad_key,
    grad_value,
    key_sum,
    value_sum,
):
    length = queries.shape[0]
    factor = HEAD_DIM ** (-0.5)

    def turn_back(values, rows):
        values = values * factor
        return (
            values * cosine[rows] - pltpu.roll(values, HEAD_DIM // 2, 1) * sine[rows]
        ).astype(jnp.bfloat16)

    for start in range(length - block, -1, -block):
        end = start + block
        query, grad_part = queries[start:end], grad_result[start:end]
        probs = block_probs(query, key_heads[:end], column[start:end], row[:, :end], start)
        grad_probs = lax.dot_general(
            grad_part, value_heads[:end], LANES, preferred_element_type=f32
        )
        row_sum = jnp.sum(probs * grad_probs, -1, keepdims=True)
        grad_scores = (probs * (grad_probs - row_sum)).astype(jnp.bfloat16)
        grad_part_query = jnp.dot(grad_scores, key_heads[:end], preferred_element_type=f32)
        grad_query[start:end, :] = turn_back(grad_part_query, pl.ds(start, block))
        key_part = lax.dot_general(grad_scores, query, ROWS, preferred_element_type=f32)
        value_part = lax.dot_general(
            probs.astype(jnp.bfloat16), grad_part, ROWS, preferred_element_type=f32
        )
        if end == length:
            key_sum[...] = key_part
            value_sum[...] = value_part
        else:
            key_sum[:end, :] += key_part
            value_sum[:end, :] += value_part
    grad_key[...] = turn_back(key_sum[...], pl.ds(0, length))
    grad_value[...] = value_sum[...].astype(jnp.bfloat16)


def attend_back(queries, key_heads, value_heads, grad_result, cosine, sine, column, row):
    length, width = queries.shape
    heads = width // HEAD_DIM
    block = min(256, length)
    head = pl.BlockSpec((length, HEAD_DIM), lambda h: (0, h))

    def fixed(array):
        return pl.BlockSpec(array.shape, lambda h: (0, 0))

    grads = pl.pallas_call(
        functools.partial(attend_back_kernel, block),
        grid=(heads,),
        out_shape=[jax.ShapeDtypeStruct((length, width), jnp.bfloat16)] * 3,
        in_specs=[head] * 4 + [fixed(array) for array in (cosine, sine, column, row)],
        out_specs=[head] * 3,
        scratch_shapes=[pltpu.VMEM((length, HEAD_DIM), f32)] * 2,
        compiler_params=pltpu.CompilerParams(vmem_limit_bytes=60 * 2**20),
        name="attend_back",
    )(queries, key_heads, value_heads, grad_result, cosine, sine, column, row)
    return jnp.concatenate(grads, 1)


def update(weight, grad, moment, average, rate):
    step_grad = grad + DECAY * weight
    moment_new = MOMENTUM * moment + step_grad
    weight_new = weight - rate * (step_grad + MOMENTUM * moment_new)
    return (weight_new, moment_new, average + (weight_new - average) / (STEP + 1))


def update_kernel(rate, turned, weight, grad, moment, average, *outs):
    value = grad[...].astype(f32)
    results = update(weight[...], value.T if turned else value, moment[...], average[...], rate)
    for out, result in zip(outs, results):
        out[...] = result


def update_blocks(weight, grad, moment, average, rate, start):
    turned = weight.ndim == 2
    rows = grad.shape[0]
    columns = weight.shape[0] if turned else weight.shape[2]
    tile = min(columns, 512)
    tiles = columns // tile
    first = start // tile
    if turned:
        grid = (tiles,)
        own = pl.BlockSpec((tile, rows), lambda j: (j, 0))
        place = pl.BlockSpec((rows, tile), lambda j: (0, first + j))
    else:
        grid = (weight.shape[0], tiles)
        own = pl.BlockSpec((None, rows, tile), lambda k, j: (k, 0, j))
        place = pl.BlockSpec((rows, tile), lambda k, j: (0, first + k * tiles + j))
    return pl.pallas_call(
        functools.partial(update_kernel, rate, turned),
        grid=grid,
        out_shape=[jax.ShapeDtypeStruct(weight.shape, f32)] * 3,
        in_specs=[own, place, own, own],
        out_specs=[own] * 3,
        compiler_params=pltpu.CompilerParams(vmem_limit_bytes=60 * 2**20),
        cost_estimate=pl.CostEstimate(
            flops=10 * weight.size, bytes_accessed=26 * weight.size, transcendentals=0
        ),
        name="update",
    )(weight, grad, moment, average)


def tie(*values):
    return lax.optimization_barrier(values)


def assemble_kernel(size, *refs):
    pieces, whole = refs[:-1], refs[-1]
    width = whole.shape[1] // size
    me = lax.axis_index("col")
    for here in range(size):

        @pl.when(me == here)
        def _():
            for place in range(size):
                columns = slice(place * width, (place + 1) * width)
                whole[:, columns] = pieces[size - 1 + place - here][...]


def assemble(pieces):
    size = (len(pieces) + 1) // 2
    tokens, width = pieces[0].shape
    tile = min(256, tokens)
    return pl.pallas_call(
        functools.partial(assemble_kernel, size),
        grid=(tokens // tile,),
        out_shape=jax.ShapeDtypeStruct((tokens, size * width), pieces[0].dtype),
        in_specs=[pl.BlockSpec((tile, width), lambda i: (i, 0))] * len(pieces),
        out_specs=pl.BlockSpec((tile, size * width), lambda i: (i, 0)),
        compiler_params=pltpu.CompilerParams(vmem_limit_bytes=60 * 2**20),
        name="assemble",
    )(*pieces)


def line_ways():
    size = lax.axis_size("col")
    up = [(i, i + 1) for i in range(size - 1)]
    down = [(i + 1, i) for i in range(size - 1)]
    return size, up, down


def gather_steps(values):
    size, up, down = line_ways()
    before, after = [values], [values]
    for _ in range(size - 1):
        step = (lax.ppermute(before[-1], "col", up), lax.ppermute(after[-1], "col", down))
        step = yield step
        before.append(step[0])
        after.append(step[1])
    yield assemble(before[:0:-1] + after)


def advance(steps, got, *values):
    moved = next(steps) if got is None else steps.send(got)
    tied = tie(*moved, *values)
    return tied[: len(moved)], tied[len(moved) :]


def finish_line(steps, got):
    moved = steps.send(got)
    while isinstance(moved, tuple):
        moved = steps.send(moved)
    return moved


def small_matmul(left, right):
    return jnp.sum(left[:, :, None] * right[None, :, :], 1)


def scatter_rows(grad):
    return lax.psum_scatter(grad, "row", scatter_dimension=0, tiled=True)


def side_by_side(weights, turned):
    return jnp.concatenate([weights[k] for k in range(weights.shape[0])] + [turned.T], 1)


def per_device(
    streams,
    segments,
    attention_in,
    attention_out,
    gate_up,
    down_weights,
    hyper_mix,
    moment_attention_in,
    moment_attention_out,
    moment_gate_up,
    moment_down_weights,
    moment_hyper_mix,
    average_attention_in,
    average_attention_out,
    average_gate_up,
    average_down_weights,
    average_hyper_mix,
    cotangent,
):
    size = lax.axis_size("col")
    low = jnp.bfloat16
    count, length, width = streams.shape
    cosine, sine = rope_tables(segments)

    def gather_rows(weights):
        return lax.all_gather(weights.astype(low), "row", axis=0, tiled=True)

    attention_weights = gather_rows(side_by_side(attention_in, attention_out))
    hidden_weights = gather_rows(side_by_side(gate_up, down_weights))

    one, two = hyper_mix[0], hyper_mix[1]
    across_one, across_two = one[:, 1 : 1 + count], two[:, 1 : 1 + count]
    through = small_matmul(across_one, across_two)
    in_two = small_matmul(across_one, two[:, :1])[:, 0]
    out_one = small_matmul(one[None, :, 1 + count], across_two)[0]
    turn = jnp.sum(one[:, 1 + count] * two[:, 0])

    whole_one, scale_one, grad_two = norm_in(
        size, streams, cotangent, jnp.concatenate([one[:, 0], two[:, 1 + count]])
    )
    heads = attention_in.shape[2]
    steps = gather_steps(grad_two)
    projected = product(whole_one, attention_weights, 0, 3 * heads, f32, heads, "project_in")
    queries, key_heads, value_heads, attended = attend_forward(
        projected, cosine, sine, segments.T, segments
    )
    got, (attended,) = advance(steps, None, attended)
    mid_coeffs = jnp.concatenate([in_two, turn[None]])
    whole_two, scale_two, branch_one = norm_mid(
        size, attended, attention_weights, streams, mid_coeffs
    )

    whole_two, *got = tie(whole_two, *got)
    active, by_gate, by_upper = gate_forward(whole_two, hidden_weights)
    got, (active,) = advance(steps, tuple(got), active)
    partial_two = product_turned(active, hidden_weights, 2, name="project_out")
    got, (partial_two,) = advance(steps, got, partial_two)
    whole_grad_two = finish_line(steps, got)
    branch_two = lax.psum_scatter(partial_two, "col", scatter_dimension=1, tiled=True)
    grad_gated = gate_back(whole_grad_two, hidden_weights, by_gate, by_upper)
    grad_hidden = outer(whole_two, grad_gated, whole_grad_two, active, name="outer_hidden")
    grad_hidden, grad_gated = tie(grad_hidden, grad_gated)
    grad_hidden = scatter_rows(grad_hidden)
    back_coeffs = jnp.concatenate([out_one, turn[None]])
    whole_grad_one, inner_two = back_mid(
        size, grad_gated, hidden_weights, cotangent, whole_two, scale_two, back_coeffs
    )

    whole_grad_one, branch_two = tie(whole_grad_one, branch_two)
    grad_attended = product(
        whole_grad_one, attention_weights, 3 * heads, heads, low, heads, "back_out"
    )
    grad_heads = attend_back(
        queries, key_heads, value_heads, grad_attended, cosine, sine, segments.T, segments
    )
    grad_attention = outer(
        whole_one, grad_heads, whole_grad_one, attended, name="outer_attention"
    )
    grad_attention, grad_heads, grad_hidden = tie(grad_attention, grad_heads, grad_hidden)
    grad_attention = scatter_rows(grad_attention)
    end_coeffs = jnp.concatenate(
        [through.reshape(-1), in_two, out_one, two[:, 1 + count], one[:, 0]]
    )
    own_normal = lax.dynamic_slice_in_dim(whole_one, lax.axis_index("col") * width, width, 1)
    final, grad_streams, products = back_in(
        size,
        end_coeffs,
        grad_heads,
        attention_weights,
        own_normal,
        scale_one,
        streams,
        cotangent,
        branch_one,
        branch_two,
        inner_two,
    )

    products = products[:, 0]
    cuts = [count * count, count, count, count, 1, count]
    parts = []
    start = 0
    for cut in cuts:
        parts.append(products[start : start + cut])
        start = start + cut
    streams_grads, streams_two, branch_grads, grads_branch, branch_inner, streams_one = parts
    streams_grads = streams_grads.reshape(count, count)
    hyper_one = jnp.concatenate(
        [
            streams_one[:, None],
            small_matmul(streams_grads, across_two.T) + streams_two[:, None] * two[None, :, 0],
            small_matmul(across_two, branch_grads[:, None]) + (two[:, 0] * branch_inner)[:, None],
        ],
        1,
    )
    hyper_two = jnp.concatenate(
        [
            small_matmul(across_one.T, streams_two[:, None])
            + (one[:, 1 + count] * branch_inner)[:, None],
            small_matmul(across_one.T, streams_grads)
            + one[:, 1 + count][:, None] * branch_grads[None, :],
            grads_branch[:, None],
        ],
        1,
    )
    grad_hyper = jnp.stack([hyper_one, hyper_two])
    tokens_all = length * lax.axis_size("row")
    token_scale = tokens_all ** (-0.5)
    model_rate = D ** (-0.5) * token_scale
    first = update_blocks(
        attention_in, grad_attention, moment_attention_in, average_attention_in, model_rate, 0
    )
    second = update_blocks(
        attention_out,
        grad_attention,
        moment_attention_out,
        average_attention_out,
        model_rate,
        attention_in.shape[0] * heads,
    )
    third = update_blocks(gate_up, grad_hidden, moment_gate_up, average_gate_up, model_rate, 0)
    fourth = update_blocks(
        down_weights,
        grad_hidden,
        moment_down_weights,
        average_down_weights,
        FF ** (-0.5) * token_scale,
        gate_up.shape[0] * gate_up.shape[2],
    )
    fifth = update(
        hyper_mix,
        grad_hyper,
        moment_hyper_mix,
        average_hyper_mix,
        0.05 * (tokens_all * D) ** (-0.5),
    )
    return (
        final,
        grad_streams,
        first[0],
        first[1],
        first[2],
        second[0],
        second[1],
        second[2],
        third[0],
        third[1],
        third[2],
        fourth[0],
        fourth[1],
        fourth[2],
        fifth[0],
        fifth[1],
        fifth[2],
    )


def solution(mesh):
    in_specs = (
        P(None, "row", "col"),
        P("row", None),
        P(None, "row", "col"),
        P("col", "row"),
        P(None, "row", "col"),
        P("col", "row"),
        P(),
        P(None, "row", "col"),
        P("col", "row"),
        P(None, "row", "col"),
        P("col", "row"),
        P(),
        P(None, "row", "col"),
        P("col", "row"),
        P(None, "row", "col"),
        P("col", "row"),
        P(),
        P(None, "row", "col"),
    )
    out_specs = (
        P(None, "row", "col"),
        P(None, "row", "col"),
        P(None, "row", "col"),
        P(None, "row", "col"),
        P(None, "row", "col"),
        P("col", "row"),
        P("col", "row"),
        P("col", "row"),
        P(None, "row", "col"),
        P(None, "row", "col"),
        P(None, "row", "col"),
        P("col", "row"),
        P("col", "row"),
        P("col", "row"),
        P(),
        P(),
        P(),
    )
    return jax.shard_map(
        per_device, mesh=mesh, in_specs=in_specs, out_specs=out_specs, check_vma=False
    )
```

```python
import functools

import jax
import jax.numpy as jnp
from jax import lax
from jax.experimental import pallas as pl
from jax.experimental.pallas import tpu as pltpu
from jax.sharding import PartitionSpec as P

D = 2048
HEAD_DIM = 128
FF = 8192
STEP = 8


EPSILON = 1e-05
MASKED = -1e30
MOMENTUM = 0.9
DECAY = 0.01
GROUP = 128
MESH = pl.DeviceIdType.MESH
VM, SM = pltpu.VMEM, pltpu.SMEM
f32 = jnp.float32
LONGEST = 512
LOG2E = 1.4426950408889634
LANES = (((1,), (1,)), ((), ()))
ROWS = (((0,), (0,)), ((), ()))


def rope_tables(segments):
    segments = segments[0]
    length = segments.shape[0]
    index = jnp.arange(length, dtype=jnp.int32)
    before = jnp.concatenate([jnp.full((1,), -1, jnp.int32), segments[:-1]])
    starts = jnp.where(segments != before, index, 0)
    places = index - lax.cummax(starts)
    rates = 10000.0 ** (-2.0 * jnp.arange(HEAD_DIM // 2).astype(jnp.float32) / HEAD_DIM)
    angle = places[:, None].astype(jnp.float32) * rates
    return (jnp.cos(angle), jnp.sin(angle))


def line_exchange(
    size, tokens, width, chunk, hop, scatter, gather, produce, prepare, finish, scratch, during=None, rows_too=0
):
    recv, blocks, facts, own_facts, sums_sent, sums_got, blocks_sent, blocks_got, facts_sent, facts_got = scratch
    me = lax.axis_index("col")
    chunks = tokens // chunk
    per_group = GROUP // chunk
    groups = tokens // GROUP
    edge = size - 1

    hop, wait_hop, pass_hop = hop

    def far(place):
        lag = jnp.maximum(place, edge - place) * hop + wait_hop
        return lag if scatter is not None else place * 0

    def remote(source, target, sent, got, device):
        return pltpu.make_async_remote_copy(
            src_ref=source,
            dst_ref=target,
            send_sem=sent,
            recv_sem=got,
            device_id={"col": device},
            device_id_type=MESH,
        )

    def rows(index):
        return pl.ds(pl.multiple_of(index * chunk, chunk), chunk)

    def group_rows(group):
        return pl.ds(pl.multiple_of(group * GROUP, GROUP), GROUP)

    def sum_copy(shard, slot, index, device):
        return remote(
            scatter.at[rows(index), pl.ds(shard * width, width)],
            recv.at[slot, rows(index)],
            sums_sent.at[shard, index],
            sums_got.at[slot, index],
            device,
        )

    def block_copy(place, index, way, device):
        return remote(
            blocks.at[place, rows(index)],
            blocks.at[place, rows(index)],
            blocks_sent.at[way, place, index],
            blocks_got.at[place, index],
            device,
        )

    def fact_copy(place, group, device):
        return remote(
            facts.at[group, pl.ds(pl.multiple_of(place * 8, 8), 8)],
            facts.at[group, pl.ds(pl.multiple_of(place * 8, 8), 8)],
            facts_sent.at[device, group],
            facts_got.at[place, group],
            device,
        )

    right = jnp.minimum(me + 1, edge)
    left = jnp.maximum(me - 1, 0)
    other = jnp.where(me == edge, left, right)

    def inside(index):
        return (index >= 0) & (index < chunks)

    def relay_sum(shard, slot, index, fresh, target):
        columns = slice(shard * width, (shard + 1) * width)

        @pl.when(jnp.logical_not(fresh))
        def _():
            sum_copy(shard, shard, index, other).wait_recv()
            total = scatter[rows(index), columns].astype(f32) + recv[shard, rows(index)].astype(f32)
            scatter[rows(index), columns] = total.astype(jnp.bfloat16)

        sum_copy(shard, slot, index, target).start()

    def relay_sums(step):
        index = step - me * hop

        @pl.when(inside(index))
        def _():
            for shard in range(size - 1, 0, -1):

                @pl.when(shard > me)
                def _():
                    slot = jnp.where(me + 1 == shard, size, shard)
                    relay_sum(shard, slot, index, me == 0, right)

        back = step - (edge - me) * hop

        @pl.when(inside(back))
        def _():
            for shard in range(size - 1):

                @pl.when(shard < me)
                def _():
                    relay_sum(shard, shard, back, me == edge, left)

    def ready(step):
        index = step - far(me)

        @pl.when(inside(index))
        def _():
            if scatter is not None:

                @pl.when(me > 0)
                def _():
                    sum_copy(0, size, index, other).wait_recv()

                @pl.when(me < edge)
                def _():
                    sum_copy(0, me, index, other).wait_recv()

                start = pl.multiple_of(me * width, width)
                total = scatter[rows(index), pl.ds(start, width)].astype(f32)
                total = total + jnp.where(me > 0, recv[size, rows(index)].astype(f32), 0.0)
                total = total + jnp.where(me < edge, recv[me, rows(index)].astype(f32), 0.0)
            else:
                total = None
            columns, block = prepare(rows(index), total)
            lane = lax.broadcasted_iota(jnp.int32, (chunk, 128), 1)
            packed = jnp.zeros((chunk, 128), f32)
            for place, column in enumerate(columns):
                packed = jnp.where(lane == place, column, packed)
            within = lax.rem(index, per_group)
            own_facts[pl.ds(pl.multiple_of(within * chunk, chunk), chunk), :] = packed
            if gather:
                blocks[me, rows(index)] = block

                @pl.when(me < edge)
                def _():
                    block_copy(me, index, 0, right).start()

                @pl.when(me > 0)
                def _():
                    block_copy(me, index, 1, left).start()

            @pl.when(within == per_group - 1)
            def _():
                group = index // per_group
                turned = own_facts[...].T
                facts[group, pl.ds(pl.multiple_of(me * 8, 8), 8), :] = turned[:8]
                for place in range(size):

                    @pl.when(place != me)
                    def _():
                        fact_copy(me, group, place).start()

    def relay_blocks(step):
        for near in range(1, size):
            for way, place in ((0, me - near), (1, me + near)):
                index = step - far(place) - near * pass_hop

                @pl.when((place >= 0) & (place < size) & inside(index))
                def _():
                    block_copy(place, index, way, other).wait_recv()
                    onward = (me < edge) if way == 0 else (me > 0)

                    @pl.when(onward)
                    def _():
                        block_copy(place, index, way, right if way == 0 else left).start()

    longest = (edge * hop + wait_hop if scatter is not None else 0) + edge * pass_hop

    def conclude(step):
        index = step - longest

        @pl.when(inside(index) & (lax.rem(index, per_group) == per_group - 1))
        def _():
            group = index // per_group
            for place in range(size):

                @pl.when(place != me)
                def _():
                    fact_copy(place, group, other).wait_recv()

            finish(group, group_rows(group), facts[group].T)

    barrier = pltpu.get_barrier_semaphore()
    for place in range(size):

        @pl.when(place != me)
        def _():
            pl.semaphore_signal(barrier, inc=1, device_id={"col": place}, device_id_type=MESH)

    line = lax.axis_index("row")
    for place in range(rows_too):

        @pl.when(place != line)
        def _():
            pl.semaphore_signal(barrier, inc=1, device_id={"row": place}, device_id_type=MESH)

    if scatter is not None:
        order = sorted(range(size), key=lambda shard: -max(shard, edge - shard))
        for shard in order:
            produce(group_rows(0), shard, True)
    pl.semaphore_wait(barrier, size - 1 + max(rows_too - 1, 0))

    def step_all(step, carry):
        if scatter is not None:
            relay_sums(step)
        ready(step)
        if gather:
            relay_blocks(step)
        conclude(step)
        if scatter is not None:
            following = step // per_group + 1
            for part in range(per_group):

                @pl.when((following < groups) & (lax.rem(step, per_group) == part))
                def _():
                    for shard in range(part * size // per_group, (part + 1) * size // per_group):
                        produce(group_rows(following), shard, False)

        if during is not None:

            @pl.when(inside(step))
            def _():
                during(rows(step))

        return carry

    lax.fori_loop(0, chunks + longest, step_all, 0)

    def drain(index, carry):
        if scatter is not None:
            for shard in range(size):

                @pl.when(shard != me)
                def _():
                    sum_copy(shard, shard, index, other).wait_send()

        if gather:
            for place in range(size):

                @pl.when((place <= me) & (me < edge))
                def _():
                    block_copy(place, index, 0, other).wait_send()

                @pl.when((place >= me) & (me > 0))
                def _():
                    block_copy(place, index, 1, other).wait_send()

        return carry

    lax.fori_loop(0, chunks, drain, 0)

    def drain_facts(group, carry):
        for place in range(size):

            @pl.when(place != me)
            def _():
                fact_copy(me, group, place).wait_send()

        return carry

    lax.fori_loop(0, groups, drain_facts, 0)


def exchange_scratch(size, tokens, width, chunk, scatter, gather):
    chunks = tokens // chunk
    groups = tokens // GROUP
    dma = pltpu.SemaphoreType.DMA
    tiny = (1, chunk, 128)
    return [
        pltpu.VMEM((size + 1, tokens, width) if scatter else tiny, jnp.bfloat16),
        pltpu.VMEM((size, tokens, width) if gather else tiny, jnp.bfloat16),
        pltpu.VMEM((groups, 128, 128), f32),
        pltpu.VMEM((GROUP, 128), f32),
        dma((size, chunks) if scatter else (1, 1)),
        dma((size + 1, chunks) if scatter else (1, 1)),
        dma((2, size, chunks) if gather else (1, 1, 1)),
        dma((size, chunks) if gather else (1, 1)),
        dma((size, groups)),
        dma((size, groups)),
    ]


def call(body, operands, places, outs, out_places, scratch, name, ident, cost=10**11):
    moved = sum(array.size * array.dtype.itemsize for array in list(operands) + outs)
    return pl.pallas_call(
        body,
        out_shape=outs,
        in_specs=[pl.BlockSpec(memory_space=place) for place in places],
        out_specs=[pl.BlockSpec(memory_space=place) for place in out_places],
        scratch_shapes=scratch,
        compiler_params=pltpu.CompilerParams(
            collective_id=ident, has_side_effects=True, vmem_limit_bytes=60 * 2**20
        ),
        cost_estimate=pl.CostEstimate(flops=cost, bytes_accessed=moved, transcendentals=0),
        name=name,
    )(*operands)


def held(*arrays):
    return [pltpu.VMEM(array.shape, array.dtype) for array in arrays]


def start_loads(pairs, sems):
    copies = [
        pltpu.make_async_copy(source, target, sems.at[place])
        for place, (source, target) in enumerate(pairs)
    ]
    for copy in copies:
        copy.start()
    return copies


def group_store(source, target, sems):
    groups = source.shape[0] // GROUP

    def copy(group):
        rows = pl.ds(pl.multiple_of(group * GROUP, GROUP), GROUP)
        return pltpu.make_async_copy(source.at[rows], target.at[rows], sems.at[group])

    def wait_all():
        def one(group, carry):
            copy(group).wait()
            return carry

        lax.fori_loop(0, groups, one, 0)

    return lambda group: copy(group).start(), wait_all


def norm_stats(value):
    mean = jnp.sum(value, -1, keepdims=True) * (1.0 / value.shape[-1])
    center = value - mean
    return mean, center, jnp.sum(center * center, -1, keepdims=True)


def norm_whole(size, width, turned):
    means = [turned[:, 8 * z : 8 * z + 1] for z in range(size)]
    squares = [turned[:, 8 * z + 1 : 8 * z + 2] for z in range(size)]
    mean = sum(means[1:], means[0]) * (1.0 / size)
    shifts = [own - mean for own in means]
    spread = sum(squares[1:], squares[0])
    for shift in shifts:
        spread = spread + width * shift * shift
    return shifts, lax.rsqrt(spread * (1.0 / (size * width)) + EPSILON)


def norm_finish(size, width, blocks, scale, whole, store):
    def finish(group, rows, turned):
        shifts, rate = norm_whole(size, width, turned)
        scale[rows, :] = rate
        for z in range(size):
            value = (blocks[z, rows].astype(f32) + shifts[z]) * rate
            whole[rows, z * width : (z + 1) * width] = value.astype(jnp.bfloat16)
        store(group)

    return finish


def mixings(mix):
    count = mix.shape[1]
    span = range(count)

    def dot(left, right):
        total = left[0] * right[0]
        for a, b in zip(left[1:], right[1:]):
            total = total + a * b
        return total

    across_one = [[mix[0, k, 1 + i] for i in span] for k in span]
    across_two = [[mix[1, i, 1 + j] for i in span] for j in span]
    through = [[dot(across_one[k], across_two[j]) for j in span] for k in span]
    second = [mix[1, i, 0] for i in span]
    outward = [mix[0, i, 1 + count] for i in span]
    in_two = [dot(across_one[k], second) for k in span]
    out_one = [dot(outward, across_two[j]) for j in span]
    return through, in_two, out_one, dot(outward, second)


def norm_in_kernel(
    size,
    chunk,
    hop,
    mix,
    streams,
    grads_in,
    gate_in,
    down_in,
    whole_out,
    scale,
    branch_grad,
    products,
    packed,
    whole,
    grads,
    gate_up,
    down,
    loads,
    stores,
    *scratch,
):
    count, tokens, width = streams.shape
    kinds, _, hidden = gate_up.shape
    tile = min(512, hidden)
    tiles = hidden // tile
    into = [mix[0, k, 0] for k in range(count)]
    onto = [mix[1, k, 1 + count] for k in range(count)]
    products[...] = jnp.zeros_like(products)
    waits = start_loads(((grads_in, grads), (gate_in, gate_up), (down_in, down)), loads)
    store, wait_stores = group_store(whole, whole_out, stores)

    def prepare(rows, total):
        mixed = into[0] * streams[0, rows].astype(f32)
        for k in range(1, count):
            mixed = mixed + into[k] * streams[k, rows].astype(f32)
        mean, center, square = norm_stats(mixed)
        return (mean, square), center.astype(jnp.bfloat16)

    def during(rows):
        @pl.when(rows.start == 0)
        def _():
            for wait in waits:
                wait.wait()

        for piece in range((kinds + 1) * tiles):

            @pl.when(rows.start == piece * chunk)
            def _():
                kind, start = piece // tiles, piece % tiles * tile
                if kind < kinds:
                    value = gate_up[kind, :, start : start + tile]
                else:
                    value = down[start : start + tile, :].T
                packed[:, piece * tile : (piece + 1) * tile] = value.astype(jnp.bfloat16)

        above = [grads[k, rows].astype(f32) for k in range(count)]
        value = onto[0] * above[0]
        for k in range(1, count):
            value = value + onto[k] * above[k]
        branch_grad[rows, :] = value.astype(jnp.bfloat16)
        for i in range(count):
            own = streams[i, rows].astype(f32)
            for k in range(count):
                place = i * count + k
                products[place] = products[place] + tile_sum(own * above[k])

    finish = norm_finish(size, width, scratch[1], scale, whole, store)
    line_exchange(
        size, tokens, width, chunk, hop, None, True, None, prepare, finish, scratch, during
    )
    wait_stores()


def norm_in(size, streams, grads, gate_up, down, mix, chunk=64, hop=(1, 0, 1)):
    _, tokens, width = streams.shape
    whole = jax.ShapeDtypeStruct((tokens, size * width), jnp.bfloat16)
    return call(
        functools.partial(norm_in_kernel, size, chunk, hop),
        (mix, streams, grads, gate_up, down),
        (SM, VM, pl.ANY, pl.ANY, pl.ANY),
        [
            whole,
            jax.ShapeDtypeStruct((tokens, 1), f32),
            jax.ShapeDtypeStruct((tokens, width), jnp.bfloat16),
            jax.ShapeDtypeStruct((streams.shape[0] * grads.shape[0], 8, 128), f32),
            jax.ShapeDtypeStruct(
                (gate_up.shape[1], (gate_up.shape[0] + 1) * gate_up.shape[2]), jnp.bfloat16
            ),
        ],
        (pl.ANY, VM, VM, VM, VM),
        held(whole, grads, gate_up, down)
        + [pltpu.SemaphoreType.DMA((3,)), pltpu.SemaphoreType.DMA((tokens // GROUP,))]
        + exchange_scratch(size, tokens, width, chunk, False, True),
        "norm_in",
        1,
    )


def norm_mid_kernel(
    size,
    chunk,
    hop,
    mix,
    attended_in,
    rows_in,
    streams_in,
    whole_out,
    scale,
    branch,
    attended,
    weights,
    streams,
    scatter,
    whole,
    loads,
    stores,
    *scratch,
):
    count, tokens, width = streams.shape
    in_two, turn = mixings(mix)[1::2]
    heads = attended.shape[1]
    own_columns = rows_in.at[:, pl.ds(rows_in.shape[1] - heads, heads)]
    waits = start_loads(
        ((attended_in, attended), (own_columns, weights), (streams_in, streams)), loads
    )
    store, wait_stores = group_store(whole, whole_out, stores)
    waits[0].wait()
    waits[1].wait()

    def produce(rows, shard, first):
        columns = slice(shard * width, (shard + 1) * width)
        scatter[rows, columns] = lax.dot_general(
            attended[rows, :], weights[columns, :], LANES, preferred_element_type=f32
        ).astype(jnp.bfloat16)
        if first and shard == size // 2:
            waits[2].wait()

    def prepare(rows, total):
        branch[rows, :] = total
        mixed = turn * total
        for k in range(count):
            mixed = mixed + in_two[k] * streams[k, rows].astype(f32)
        mean, center, square = norm_stats(mixed)
        return (mean, square), center.astype(jnp.bfloat16)

    finish = norm_finish(size, width, scratch[1], scale, whole, store)
    line_exchange(size, tokens, width, chunk, hop, scatter, True, produce, prepare, finish, scratch)
    wait_stores()


def norm_mid(size, attended, rows, streams, mix, chunk=64, hop=(1, 0, 1)):
    _, tokens, width = streams.shape
    weights = jax.ShapeDtypeStruct((size * width, attended.shape[1]), jnp.bfloat16)
    whole = jax.ShapeDtypeStruct((tokens, size * width), jnp.bfloat16)
    return call(
        functools.partial(norm_mid_kernel, size, chunk, hop),
        (mix, attended, rows, streams),
        (SM, pl.ANY, pl.ANY, pl.ANY),
        [
            whole,
            jax.ShapeDtypeStruct((tokens, 1), f32),
            jax.ShapeDtypeStruct((tokens, width), f32),
        ],
        (pl.ANY, VM, VM),
        held(attended, weights, streams, whole, whole)
        + [pltpu.SemaphoreType.DMA((3,)), pltpu.SemaphoreType.DMA((tokens // GROUP,))]
        + exchange_scratch(size, tokens, width, chunk, True, True),
        "norm_mid",
        2,
    )


def back_mid_kernel(
    size,
    chunk,
    hop,
    mix,
    gated_in,
    rows_in,
    grads_in,
    normal_in,
    scale,
    output_in,
    whole_out,
    inner_out,
    grad_attended,
    gated,
    weights,
    grads,
    whole_normal,
    output_rows,
    scatter,
    inner,
    whole,
    loads,
    stores,
    inner_stores,
    *scratch,
):
    count, tokens, width = grads.shape
    out_one, turn = mixings(mix)[2:]
    blocks = scratch[1]
    hidden = gated.shape[2]
    heads = output_rows.shape[1]
    me = lax.axis_index("col")
    edge = size - 1
    order = sorted(range(size), key=lambda shard: -max(shard, edge - shard))
    pairs = [(gated_in.at[:, pl.ds(0, GROUP)], gated.at[:, pl.ds(0, GROUP)])]
    for shard in order:
        shard_rows = pl.ds(shard * width, width)
        pairs.append((rows_in.at[shard_rows, pl.ds(0, 2 * hidden)], weights.at[shard_rows]))
    rest = pl.ds(GROUP, tokens - GROUP)
    pairs = pairs + [
        (gated_in.at[:, rest], gated.at[:, rest]),
        (grads_in, grads),
        (normal_in, whole_normal),
        (output_in.at[:, pl.ds(output_in.shape[1] - heads, heads)], output_rows),
    ]
    waits = start_loads(pairs, loads)
    store, wait_stores = group_store(whole, whole_out, stores)
    store_inner, wait_inner = group_store(inner, inner_out, inner_stores)
    waits[0].wait()

    def produce(rows, shard, first):
        if first:
            waits[1 + order.index(shard)].wait()
        shard_rows = slice(shard * width, (shard + 1) * width)
        total = lax.dot_general(
            gated[0, rows], weights[shard_rows, :hidden], LANES, preferred_element_type=f32
        )
        total = total + lax.dot_general(
            gated[1, rows], weights[shard_rows, hidden:], LANES, preferred_element_type=f32
        )
        scatter[rows, shard_rows] = total.astype(jnp.bfloat16)
        if first and shard == order[-1]:
            for wait in waits[1 + size :]:
                wait.wait()

    def own_normal(rows):
        return whole_normal[rows, pl.ds(pl.multiple_of(me * width, width), width)].astype(f32)

    def prepare(rows, total):
        inner[rows, :] = total
        normal = own_normal(rows)
        part = 1.0 / width
        first = jnp.sum(total, -1, keepdims=True)
        second = jnp.sum(total * normal, -1, keepdims=True)
        plain = jnp.sum(normal, -1, keepdims=True)
        square = jnp.sum(normal * normal, -1, keepdims=True)
        spread = square - plain * plain * part
        cross = second - first * plain * part
        slope = jnp.where(spread > 1e-3, cross / jnp.maximum(spread, 1e-3), 0.0)
        level = (first - slope * plain) * part
        known = out_one[0] * grads[0, rows].astype(f32)
        for k in range(1, count):
            known = known + out_one[k] * grads[k, rows].astype(f32)
        block = known + (turn * scale[rows, :]) * (total - level - slope * normal)
        return (first, second, level, slope), block.astype(jnp.bfloat16)

    def finish(group, rows, turned):
        first, second = whole_sums(size, width, turned)
        rate = scale[rows, :]
        gain = turn * rate
        for z in range(size):
            level = gain * (turned[:, 8 * z + 2 : 8 * z + 3] - first)
            slope = gain * (turned[:, 8 * z + 3 : 8 * z + 4] - second)
            columns = slice(z * width, (z + 1) * width)
            value = blocks[z, rows].astype(f32) + level
            value = value + slope * whole_normal[rows, columns].astype(f32)
            whole[rows, columns] = value.astype(jnp.bfloat16)
        store(group)
        grad_attended[rows, :] = jnp.dot(
            whole[rows, :], output_rows[...], preferred_element_type=f32
        ).astype(jnp.bfloat16)
        inner[rows, :] = rate * (inner[rows, :] - first - second * own_normal(rows))
        store_inner(group)

    line_exchange(size, tokens, width, chunk, hop, scatter, True, produce, prepare, finish, scratch)
    wait_stores()
    wait_inner()


def whole_sums(size, width, turned):
    first = turned[:, 0:1]
    second = turned[:, 1:2]
    for z in range(1, size):
        first = first + turned[:, 8 * z : 8 * z + 1]
        second = second + turned[:, 8 * z + 1 : 8 * z + 2]
    return first * (1.0 / (size * width)), second * (1.0 / (size * width))


def back_mid(
    size, gated, rows, grads, whole_normal, scale, output_rows, mix, chunk=64, hop=(1, 0, 1)
):
    _, tokens, width = grads.shape
    whole = jax.ShapeDtypeStruct((tokens, size * width), jnp.bfloat16)
    inner = jax.ShapeDtypeStruct((tokens, width), f32)
    groups = tokens // GROUP
    weights = jax.ShapeDtypeStruct((size * width, 2 * gated.shape[2]), jnp.bfloat16)
    heads = output_rows.shape[1] // 4
    output_own = jax.ShapeDtypeStruct((size * width, heads), jnp.bfloat16)
    return call(
        functools.partial(back_mid_kernel, size, chunk, hop),
        (mix, gated, rows, grads, whole_normal, scale, output_rows),
        (SM,) + (pl.ANY,) * 4 + (VM, pl.ANY),
        [whole, inner, jax.ShapeDtypeStruct((tokens, heads), jnp.bfloat16)],
        (pl.ANY, pl.ANY, VM),
        held(gated, weights, grads, whole_normal, output_own, whole, inner, whole)
        + [
            pltpu.SemaphoreType.DMA((size + 5,)),
            pltpu.SemaphoreType.DMA((groups,)),
            pltpu.SemaphoreType.DMA((groups,)),
        ]
        + exchange_scratch(size, tokens, width, chunk, True, True),
        "back_mid",
        3,
        10**9,
    )


def tile_sum(product):
    height, width = product.shape
    folded = jnp.sum(product.reshape(height // 8, 8, width), 0)
    total = folded[:, :128]
    for start in range(128, width, 128):
        total = total + folded[:, start : start + 128]
    return total


def back_in_kernel(
    size,
    partial_in,
    first_in,
    last_in,
    normal_in,
    scale,
    streams_in,
    streams_grads,
    other_products,
    inner,
    whole_products,
    share,
    first,
    last,
    normal,
    streams,
    facts,
    products,
    shares,
    loads,
    facts_sent,
    facts_got,
    shares_sent,
    shares_got,
):
    count, tokens, width = streams.shape
    groups = tokens // GROUP
    me = lax.axis_index("col")
    count_rows = lax.axis_size("row")
    own_columns = pl.ds(pl.multiple_of(me * width, width), width)
    waits = start_loads(
        (
            (partial_in.at[:, own_columns], share),
            (first_in, first),
            (last_in, last),
            (normal_in.at[:, own_columns], normal),
            (streams_in, streams),
        ),
        loads,
    )
    barrier = pltpu.get_barrier_semaphore()
    for axis, members in (("col", size), ("row", count_rows)):
        for member in range(members):

            @pl.when(member != lax.axis_index(axis))
            def _():
                pl.semaphore_signal(
                    barrier, inc=1, device_id={axis: member}, device_id_type=MESH
                )

    for wait in waits[:4]:
        wait.wait()

    def rows_of(group):
        return pl.ds(pl.multiple_of(group * GROUP, GROUP), GROUP)

    def sums(group, carry):
        rows = rows_of(group)
        total = share[rows, :].astype(f32) + first[rows, :].astype(f32) + last[rows, :].astype(f32)
        inner[rows, :] = total
        one = jnp.sum(total, -1, keepdims=True)
        two = jnp.sum(total * normal[rows, :].astype(f32), -1, keepdims=True)
        lane = lax.broadcasted_iota(jnp.int32, (GROUP, 128), 1)
        packed = jnp.where(lane == 0, one, jnp.where(lane == 1, two, 0.0))
        facts[me, pl.ds(pl.multiple_of(group * 8, 8), 8)] = packed.T[:8]
        return carry

    lax.fori_loop(0, groups, sums, 0)
    pl.semaphore_wait(barrier, size - 1 + count_rows - 1)

    def fact_copy(place, member):
        return pltpu.make_async_remote_copy(
            src_ref=facts.at[place],
            dst_ref=facts.at[place],
            send_sem=facts_sent.at[member],
            recv_sem=facts_got.at[place],
            device_id={"col": member},
            device_id_type=MESH,
        )

    for member in range(size):

        @pl.when(member != me)
        def _():
            fact_copy(me, member).start()

    products[...] = jnp.zeros_like(products)
    waits[4].wait()
    for member in range(size):

        @pl.when(member != me)
        def _():
            fact_copy(member, member).wait()

    def conclude(group, carry):
        rows = rows_of(group)
        fact_rows = pl.ds(pl.multiple_of(group * 8, 8), 8)
        total = facts[0, fact_rows]
        for place in range(1, size):
            total = total + facts[place, fact_rows]
        total = total * (1.0 / (size * width))
        turned = jnp.concatenate([total, jnp.zeros((GROUP - 8, 128), f32)], 0).T
        own = scale[rows, :] * (
            inner[rows, :] - turned[:, :1] - turned[:, 1:2] * normal[rows, :].astype(f32)
        )
        inner[rows, :] = own
        for i in range(count):
            products[i] = products[i] + tile_sum(streams[i, rows].astype(f32) * own)
        return carry

    lax.fori_loop(0, groups, conclude, 0)
    parts = [streams_grads[...], other_products[...], products[...]]
    total = jnp.concatenate([jnp.sum(jnp.sum(part, 1), -1, keepdims=True) for part in parts], 0)
    total = jnp.concatenate([total, jnp.zeros((128 - total.shape[0], 1), f32)], 0)
    total = jnp.broadcast_to(total, (128, 128)).T[:8]
    for axis, members, base in (("col", size, 0), ("row", count_rows, size)):
        here = lax.axis_index(axis)

        def share_copy(source, member):
            return pltpu.make_async_remote_copy(
                src_ref=shares.at[base + source],
                dst_ref=shares.at[base + source],
                send_sem=shares_sent.at[base + member],
                recv_sem=shares_got.at[base + source],
                device_id={axis: member},
                device_id_type=MESH,
            )

        shares[base + here] = total
        for member in range(members):

            @pl.when(member != here)
            def _():
                share_copy(here, member).start()

        for member in range(members):

            @pl.when(member != here)
            def _():
                share_copy(member, member).wait()

        total = shares[base]
        for member in range(1, members):
            total = total + shares[base + member]
    whole_products[...] = total


def back_in(size, partial, first, last, normal, scale, streams, streams_grads, other_products):
    count, tokens, width = streams.shape
    own = -(-count // 8) * 8
    members = size + lax.axis_size("row")
    dma = pltpu.SemaphoreType.DMA
    return call(
        functools.partial(back_in_kernel, size),
        (partial, first, last, normal, scale, streams, streams_grads, other_products),
        (pl.ANY, pl.ANY, pl.ANY, pl.ANY, VM, pl.ANY, VM, VM),
        [
            jax.ShapeDtypeStruct((tokens, width), f32),
            jax.ShapeDtypeStruct((8, 128), f32),
        ],
        (VM, VM),
        held(first, first, last, first, streams)
        + [
            pltpu.VMEM((size, tokens // GROUP * 8, 128), f32),
            pltpu.VMEM((own, 8, 128), f32),
            pltpu.VMEM((members, 8, 128), f32),
            dma((5,)),
            dma((size,)),
            dma((size,)),
            dma((members,)),
            dma((members,)),
        ],
        "back_in",
        4,
        10**9,
    )


def end_kernel(mix, streams, grads, branch_one, branch_two, inner_two, final, products):
    count, tokens, width = streams.shape
    through, _, out_one, _ = mixings(mix)
    out_two = [mix[1, j, 1 + count] for j in range(count)]

    @pl.when(pl.program_id(0) == 0)
    def _():
        products[...] = jnp.zeros_like(products)

    def slab(index, sums):
        rows = pl.ds(pl.multiple_of(index * 16, 16), 16)
        sums = list(sums)
        for start in range(0, width, 128):
            columns = slice(start, start + 128)
            values = [streams[i, rows, columns].astype(f32) for i in range(count)]
            above = [grads[i, rows, columns].astype(f32) for i in range(count)]
            one = branch_one[rows, columns]
            two = branch_two[rows, columns].astype(f32)
            below = inner_two[rows, columns]
            for j in range(count):
                value = out_one[j] * one + out_two[j] * two
                for k in range(count):
                    value = value + through[k][j] * values[k]
                final[j, rows, columns] = value.astype(jnp.bfloat16)
            pairs = [(a, below) for a in values]
            pairs = pairs + [(one, b) for b in above]
            pairs = pairs + [(a, two) for a in above]
            pairs = pairs + [(one, below)]
            for place, (a, b) in enumerate(pairs):
                product = a * b
                sums[place] = sums[place] + product[:8] + product[8:]
        return tuple(sums)

    used = 3 * count + 1
    sums = lax.fori_loop(0, tokens // 16, slab, (jnp.zeros((8, 128), f32),) * used)
    for place in range(used):
        products[place] = products[place] + sums[place]


def end_streams(mix, streams, grads, branch_one, branch_two, inner_two, tile=256):
    count, tokens, width = streams.shape
    used = -(-(3 * count + 1) // 8) * 8
    many = pl.BlockSpec((count, tile, width), lambda i: (0, i, 0))
    own = pl.BlockSpec((tile, width), lambda i: (i, 0))
    return pl.pallas_call(
        end_kernel,
        grid=(tokens // tile,),
        out_shape=[
            jax.ShapeDtypeStruct(streams.shape, jnp.bfloat16),
            jax.ShapeDtypeStruct((used, 8, 128), f32),
        ],
        in_specs=[pl.BlockSpec(memory_space=SM), many, many, own, own, own],
        out_specs=[many, pl.BlockSpec((used, 8, 128), lambda i: (0, 0, 0))],
        compiler_params=pltpu.CompilerParams(vmem_limit_bytes=60 * 2**20),
        cost_estimate=pl.CostEstimate(
            flops=60 * streams.size, bytes_accessed=9 * streams.size, transcendentals=0
        ),
        name="end_streams",
    )(mix, streams, grads, branch_one, branch_two, inner_two)


def grad_kernel(mix, grads, inner_two, inner_one, out):
    count = grads.shape[0]
    through, in_two, _, _ = mixings(mix)
    above = [grads[k].astype(f32) for k in range(count)]
    below, own = inner_two[...], inner_one[...]
    for i in range(count):
        value = in_two[i] * below + mix[0, i, 0] * own
        for k in range(count):
            value = value + through[i][k] * above[k]
        out[i] = value


def grad_streams_of(mix, grads, inner_two, inner_one, tile=256):
    count, tokens, width = grads.shape
    many = pl.BlockSpec((count, tile, width), lambda i: (0, i, 0))
    own = pl.BlockSpec((tile, width), lambda i: (i, 0))
    return pl.pallas_call(
        grad_kernel,
        grid=(tokens // tile,),
        out_shape=jax.ShapeDtypeStruct(grads.shape, f32),
        in_specs=[pl.BlockSpec(memory_space=SM), many, own, own],
        out_specs=many,
        compiler_params=pltpu.CompilerParams(vmem_limit_bytes=60 * 2**20),
        cost_estimate=pl.CostEstimate(
            flops=10 * grads.size, bytes_accessed=8 * grads.size, transcendentals=0
        ),
        name="grad_streams",
    )(mix, grads, inner_two, inner_one)


def tiled(body, grid, operands, specs, outs, out_specs, scratch, flops, name):
    moved = sum(array.size * array.dtype.itemsize for array in list(operands) + (list(outs) if isinstance(outs, list) else [outs]))
    return pl.pallas_call(
        body,
        grid=grid,
        out_shape=outs,
        in_specs=specs,
        out_specs=out_specs,
        scratch_shapes=scratch,
        compiler_params=pltpu.CompilerParams(vmem_limit_bytes=60 * 2**20),
        cost_estimate=pl.CostEstimate(flops=flops, bytes_accessed=moved, transcendentals=0),
        name=name,
    )(*operands)


def gate_kernel(
    size,
    steps,
    chunks,
    whole,
    gate_rows,
    upper_rows,
    down_rows,
    own_in,
    before_in,
    after_in,
    active_out,
    by_gate,
    by_upper,
    partial,
    gathered,
    active,
    blocks,
    loads,
    stores,
    sent,
    got,
):
    step = pl.program_id(0)
    me = lax.axis_index("col")
    tiles, tile = active.shape[1] // gate_rows.shape[1], gate_rows.shape[1]
    tokens, width = blocks.shape[1:]
    chunk = tokens // chunks
    edge = size - 1
    right, left = jnp.minimum(me + 1, edge), jnp.maximum(me - 1, 0)
    other = jnp.where(me == edge, left, right)

    def load(place, way):
        source = (own_in, before_in, after_in)[way]
        return pltpu.make_async_copy(source, blocks.at[place], loads.at[way])

    def store(place):
        return pltpu.make_async_copy(
            blocks.at[place],
            gathered.at[:, pl.ds(pl.multiple_of(place * width, width), width)],
            stores.at[place],
        )

    def send(place, index, way, device):
        rows = pl.ds(pl.multiple_of(index * chunk, chunk), chunk)
        return pltpu.make_async_remote_copy(
            src_ref=blocks.at[place, rows],
            dst_ref=blocks.at[place, rows],
            send_sem=sent.at[way, place, index],
            recv_sem=got.at[place, index],
            device_id={"col": device},
            device_id_type=MESH,
        )

    def both_ways(near, act):
        for way, place, target, onward in (
            (0, me - near, right, me < edge),
            (1, me + near, left, me > 0),
        ):

            @pl.when((place >= 0) & (place < size))
            def _():
                act(way, place, target, onward)

    @pl.when(step == 0)
    def _():
        load(me, 0).start()
        both_ways(1, lambda way, place, target, onward: load(place, 1 + way).start())
        barrier = pltpu.get_barrier_semaphore()
        both_ways(
            1,
            lambda way, place, target, onward: pl.semaphore_signal(
                barrier, inc=1, device_id={"col": place}, device_id_type=MESH
            ),
        )
        load(me, 0).wait()
        store(me).start()
        both_ways(1, lambda way, place, target, onward: load(place, 1 + way).wait())

        @pl.when((me > 0) & (me < edge))
        def _():
            pl.semaphore_wait(barrier, 2)

        @pl.when((me == 0) | (me == edge))
        def _():
            pl.semaphore_wait(barrier, 1)


        def begin(way, place, target, onward):
            store(place).start()

            @pl.when(onward)
            def _():
                for index in range(chunks):
                    send(place, index, way, target).start()

        both_ways(1, begin)

    for near in range(2, size - 1):
        index = step - (steps - chunks - (size - 2 - near))

        def forward(way, place, target, onward):
            send(place, index, way, other).wait_recv()

            @pl.when(onward)
            def _():
                send(place, index, way, target).start()

        @pl.when((index >= 0) & (index < chunks))
        def _():
            both_ways(near, forward)

    @pl.when(step < tiles)
    def _():
        gate = jnp.dot(whole[...], gate_rows[...], preferred_element_type=f32)
        upper = jnp.dot(whole[...], upper_rows[...], preferred_element_type=f32)
        sigma = jax.nn.sigmoid(gate)
        silu = gate * sigma
        value = (silu * upper).astype(jnp.bfloat16)
        active_out[...] = value
        active[:, pl.ds(pl.multiple_of(step * tile, tile), tile)] = value
        by_gate[...] = (upper * sigma * (1.0 + gate * (1.0 - sigma))).astype(jnp.bfloat16)
        by_upper[...] = silu.astype(jnp.bfloat16)

    @pl.when(step >= tiles)
    def _():
        partial[...] = lax.dot_general(
            active[...], down_rows[...], LANES, preferred_element_type=f32
        ).astype(jnp.bfloat16)

    @pl.when(step == steps - 1)
    def _():
        def last(way, place, target, onward):
            for index in range(chunks):
                send(place, index, way, other).wait_recv()

        both_ways(size - 1, last)
        for near in range(2, size):
            both_ways(near, lambda way, place, target, onward: store(place).start())

        def sends_done(way, place, target, onward):
            @pl.when(onward)
            def _():
                for index in range(chunks):
                    send(place, index, way, other).wait_send()

        for near in range(1, size - 1):
            both_ways(near, sends_done)
        for place in range(size):
            store(place).wait()


def gate_forward(size, whole, weights, own, before, after, tile=256):
    tokens, features = whole.shape
    hidden = weights.shape[1] // 3
    tile = min(tile, hidden)
    tiles = hidden // tile
    down_tile = min(512, features)
    steps = tiles + features // down_tile
    chunks = 1
    while 2 * chunks <= min(8, steps - size + 3):
        chunks = 2 * chunks
    wide = pl.BlockSpec((tokens, tile), lambda j: (0, jnp.minimum(j, tiles - 1)))
    plain = pl.BlockSpec(memory_space=pl.ANY)
    dma = pltpu.SemaphoreType.DMA
    wide_shape = jax.ShapeDtypeStruct((tokens, hidden), jnp.bfloat16)
    return pl.pallas_call(
        functools.partial(gate_kernel, size, steps, chunks),
        grid=(steps,),
        out_shape=[wide_shape] * 3 + [jax.ShapeDtypeStruct((tokens, features), jnp.bfloat16)] * 2,
        in_specs=[
            pl.BlockSpec((tokens, features), lambda j: (0, 0)),
            pl.BlockSpec((features, tile), lambda j: (0, jnp.minimum(j, tiles - 1))),
            pl.BlockSpec((features, tile), lambda j: (0, tiles + jnp.minimum(j, tiles - 1))),
            pl.BlockSpec((down_tile, hidden), lambda j: (jnp.maximum(j - tiles, 0), 2)),
            plain,
            plain,
            plain,
        ],
        out_specs=[wide] * 3
        + [pl.BlockSpec((tokens, down_tile), lambda j: (0, jnp.maximum(j - tiles, 0))), plain],
        scratch_shapes=[
            pltpu.VMEM((tokens, hidden), jnp.bfloat16),
            pltpu.VMEM((size, tokens, own.shape[1]), jnp.bfloat16),
            dma((3,)),
            dma((size,)),
            dma((2, size, chunks)),
            dma((size, chunks)),
        ],
        compiler_params=pltpu.CompilerParams(
            collective_id=5, has_side_effects=True, vmem_limit_bytes=60 * 2**20
        ),
        cost_estimate=pl.CostEstimate(
            flops=6 * tokens * features * hidden,
            bytes_accessed=2 * weights.size,
            transcendentals=0,
        ),
        name="gate_forward",
    )(whole, weights, weights, weights, own, before, after)


def gate_back_kernel(whole, rows, by_gate, by_upper, grads):
    grad = jnp.dot(whole[...], rows[...], preferred_element_type=f32)
    grads[0] = (grad * by_gate[...].astype(f32)).astype(jnp.bfloat16)
    grads[1] = (grad * by_upper[...].astype(f32)).astype(jnp.bfloat16)


def gate_back(whole, weights, by_gate, by_upper, tile=512):
    tokens, features = whole.shape
    hidden = weights.shape[1] // 3
    tile = min(tile, hidden)
    tiles = hidden // tile
    part = pl.BlockSpec((tokens, tile), lambda j: (0, j))
    return tiled(
        gate_back_kernel,
        (tiles,),
        (whole, weights, by_gate, by_upper),
        [
            pl.BlockSpec((tokens, features), lambda j: (0, 0)),
            pl.BlockSpec((features, tile), lambda j: (0, 2 * tiles + j)),
            part,
            part,
        ],
        jax.ShapeDtypeStruct((2, tokens, hidden), jnp.bfloat16),
        pl.BlockSpec((2, tokens, tile), lambda j: (0, 0, j)),
        [],
        2 * tokens * features * hidden,
        "gate_back",
    )


def outer_kernel(cut, left, right, other_left, other_right, out, turned):
    step = pl.program_id(0)

    @pl.when(step == 0)
    def _():
        turned[...] = left[...].T

    @pl.when(step == cut)
    def _():
        turned[...] = other_left[...].T

    @pl.when(step < cut)
    def _():
        out[...] = jnp.dot(turned[...], right[...], preferred_element_type=f32).astype(jnp.bfloat16)

    @pl.when(step >= cut)
    def _():
        out[...] = jnp.dot(turned[...], other_right[...], preferred_element_type=f32).astype(
            jnp.bfloat16
        )


def outer(left, right, other_left, other_right, tile=512, name="outer"):
    tokens, rows = left.shape
    tile = min(tile, other_right.shape[1])
    other = other_right.shape[1] // tile
    if right.ndim == 3:
        tiles = right.shape[2] // tile
        cut = right.shape[0] * tiles
        clip = lambda j: jnp.minimum(j, cut - 1)
        spec = pl.BlockSpec((None, tokens, tile), lambda j: (clip(j) // tiles, 0, clip(j) % tiles))
    else:
        cut = right.shape[1] // tile
        spec = pl.BlockSpec((tokens, tile), lambda j: (0, jnp.minimum(j, cut - 1)))
    whole = pl.BlockSpec((tokens, rows), lambda j: (0, 0))
    return tiled(
        functools.partial(outer_kernel, cut),
        (cut + other,),
        (left, right, other_left, other_right),
        [whole, spec, whole, pl.BlockSpec((tokens, tile), lambda j: (0, jnp.maximum(j - cut, 0)))],
        jax.ShapeDtypeStruct((rows, (cut + other) * tile), jnp.bfloat16),
        pl.BlockSpec((rows, tile), lambda j: (0, j)),
        [pltpu.VMEM((rows, tokens), jnp.bfloat16)],
        2 * tokens * rows * (cut + other) * tile,
        name,
    )


def product_kernel(dims, left, right, out):
    total = lax.dot_general(left[...], right[...], dims, preferred_element_type=f32)
    out[...] = total.astype(out.dtype)


def product(left, right, start, columns, kind=jnp.bfloat16, tile=512, name="product"):
    tokens, depth = left.shape
    tile = min(tile, columns)
    first = start // tile
    return tiled(
        functools.partial(product_kernel, (((1,), (0,)), ((), ()))),
        (columns // tile,),
        (left, right),
        [
            pl.BlockSpec((tokens, depth), lambda j: (0, 0)),
            pl.BlockSpec((depth, tile), lambda j: (0, first + j)),
        ],
        jax.ShapeDtypeStruct((tokens, columns), kind),
        pl.BlockSpec((tokens, tile), lambda j: (0, j)),
        [],
        2 * tokens * depth * columns,
        name,
    )


def heads_kernel(grads, rows, out):
    width = grads.shape[2]
    total = 0.0
    for k in range(grads.shape[0]):
        total = total + lax.dot_general(
            grads[k], rows[:, k * width : (k + 1) * width], LANES, preferred_element_type=f32
        )
    out[...] = total.astype(jnp.bfloat16)


def heads_product(grads, weights, tile=512):
    count, tokens, width = grads.shape
    rows = weights.shape[0]
    tile = min(tile, rows)
    return tiled(
        heads_kernel,
        (rows // tile,),
        (grads, weights),
        [
            pl.BlockSpec((count, tokens, width), lambda j: (0, 0, 0)),
            pl.BlockSpec((tile, count * width), lambda j: (j, 0)),
        ],
        jax.ShapeDtypeStruct((tokens, rows), jnp.bfloat16),
        pl.BlockSpec((tokens, tile), lambda j: (0, j)),
        [],
        2 * count * tokens * width * rows,
        "heads_product",
    )


def fill_bias(bias, column, row):
    tile = min(256, bias.shape[0])
    for start in range(0, bias.shape[0], tile):
        shape = (tile, bias.shape[1])
        index = lax.broadcasted_iota(jnp.int32, shape, 0) + start
        allowed = (column[start : start + tile] == row[...]) & (
            lax.broadcasted_iota(jnp.int32, shape, 1) <= index
        )
        bias[start : start + tile] = jnp.where(allowed, 0.0, MASKED)


def key_span(start, block):
    return max(0, start + 1 - LONGEST) // 128 * 128, start + block


def block_probs(queries, key_heads, bias):
    scores = lax.dot_general(queries, key_heads, LANES, preferred_element_type=f32) + bias
    expo = jnp.exp2(scores - jnp.max(scores, -1, keepdims=True))
    return expo * (1.0 / jnp.sum(expo, -1, keepdims=True))


def attend_forward_kernel(
    block,
    query,
    key,
    value,
    cosine,
    sine,
    column,
    row,
    queries,
    key_heads,
    value_heads,
    attended,
    bias,
):
    length = query.shape[0]

    @pl.when(pl.program_id(0) == 0)
    def _():
        fill_bias(bias, column, row)

    cosines = jnp.concatenate([cosine[...], cosine[...]], 1)
    sines = jnp.concatenate([-sine[...], sine[...]], 1)

    def turn(values):
        return values * cosines + pltpu.roll(values, HEAD_DIM // 2, 1) * sines

    queries[...] = (turn(query[...]) * (HEAD_DIM ** (-0.5) * LOG2E)).astype(jnp.bfloat16)
    key_heads[...] = turn(key[...]).astype(jnp.bfloat16)
    value_heads[...] = value[...].astype(jnp.bfloat16)
    for start in range(0, length, block):
        first, end = key_span(start, block)
        probs = block_probs(
            queries[start:end], key_heads[first:end], bias[start:end, first:end]
        )
        result = jnp.dot(
            probs.astype(jnp.bfloat16), value_heads[first:end], preferred_element_type=f32
        )
        attended[start:end, :] = result.astype(jnp.bfloat16)


def attend_forward(projected, cosine, sine, column, row):
    length, width = projected.shape
    width = width // 3
    heads = width // HEAD_DIM
    block = min(256, length)

    def head(offset):
        return pl.BlockSpec((length, HEAD_DIM), lambda h: (0, h + offset))

    def fixed(array):
        return pl.BlockSpec(array.shape, lambda h: (0, 0))

    return pl.pallas_call(
        functools.partial(attend_forward_kernel, block),
        grid=(heads,),
        out_shape=[jax.ShapeDtypeStruct((length, width), jnp.bfloat16)] * 4,
        in_specs=[head(0), head(heads), head(2 * heads)]
        + [fixed(array) for array in (cosine, sine, column, row)],
        out_specs=[head(0)] * 4,
        scratch_shapes=[pltpu.VMEM((length, length), f32)],
        compiler_params=pltpu.CompilerParams(vmem_limit_bytes=60 * 2**20),
        name="attend_forward",
    )(projected, projected, projected, cosine, sine, column, row)


def attend_back_kernel(
    block,
    queries,
    key_heads,
    value_heads,
    grad_result,
    cosine,
    sine,
    column,
    row,
    grads,
    key_sum,
    value_sum,
    bias,
):
    length = queries.shape[0]

    @pl.when(pl.program_id(0) == 0)
    def _():
        fill_bias(bias, column, row)

    key_sum[...] = jnp.zeros_like(key_sum)
    value_sum[...] = jnp.zeros_like(value_sum)

    def turn_back(values, rows, factor):
        values = values * factor
        cosines = jnp.concatenate([cosine[rows], cosine[rows]], 1)
        sines = jnp.concatenate([-sine[rows], sine[rows]], 1)
        return (values * cosines - pltpu.roll(values, HEAD_DIM // 2, 1) * sines).astype(
            jnp.bfloat16
        )

    for start in range(0, length, block):
        first, end = key_span(start, block)
        query, grad_part = queries[start:end], grad_result[start:end]
        probs = block_probs(query, key_heads[first:end], bias[start:end, first:end])
        grad_probs = lax.dot_general(
            grad_part, value_heads[first:end], LANES, preferred_element_type=f32
        )
        row_sum = jnp.sum(probs * grad_probs, -1, keepdims=True)
        grad_scores = (probs * (grad_probs - row_sum)).astype(jnp.bfloat16)
        grad_part_query = jnp.dot(grad_scores, key_heads[first:end], preferred_element_type=f32)
        grads[0, start:end] = turn_back(
            grad_part_query, pl.ds(start, block), HEAD_DIM ** (-0.5)
        )
        key_sum[first:end, :] += lax.dot_general(
            grad_scores, query, ROWS, preferred_element_type=f32
        )
        value_sum[first:end, :] += lax.dot_general(
            probs.astype(jnp.bfloat16), grad_part, ROWS, preferred_element_type=f32
        )
    grads[1] = turn_back(key_sum[...], pl.ds(0, length), 1.0 / LOG2E)
    grads[2] = value_sum[...].astype(jnp.bfloat16)


def attend_back(queries, key_heads, value_heads, grad_result, cosine, sine, column, row):
    length, width = queries.shape
    heads = width // HEAD_DIM
    block = min(256, length)
    head = pl.BlockSpec((length, HEAD_DIM), lambda h: (0, h))

    def fixed(array):
        return pl.BlockSpec(array.shape, lambda h: (0, 0))

    return pl.pallas_call(
        functools.partial(attend_back_kernel, block),
        grid=(heads,),
        out_shape=jax.ShapeDtypeStruct((3, length, width), jnp.bfloat16),
        in_specs=[head] * 4 + [fixed(array) for array in (cosine, sine, column, row)],
        out_specs=pl.BlockSpec((3, length, HEAD_DIM), lambda h: (0, 0, h)),
        scratch_shapes=[pltpu.VMEM((length, HEAD_DIM), f32)] * 2
        + [pltpu.VMEM((length, length), f32)],
        compiler_params=pltpu.CompilerParams(vmem_limit_bytes=60 * 2**20),
        name="attend_back",
    )(queries, key_heads, value_heads, grad_result, cosine, sine, column, row)


def update(weight, grad, moment, average, rate):
    step_grad = grad + DECAY * weight
    moment_new = MOMENTUM * moment + step_grad
    weight_new = weight - rate * (step_grad + MOMENTUM * moment_new)
    return (weight_new, moment_new, average + (weight_new - average) / (STEP + 1))


def update_kernel(rate, turned, weight, grad, moment, average, *outs):
    value = grad[...].astype(f32)
    results = update(weight[...], value.T if turned else value, moment[...], average[...], rate)
    for out, result in zip(outs, results):
        out[...] = result


def update_blocks(weight, grad, moment, average, rate, start):
    turned = weight.ndim == 2
    rows = grad.shape[0]
    columns = weight.shape[0] if turned else weight.shape[2]
    tile = min(columns, 512)
    tiles = columns // tile
    first = start // tile
    if turned:
        grid = (tiles,)
        own = pl.BlockSpec((tile, rows), lambda j: (j, 0))
        place = pl.BlockSpec((rows, tile), lambda j: (0, first + j))
    else:
        grid = (weight.shape[0], tiles)
        own = pl.BlockSpec((None, rows, tile), lambda k, j: (k, 0, j))
        place = pl.BlockSpec((rows, tile), lambda k, j: (0, first + k * tiles + j))
    return pl.pallas_call(
        functools.partial(update_kernel, rate, turned),
        grid=grid,
        out_shape=[jax.ShapeDtypeStruct(weight.shape, f32)] * 3,
        in_specs=[own, place, own, own],
        out_specs=[own] * 3,
        compiler_params=pltpu.CompilerParams(vmem_limit_bytes=60 * 2**20),
        cost_estimate=pl.CostEstimate(
            flops=10 * weight.size, bytes_accessed=26 * weight.size, transcendentals=0
        ),
        name="update",
    )(weight, grad, moment, average)


def tie(*values):
    return lax.optimization_barrier(values)


def line_ways():
    size = lax.axis_size("col")
    up = [(i, i + 1) for i in range(size - 1)]
    down = [(i + 1, i) for i in range(size - 1)]
    return size, up, down


def scatter_steps(partial):
    size, up, down = line_ways()
    me = lax.axis_index("col")
    width = partial.shape[1] // size

    def share(place):
        return lax.dynamic_slice_in_dim(partial, place * width, width, 1)

    first = share(jnp.minimum(me + size - 1, size - 1))
    last = share(jnp.maximum(me - size + 1, 0))
    for step in range(1, size):
        if step > 1:
            first = share(jnp.minimum(me + size - step, size - 1)).astype(f32) + first.astype(f32)
            last = share(jnp.maximum(me - size + step, 0)).astype(f32) + last.astype(f32)
            first = first.astype(jnp.bfloat16)
            last = last.astype(jnp.bfloat16)
        first, last = yield (lax.ppermute(first, "col", up), lax.ppermute(last, "col", down))
    yield [first, last]


def advance(steps, got, *values):
    moved = next(steps) if got is None else steps.send(got)
    tied = tie(*moved, *values)
    return tied[: len(moved)], tied[len(moved) :]


def finish_line(steps, got):
    moved = steps.send(got)
    while isinstance(moved, tuple):
        moved = steps.send(moved)
    return moved


def small_matmul(left, right):
    return jnp.sum(left[:, :, None] * right[None, :, :], 1)


def scatter_rows(grad):
    return lax.psum_scatter(grad, "row", scatter_dimension=0, tiled=True)


def side_by_side(weights, turned):
    return jnp.concatenate([weights[k] for k in range(weights.shape[0])] + [turned.T], 1)


def per_device(
    streams,
    segments,
    attention_in,
    attention_out,
    gate_up,
    down_weights,
    hyper_mix,
    moment_attention_in,
    moment_attention_out,
    moment_gate_up,
    moment_down_weights,
    moment_hyper_mix,
    average_attention_in,
    average_attention_out,
    average_gate_up,
    average_down_weights,
    average_hyper_mix,
    cotangent,
):
    size = lax.axis_size("col")
    low = jnp.bfloat16
    count, length, width = streams.shape
    cosine, sine = rope_tables(segments)

    def gather_rows(weights):
        return lax.all_gather(weights.astype(low), "row", axis=0, tiled=True)

    attention_weights = gather_rows(side_by_side(attention_in, attention_out))

    one, two = hyper_mix[0], hyper_mix[1]
    across_one, across_two = one[:, 1 : 1 + count], two[:, 1 : 1 + count]
    whole_one, scale_one, grad_two, streams_grads, hidden_weights = norm_in(
        size, streams, cotangent, gate_up, down_weights, hyper_mix
    )
    hidden_weights = lax.all_gather(hidden_weights, "row", axis=0, tiled=True)
    heads = attention_in.shape[2]
    _, up, down = line_ways()
    before = lax.ppermute(grad_two, "col", up)
    after = lax.ppermute(grad_two, "col", down)
    projected = product(whole_one, attention_weights, 0, 3 * heads, f32, heads, "project_in")
    queries, key_heads, value_heads, attended = attend_forward(
        projected, cosine, sine, segments.T, segments
    )
    attended, before, after = tie(attended, before, after)
    whole_two, scale_two, branch_one = norm_mid(
        size, attended, attention_weights, streams, hyper_mix
    )

    active, by_gate, by_upper, partial_two, whole_grad_two = gate_forward(
        size, whole_two, hidden_weights, grad_two, before, after
    )
    branch_two = lax.psum_scatter(partial_two, "col", scatter_dimension=1, tiled=True)
    grad_gated = gate_back(whole_grad_two, hidden_weights, by_gate, by_upper)
    grad_hidden = outer(whole_two, grad_gated, whole_grad_two, active, name="outer_hidden")
    grad_hidden, grad_gated = tie(grad_hidden, grad_gated)
    grad_hidden = scatter_rows(grad_hidden)
    whole_grad_one, inner_two, grad_attended = back_mid(
        size,
        grad_gated,
        hidden_weights,
        cotangent,
        whole_two,
        scale_two,
        attention_weights,
        hyper_mix,
    )

    grad_attended, branch_two = tie(grad_attended, branch_two)
    grad_heads = attend_back(
        queries, key_heads, value_heads, grad_attended, cosine, sine, segments.T, segments
    )
    tokens_all = length * lax.axis_size("row")
    token_scale = tokens_all ** (-0.5)
    model_rate = D ** (-0.5) * token_scale
    partial_one = heads_product(grad_heads, attention_weights)
    steps = scatter_steps(partial_one)
    grad_attention = outer(
        whole_one, grad_heads, whole_grad_one, attended, name="outer_attention"
    )
    got, (grad_attention,) = advance(steps, None, grad_attention)
    grad_attention, grad_hidden = tie(grad_attention, grad_hidden)
    grad_attention = scatter_rows(grad_attention)
    third = update_blocks(gate_up, grad_hidden, moment_gate_up, average_gate_up, model_rate, 0)
    fourth = update_blocks(
        down_weights,
        grad_hidden,
        moment_down_weights,
        average_down_weights,
        FF ** (-0.5) * token_scale,
        gate_up.shape[0] * gate_up.shape[2],
    )
    got, hidden = advance(steps, got, *third, *fourth)
    third, fourth = hidden[:3], hidden[3:]
    final, other_products = end_streams(
        hyper_mix,
        streams,
        cotangent,
        branch_one,
        branch_two,
        inner_two,
    )
    got, (other_products,) = advance(steps, got, other_products)
    first_part, last_part = finish_line(steps, got)
    inner_one, products = back_in(
        size,
        partial_one,
        first_part,
        last_part,
        whole_one,
        scale_one,
        streams,
        streams_grads,
        other_products,
    )
    grad_streams = grad_streams_of(hyper_mix, cotangent, inner_two, inner_one)

    products = products[0]
    streams_one = products[count * count + other_products.shape[0] :][:count]
    cuts = [count * count, count, count, count, 1]
    parts = []
    start = 0
    for cut in cuts:
        parts.append(products[start : start + cut])
        start = start + cut
    streams_grads, streams_two, branch_grads, grads_branch, branch_inner = parts
    streams_grads = streams_grads.reshape(count, count)
    hyper_one = jnp.concatenate(
        [
            streams_one[:, None],
            small_matmul(streams_grads, across_two.T) + streams_two[:, None] * two[None, :, 0],
            small_matmul(across_two, branch_grads[:, None]) + (two[:, 0] * branch_inner)[:, None],
        ],
        1,
    )
    hyper_two = jnp.concatenate(
        [
            small_matmul(across_one.T, streams_two[:, None])
            + (one[:, 1 + count] * branch_inner)[:, None],
            small_matmul(across_one.T, streams_grads)
            + one[:, 1 + count][:, None] * branch_grads[None, :],
            grads_branch[:, None],
        ],
        1,
    )
    grad_hyper = jnp.stack([hyper_one, hyper_two])
    first = update_blocks(
        attention_in, grad_attention, moment_attention_in, average_attention_in, model_rate, 0
    )
    second = update_blocks(
        attention_out,
        grad_attention,
        moment_attention_out,
        average_attention_out,
        model_rate,
        attention_in.shape[0] * heads,
    )
    fifth = update(
        hyper_mix,
        grad_hyper,
        moment_hyper_mix,
        average_hyper_mix,
        0.05 * (tokens_all * D) ** (-0.5),
    )
    return (
        final,
        grad_streams,
        first[0],
        first[1],
        first[2],
        second[0],
        second[1],
        second[2],
        third[0],
        third[1],
        third[2],
        fourth[0],
        fourth[1],
        fourth[2],
        fifth[0],
        fifth[1],
        fifth[2],
    )


def solution(mesh):
    in_specs = (
        P(None, "row", "col"),
        P("row", None),
        P(None, "row", "col"),
        P("col", "row"),
        P(None, "row", "col"),
        P("col", "row"),
        P(),
        P(None, "row", "col"),
        P("col", "row"),
        P(None, "row", "col"),
        P("col", "row"),
        P(),
        P(None, "row", "col"),
        P("col", "row"),
        P(None, "row", "col"),
        P("col", "row"),
        P(),
        P(None, "row", "col"),
    )
    out_specs = (
        P(None, "row", "col"),
        P(None, "row", "col"),
        P(None, "row", "col"),
        P(None, "row", "col"),
        P(None, "row", "col"),
        P("col", "row"),
        P("col", "row"),
        P("col", "row"),
        P(None, "row", "col"),
        P(None, "row", "col"),
        P(None, "row", "col"),
        P("col", "row"),
        P("col", "row"),
        P("col", "row"),
        P(),
        P(),
        P(),
    )
    return jax.shard_map(
        per_device, mesh=mesh, in_specs=in_specs, out_specs=out_specs, check_vma=False
    )
```

```python
import functools

import jax
import jax.numpy as jnp
from jax import lax
from jax.experimental import pallas as pl
from jax.experimental.pallas import tpu as pltpu
from jax.sharding import PartitionSpec as P

D = 2048
HEAD_DIM = 128
FF = 8192
STEP = 8


EPSILON = 1e-05
MASKED = -1e30
MOMENTUM = 0.9
DECAY = 0.01
GROUP = 128
MESH = pl.DeviceIdType.MESH
VM, SM = pltpu.VMEM, pltpu.SMEM
f32 = jnp.float32
LONGEST = 512
LOG2E = 1.4426950408889634
LANES = (((1,), (1,)), ((), ()))
ROWS = (((0,), (0,)), ((), ()))


def line_exchange(
    size, tokens, width, chunk, hop, scatter, gather, produce, prepare, finish, scratch, during=None, rows_too=0
):
    recv, blocks, facts, own_facts, sums_sent, sums_got, blocks_sent, blocks_got, facts_sent, facts_got = scratch
    me = lax.axis_index("col")
    chunks = tokens // chunk
    per_group = GROUP // chunk
    groups = tokens // GROUP
    edge = size - 1

    hop, wait_hop, pass_hop = hop

    def far(place):
        lag = jnp.maximum(place, edge - place) * hop + wait_hop
        return lag if scatter is not None else place * 0

    def remote(source, target, sent, got, device):
        return pltpu.make_async_remote_copy(
            src_ref=source,
            dst_ref=target,
            send_sem=sent,
            recv_sem=got,
            device_id={"col": device},
            device_id_type=MESH,
        )

    def rows(index):
        return pl.ds(pl.multiple_of(index * chunk, chunk), chunk)

    def group_rows(group):
        return pl.ds(pl.multiple_of(group * GROUP, GROUP), GROUP)

    def sum_copy(shard, slot, index, device):
        return remote(
            scatter.at[rows(index), pl.ds(shard * width, width)],
            recv.at[slot, rows(index)],
            sums_sent.at[shard, index],
            sums_got.at[slot, index],
            device,
        )

    def block_copy(place, index, way, device):
        return remote(
            blocks.at[place, rows(index)],
            blocks.at[place, rows(index)],
            blocks_sent.at[way, place, index],
            blocks_got.at[place, index],
            device,
        )

    def fact_copy(place, group, device):
        return remote(
            facts.at[group, pl.ds(pl.multiple_of(place * 8, 8), 8)],
            facts.at[group, pl.ds(pl.multiple_of(place * 8, 8), 8)],
            facts_sent.at[device, group],
            facts_got.at[place, group],
            device,
        )

    right = jnp.minimum(me + 1, edge)
    left = jnp.maximum(me - 1, 0)
    other = jnp.where(me == edge, left, right)

    def inside(index):
        return (index >= 0) & (index < chunks)

    def relay_sum(shard, slot, index, fresh, target):
        columns = slice(shard * width, (shard + 1) * width)

        @pl.when(jnp.logical_not(fresh))
        def _():
            sum_copy(shard, shard, index, other).wait_recv()
            total = scatter[rows(index), columns].astype(f32) + recv[shard, rows(index)].astype(f32)
            scatter[rows(index), columns] = total.astype(jnp.bfloat16)

        sum_copy(shard, slot, index, target).start()

    def relay_sums(step):
        index = step - me * hop

        @pl.when(inside(index))
        def _():
            for shard in range(size - 1, 0, -1):

                @pl.when(shard > me)
                def _():
                    slot = jnp.where(me + 1 == shard, size, shard)
                    relay_sum(shard, slot, index, me == 0, right)

        back = step - (edge - me) * hop

        @pl.when(inside(back))
        def _():
            for shard in range(size - 1):

                @pl.when(shard < me)
                def _():
                    relay_sum(shard, shard, back, me == edge, left)

    def ready(step):
        index = step - far(me)

        @pl.when(inside(index))
        def _():
            if scatter is not None:

                @pl.when(me > 0)
                def _():
                    sum_copy(0, size, index, other).wait_recv()

                @pl.when(me < edge)
                def _():
                    sum_copy(0, me, index, other).wait_recv()

                start = pl.multiple_of(me * width, width)
                total = scatter[rows(index), pl.ds(start, width)].astype(f32)
                total = total + jnp.where(me > 0, recv[size, rows(index)].astype(f32), 0.0)
                total = total + jnp.where(me < edge, recv[me, rows(index)].astype(f32), 0.0)
            else:
                total = None
            columns, block = prepare(rows(index), total)
            lane = lax.broadcasted_iota(jnp.int32, (chunk, 128), 1)
            packed = jnp.zeros((chunk, 128), f32)
            for place, column in enumerate(columns):
                packed = jnp.where(lane == place, column, packed)
            within = lax.rem(index, per_group)
            own_facts[pl.ds(pl.multiple_of(within * chunk, chunk), chunk), :] = packed
            if gather:
                blocks[me, rows(index)] = block

                @pl.when(me < edge)
                def _():
                    block_copy(me, index, 0, right).start()

                @pl.when(me > 0)
                def _():
                    block_copy(me, index, 1, left).start()

            @pl.when(within == per_group - 1)
            def _():
                group = index // per_group
                turned = own_facts[...].T
                facts[group, pl.ds(pl.multiple_of(me * 8, 8), 8), :] = turned[:8]
                for place in range(size):

                    @pl.when(place != me)
                    def _():
                        fact_copy(me, group, place).start()

    def relay_blocks(step):
        for near in range(1, size):
            for way, place in ((0, me - near), (1, me + near)):
                index = step - far(place) - near * pass_hop

                @pl.when((place >= 0) & (place < size) & inside(index))
                def _():
                    block_copy(place, index, way, other).wait_recv()
                    onward = (me < edge) if way == 0 else (me > 0)

                    @pl.when(onward)
                    def _():
                        block_copy(place, index, way, right if way == 0 else left).start()

    longest = (edge * hop + wait_hop if scatter is not None else 0) + edge * pass_hop

    def conclude(step):
        index = step - longest

        @pl.when(inside(index) & (lax.rem(index, per_group) == per_group - 1))
        def _():
            group = index // per_group
            for place in range(size):

                @pl.when(place != me)
                def _():
                    fact_copy(place, group, other).wait_recv()

            finish(group, group_rows(group), facts[group].T)

    barrier = pltpu.get_barrier_semaphore()
    for place in range(size):

        @pl.when(place != me)
        def _():
            pl.semaphore_signal(barrier, inc=1, device_id={"col": place}, device_id_type=MESH)

    line = lax.axis_index("row")
    for place in range(rows_too):

        @pl.when(place != line)
        def _():
            pl.semaphore_signal(barrier, inc=1, device_id={"row": place}, device_id_type=MESH)

    if scatter is not None:
        order = sorted(range(size), key=lambda shard: -max(shard, edge - shard))
        for shard in order:
            produce(group_rows(0), shard, True)
    pl.semaphore_wait(barrier, size - 1 + max(rows_too - 1, 0))

    def step_all(step, carry):
        if scatter is not None:
            relay_sums(step)
        ready(step)
        if gather:
            relay_blocks(step)
        conclude(step)
        if scatter is not None:
            following = step // per_group + 1
            for part in range(per_group):

                @pl.when((following < groups) & (lax.rem(step, per_group) == part))
                def _():
                    for shard in range(part * size // per_group, (part + 1) * size // per_group):
                        produce(group_rows(following), shard, False)

        if during is not None:

            @pl.when(inside(step))
            def _():
                during(rows(step))

        return carry

    lax.fori_loop(0, chunks + longest, step_all, 0)

    def drain(index, carry):
        if scatter is not None:
            for shard in range(size):

                @pl.when(shard != me)
                def _():
                    sum_copy(shard, shard, index, other).wait_send()

        if gather:
            for place in range(size):

                @pl.when((place <= me) & (me < edge))
                def _():
                    block_copy(place, index, 0, other).wait_send()

                @pl.when((place >= me) & (me > 0))
                def _():
                    block_copy(place, index, 1, other).wait_send()

        return carry

    lax.fori_loop(0, chunks, drain, 0)

    def drain_facts(group, carry):
        for place in range(size):

            @pl.when(place != me)
            def _():
                fact_copy(me, group, place).wait_send()

        return carry

    lax.fori_loop(0, groups, drain_facts, 0)


def exchange_scratch(size, tokens, width, chunk, scatter, gather):
    chunks = tokens // chunk
    groups = tokens // GROUP
    dma = pltpu.SemaphoreType.DMA
    tiny = (1, chunk, 128)
    return [
        pltpu.VMEM((size + 1, tokens, width) if scatter else tiny, jnp.bfloat16),
        pltpu.VMEM((size, tokens, width) if gather else tiny, jnp.bfloat16),
        pltpu.VMEM((groups, 128, 128), f32),
        pltpu.VMEM((GROUP, 128), f32),
        dma((size, chunks) if scatter else (1, 1)),
        dma((size + 1, chunks) if scatter else (1, 1)),
        dma((2, size, chunks) if gather else (1, 1, 1)),
        dma((size, chunks) if gather else (1, 1)),
        dma((size, groups)),
        dma((size, groups)),
    ]


def call(body, operands, places, outs, out_places, scratch, name, ident, cost=10**11):
    moved = sum(array.size * array.dtype.itemsize for array in list(operands) + outs)
    return pl.pallas_call(
        body,
        out_shape=outs,
        in_specs=[pl.BlockSpec(memory_space=place) for place in places],
        out_specs=[pl.BlockSpec(memory_space=place) for place in out_places],
        scratch_shapes=scratch,
        compiler_params=pltpu.CompilerParams(
            collective_id=ident, has_side_effects=True, vmem_limit_bytes=60 * 2**20
        ),
        cost_estimate=pl.CostEstimate(flops=cost, bytes_accessed=moved, transcendentals=0),
        name=name,
    )(*operands)


def held(*arrays):
    return [pltpu.VMEM(array.shape, array.dtype) for array in arrays]


def start_loads(pairs, sems):
    copies = [
        pltpu.make_async_copy(source, target, sems.at[place])
        for place, (source, target) in enumerate(pairs)
    ]
    for copy in copies:
        copy.start()
    return copies


def group_store(source, target, sems):
    groups = source.shape[0] // GROUP

    def copy(group):
        rows = pl.ds(pl.multiple_of(group * GROUP, GROUP), GROUP)
        return pltpu.make_async_copy(source.at[rows], target.at[rows], sems.at[group])

    def wait_all():
        def one(group, carry):
            copy(group).wait()
            return carry

        lax.fori_loop(0, groups, one, 0)

    return lambda group: copy(group).start(), wait_all


def norm_stats(value):
    mean = jnp.sum(value, -1, keepdims=True) * (1.0 / value.shape[-1])
    center = value - mean
    return mean, center, jnp.sum(center * center, -1, keepdims=True)


def norm_whole(size, width, turned):
    means = [turned[:, 8 * z : 8 * z + 1] for z in range(size)]
    squares = [turned[:, 8 * z + 1 : 8 * z + 2] for z in range(size)]
    mean = sum(means[1:], means[0]) * (1.0 / size)
    shifts = [own - mean for own in means]
    spread = sum(squares[1:], squares[0])
    for shift in shifts:
        spread = spread + width * shift * shift
    return shifts, lax.rsqrt(spread * (1.0 / (size * width)) + EPSILON)


def norm_finish(size, width, blocks, scale, whole, store):
    def finish(group, rows, turned):
        shifts, rate = norm_whole(size, width, turned)
        scale[rows, :] = rate
        for z in range(size):
            value = (blocks[z, rows].astype(f32) + shifts[z]) * rate
            whole[rows, z * width : (z + 1) * width] = value.astype(jnp.bfloat16)
        store(group)

    return finish


def mixings(mix):
    count = mix.shape[1]
    span = range(count)

    def dot(left, right):
        total = left[0] * right[0]
        for a, b in zip(left[1:], right[1:]):
            total = total + a * b
        return total

    across_one = [[mix[0, k, 1 + i] for i in span] for k in span]
    across_two = [[mix[1, i, 1 + j] for i in span] for j in span]
    through = [[dot(across_one[k], across_two[j]) for j in span] for k in span]
    second = [mix[1, i, 0] for i in span]
    outward = [mix[0, i, 1 + count] for i in span]
    in_two = [dot(across_one[k], second) for k in span]
    out_one = [dot(outward, across_two[j]) for j in span]
    return through, in_two, out_one, dot(outward, second)


def norm_in_kernel(
    size,
    chunk,
    hop,
    mix,
    streams,
    grads_in,
    gate_in,
    down_in,
    documents,
    rates,
    whole_out,
    scale,
    branch_grad,
    products,
    packed,
    column,
    cosine,
    sine,
    whole,
    grads,
    gate_up,
    down,
    loads,
    stores,
    *scratch,
):
    count, tokens, width = streams.shape
    kinds, _, hidden = gate_up.shape
    tile = min(512, hidden)
    tiles = hidden // tile
    into = [mix[0, k, 0] for k in range(count)]
    onto = [mix[1, k, 1 + count] for k in range(count)]
    products[...] = jnp.zeros_like(products)
    waits = start_loads(((grads_in, grads), (gate_in, gate_up), (down_in, down)), loads)
    store, wait_stores = group_store(whole, whole_out, stores)

    def prepare(rows, total):
        mixed = into[0] * streams[0, rows].astype(f32)
        for k in range(1, count):
            mixed = mixed + into[k] * streams[k, rows].astype(f32)
        mean, center, square = norm_stats(mixed)
        return (mean, square), center.astype(jnp.bfloat16)

    def during(rows):
        @pl.when(rows.start == 0)
        def _():
            for wait in waits:
                wait.wait()

        own_docs = documents[:, pl.ds(pl.multiple_of(rows.start // GROUP * GROUP, GROUP), GROUP)]
        turned = jnp.broadcast_to(own_docs.astype(f32), (GROUP, GROUP)).T

        @pl.when(lax.rem(rows.start, GROUP) == 0)
        def _():
            group = pl.ds(pl.multiple_of(rows.start, GROUP), GROUP)
            docs = turned[:, :1]
            shape = (GROUP, tokens)
            index = lax.broadcasted_iota(jnp.int32, shape, 0) + rows.start
            before = lax.broadcasted_iota(jnp.int32, shape, 1) < index
            same = (docs == documents[...].astype(f32)) & before
            place = jnp.sum(jnp.where(same, 1.0, 0.0), -1, keepdims=True)
            angle = place * rates[...]
            column[group, :] = docs
            cosine[group, :] = jnp.cos(angle)
            sine[group, :] = jnp.sin(angle)

        for piece in range((kinds + 1) * tiles):

            @pl.when(rows.start == piece * chunk)
            def _():
                kind, start = piece // tiles, piece % tiles * tile
                if kind < kinds:
                    value = gate_up[kind, :, start : start + tile]
                else:
                    value = down[start : start + tile, :].T
                packed[:, piece * tile : (piece + 1) * tile] = value.astype(jnp.bfloat16)

        above = [grads[k, rows].astype(f32) for k in range(count)]
        value = onto[0] * above[0]
        for k in range(1, count):
            value = value + onto[k] * above[k]
        branch_grad[rows, :] = value.astype(jnp.bfloat16)
        for i in range(count):
            own = streams[i, rows].astype(f32)
            for k in range(count):
                place = i * count + k
                products[place] = products[place] + tile_sum(own * above[k])

    finish = norm_finish(size, width, scratch[1], scale, whole, store)
    line_exchange(
        size, tokens, width, chunk, hop, None, True, None, prepare, finish, scratch, during
    )
    wait_stores()


def norm_in(size, streams, grads, gate_up, down, documents, mix, chunk=64, hop=(1, 0, 1)):
    _, tokens, width = streams.shape
    whole = jax.ShapeDtypeStruct((tokens, size * width), jnp.bfloat16)
    half = HEAD_DIM // 2
    rates = 10000.0 ** (-2.0 * jnp.arange(half).astype(f32) / HEAD_DIM)
    return call(
        functools.partial(norm_in_kernel, size, chunk, hop),
        (mix, streams, grads, gate_up, down, documents, rates[None]),
        (SM, VM, pl.ANY, pl.ANY, pl.ANY, VM, VM),
        [
            whole,
            jax.ShapeDtypeStruct((tokens, 1), f32),
            jax.ShapeDtypeStruct((tokens, width), jnp.bfloat16),
            jax.ShapeDtypeStruct((streams.shape[0] * grads.shape[0], 8, 128), f32),
            jax.ShapeDtypeStruct(
                (gate_up.shape[1], (gate_up.shape[0] + 1) * gate_up.shape[2]), jnp.bfloat16
            ),
            jax.ShapeDtypeStruct((tokens, 1), f32),
            jax.ShapeDtypeStruct((tokens, half), f32),
            jax.ShapeDtypeStruct((tokens, half), f32),
        ],
        (pl.ANY,) + (VM,) * 7,
        held(whole, grads, gate_up, down)
        + [pltpu.SemaphoreType.DMA((3,)), pltpu.SemaphoreType.DMA((tokens // GROUP,))]
        + exchange_scratch(size, tokens, width, chunk, False, True),
        "norm_in",
        1,
    )


def norm_mid_kernel(
    size,
    chunk,
    hop,
    mix,
    attended_in,
    rows_in,
    streams_in,
    whole_out,
    scale,
    branch,
    attended,
    weights,
    streams,
    scatter,
    whole,
    loads,
    stores,
    *scratch,
):
    count, tokens, width = streams.shape
    in_two, turn = mixings(mix)[1::2]
    heads = attended.shape[1]
    own_columns = rows_in.at[:, pl.ds(rows_in.shape[1] - heads, heads)]
    waits = start_loads(
        ((attended_in, attended), (own_columns, weights), (streams_in, streams)), loads
    )
    store, wait_stores = group_store(whole, whole_out, stores)
    waits[0].wait()
    waits[1].wait()

    def produce(rows, shard, first):
        columns = slice(shard * width, (shard + 1) * width)
        scatter[rows, columns] = lax.dot_general(
            attended[rows, :], weights[columns, :], LANES, preferred_element_type=f32
        ).astype(jnp.bfloat16)
        if first and shard == size // 2:
            waits[2].wait()

    def prepare(rows, total):
        branch[rows, :] = total
        mixed = turn * total
        for k in range(count):
            mixed = mixed + in_two[k] * streams[k, rows].astype(f32)
        mean, center, square = norm_stats(mixed)
        return (mean, square), center.astype(jnp.bfloat16)

    finish = norm_finish(size, width, scratch[1], scale, whole, store)
    line_exchange(size, tokens, width, chunk, hop, scatter, True, produce, prepare, finish, scratch)
    wait_stores()


def norm_mid(size, attended, rows, streams, mix, chunk=64, hop=(1, 0, 1)):
    _, tokens, width = streams.shape
    weights = jax.ShapeDtypeStruct((size * width, attended.shape[1]), jnp.bfloat16)
    whole = jax.ShapeDtypeStruct((tokens, size * width), jnp.bfloat16)
    return call(
        functools.partial(norm_mid_kernel, size, chunk, hop),
        (mix, attended, rows, streams),
        (SM, pl.ANY, pl.ANY, pl.ANY),
        [
            whole,
            jax.ShapeDtypeStruct((tokens, 1), f32),
            jax.ShapeDtypeStruct((tokens, width), f32),
        ],
        (pl.ANY, VM, VM),
        held(attended, weights, streams, whole, whole)
        + [pltpu.SemaphoreType.DMA((3,)), pltpu.SemaphoreType.DMA((tokens // GROUP,))]
        + exchange_scratch(size, tokens, width, chunk, True, True),
        "norm_mid",
        2,
    )


def back_mid_kernel(
    size,
    chunk,
    hop,
    mix,
    gated_in,
    rows_in,
    grads_in,
    normal_in,
    scale,
    output_in,
    whole_out,
    inner_out,
    grad_attended,
    gated,
    weights,
    grads,
    whole_normal,
    output_rows,
    scatter,
    inner,
    whole,
    loads,
    stores,
    inner_stores,
    *scratch,
):
    count, tokens, width = grads.shape
    out_one, turn = mixings(mix)[2:]
    blocks = scratch[1]
    hidden = gated.shape[2]
    heads = output_rows.shape[1]
    me = lax.axis_index("col")
    edge = size - 1
    order = sorted(range(size), key=lambda shard: -max(shard, edge - shard))
    pairs = [(gated_in.at[:, pl.ds(0, GROUP)], gated.at[:, pl.ds(0, GROUP)])]
    for shard in order:
        shard_rows = pl.ds(shard * width, width)
        pairs.append((rows_in.at[shard_rows, pl.ds(0, 2 * hidden)], weights.at[shard_rows]))
    rest = pl.ds(GROUP, tokens - GROUP)
    pairs = pairs + [
        (gated_in.at[:, rest], gated.at[:, rest]),
        (grads_in, grads),
        (normal_in, whole_normal),
        (output_in.at[:, pl.ds(output_in.shape[1] - heads, heads)], output_rows),
    ]
    waits = start_loads(pairs, loads)
    store, wait_stores = group_store(whole, whole_out, stores)
    store_inner, wait_inner = group_store(inner, inner_out, inner_stores)
    waits[0].wait()

    def produce(rows, shard, first):
        if first:
            waits[1 + order.index(shard)].wait()
        shard_rows = slice(shard * width, (shard + 1) * width)
        total = lax.dot_general(
            gated[0, rows], weights[shard_rows, :hidden], LANES, preferred_element_type=f32
        )
        total = total + lax.dot_general(
            gated[1, rows], weights[shard_rows, hidden:], LANES, preferred_element_type=f32
        )
        scatter[rows, shard_rows] = total.astype(jnp.bfloat16)
        if first and shard == order[-1]:
            for wait in waits[1 + size :]:
                wait.wait()

    def own_normal(rows):
        return whole_normal[rows, pl.ds(pl.multiple_of(me * width, width), width)].astype(f32)

    def prepare(rows, total):
        inner[rows, :] = total
        normal = own_normal(rows)
        part = 1.0 / width
        first = jnp.sum(total, -1, keepdims=True)
        second = jnp.sum(total * normal, -1, keepdims=True)
        plain = jnp.sum(normal, -1, keepdims=True)
        square = jnp.sum(normal * normal, -1, keepdims=True)
        spread = square - plain * plain * part
        cross = second - first * plain * part
        slope = jnp.where(spread > 1e-3, cross / jnp.maximum(spread, 1e-3), 0.0)
        level = (first - slope * plain) * part
        known = out_one[0] * grads[0, rows].astype(f32)
        for k in range(1, count):
            known = known + out_one[k] * grads[k, rows].astype(f32)
        block = known + (turn * scale[rows, :]) * (total - level - slope * normal)
        return (first, second, level, slope), block.astype(jnp.bfloat16)

    def finish(group, rows, turned):
        first, second = whole_sums(size, width, turned)
        rate = scale[rows, :]
        gain = turn * rate
        for z in range(size):
            level = gain * (turned[:, 8 * z + 2 : 8 * z + 3] - first)
            slope = gain * (turned[:, 8 * z + 3 : 8 * z + 4] - second)
            columns = slice(z * width, (z + 1) * width)
            value = blocks[z, rows].astype(f32) + level
            value = value + slope * whole_normal[rows, columns].astype(f32)
            whole[rows, columns] = value.astype(jnp.bfloat16)
        store(group)
        grad_attended[rows, :] = jnp.dot(
            whole[rows, :], output_rows[...], preferred_element_type=f32
        ).astype(jnp.bfloat16)
        inner[rows, :] = rate * (inner[rows, :] - first - second * own_normal(rows))
        store_inner(group)

    line_exchange(size, tokens, width, chunk, hop, scatter, True, produce, prepare, finish, scratch)
    wait_stores()
    wait_inner()


def whole_sums(size, width, turned):
    first = turned[:, 0:1]
    second = turned[:, 1:2]
    for z in range(1, size):
        first = first + turned[:, 8 * z : 8 * z + 1]
        second = second + turned[:, 8 * z + 1 : 8 * z + 2]
    return first * (1.0 / (size * width)), second * (1.0 / (size * width))


def back_mid(
    size, gated, rows, grads, whole_normal, scale, output_rows, mix, chunk=64, hop=(1, 0, 1)
):
    _, tokens, width = grads.shape
    whole = jax.ShapeDtypeStruct((tokens, size * width), jnp.bfloat16)
    inner = jax.ShapeDtypeStruct((tokens, width), f32)
    groups = tokens // GROUP
    weights = jax.ShapeDtypeStruct((size * width, 2 * gated.shape[2]), jnp.bfloat16)
    heads = output_rows.shape[1] // 4
    output_own = jax.ShapeDtypeStruct((size * width, heads), jnp.bfloat16)
    return call(
        functools.partial(back_mid_kernel, size, chunk, hop),
        (mix, gated, rows, grads, whole_normal, scale, output_rows),
        (SM,) + (pl.ANY,) * 4 + (VM, pl.ANY),
        [whole, inner, jax.ShapeDtypeStruct((tokens, heads), jnp.bfloat16)],
        (pl.ANY, pl.ANY, VM),
        held(gated, weights, grads, whole_normal, output_own, whole, inner, whole)
        + [
            pltpu.SemaphoreType.DMA((size + 5,)),
            pltpu.SemaphoreType.DMA((groups,)),
            pltpu.SemaphoreType.DMA((groups,)),
        ]
        + exchange_scratch(size, tokens, width, chunk, True, True),
        "back_mid",
        3,
        10**9,
    )


def tile_sum(product):
    height, width = product.shape
    folded = jnp.sum(product.reshape(height // 8, 8, width), 0)
    total = folded[:, :128]
    for start in range(128, width, 128):
        total = total + folded[:, start : start + 128]
    return total


def back_sums_kernel(
    size, partial_in, normal_in, first_sum, second_sum, partial, normal, facts, loads, sent, got
):
    tokens, features = partial.shape
    groups = tokens // GROUP
    me = lax.axis_index("col")

    def rows_of(group):
        return pl.ds(pl.multiple_of(group * GROUP, GROUP), GROUP)

    def load(way, group):
        source, target = ((partial_in, partial), (normal_in, normal))[way]
        rows = rows_of(group)
        return pltpu.make_async_copy(source.at[rows], target.at[rows], loads.at[way, group])

    def start_load(group, carry):
        load(0, group).start()
        load(1, group).start()
        return carry

    lax.fori_loop(0, groups, start_load, 0)
    barrier = pltpu.get_barrier_semaphore()
    for member in range(size):

        @pl.when(member != me)
        def _():
            pl.semaphore_signal(barrier, inc=1, device_id={"col": member}, device_id_type=MESH)

    def own(group, carry):
        load(0, group).wait()
        load(1, group).wait()
        rows = rows_of(group)
        total = partial[rows, :].astype(f32)
        one = jnp.sum(total, -1, keepdims=True)
        two = jnp.sum(total * normal[rows, :].astype(f32), -1, keepdims=True)
        lane = lax.broadcasted_iota(jnp.int32, (GROUP, 128), 1)
        packed = jnp.where(lane == 0, one, jnp.where(lane == 1, two, 0.0))
        facts[me, pl.ds(pl.multiple_of(group * 8, 8), 8)] = packed.T[:8]
        return carry

    lax.fori_loop(0, groups, own, 0)
    pl.semaphore_wait(barrier, size - 1)

    def fact_copy(place, member):
        return pltpu.make_async_remote_copy(
            src_ref=facts.at[place],
            dst_ref=facts.at[place],
            send_sem=sent.at[member],
            recv_sem=got.at[place],
            device_id={"col": member},
            device_id_type=MESH,
        )

    for member in range(size):

        @pl.when(member != me)
        def _():
            fact_copy(me, member).start()

    for member in range(size):

        @pl.when(member != me)
        def _():
            fact_copy(member, member).wait()

    def conclude(group, carry):
        fact_rows = pl.ds(pl.multiple_of(group * 8, 8), 8)
        total = facts[0, fact_rows]
        for place in range(1, size):
            total = total + facts[place, fact_rows]
        total = total * (1.0 / features)
        turned = jnp.concatenate([total, jnp.zeros((GROUP - 8, 128), f32)], 0).T
        first_sum[rows_of(group), :] = turned[:, :1]
        second_sum[rows_of(group), :] = turned[:, 1:2]
        return carry

    lax.fori_loop(0, groups, conclude, 0)


def back_sums(size, partial, normal):
    tokens = partial.shape[0]
    dma = pltpu.SemaphoreType.DMA
    return call(
        functools.partial(back_sums_kernel, size),
        (partial, normal),
        (pl.ANY, pl.ANY),
        [jax.ShapeDtypeStruct((tokens, 1), f32)] * 2,
        (VM, VM),
        held(partial, normal)
        + [
            pltpu.VMEM((size, tokens // GROUP * 8, 128), f32),
            dma((2, tokens // GROUP)),
            dma((size,)),
            dma((size,)),
        ],
        "back_sums",
        6,
        10**9,
    )


def back_in_kernel(
    size,
    partial_in,
    first_in,
    last_in,
    normal_in,
    scale,
    first_sum,
    second_sum,
    streams_in,
    streams_grads,
    other_products,
    inner,
    whole_products,
    share,
    first,
    last,
    normal,
    streams,
    products,
    shares,
    loads,
    shares_sent,
    shares_got,
):
    count, tokens, width = streams.shape
    groups = tokens // GROUP
    me = lax.axis_index("col")
    count_rows = lax.axis_size("row")
    own_columns = pl.ds(pl.multiple_of(me * width, width), width)
    waits = start_loads(
        (
            (partial_in.at[:, own_columns], share),
            (first_in, first),
            (last_in, last),
            (normal_in.at[:, own_columns], normal),
            (streams_in, streams),
        ),
        loads,
    )
    barrier = pltpu.get_barrier_semaphore()
    for axis, members in (("col", size), ("row", count_rows)):
        for member in range(members):

            @pl.when(member != lax.axis_index(axis))
            def _():
                pl.semaphore_signal(
                    barrier, inc=1, device_id={axis: member}, device_id_type=MESH
                )

    products[...] = jnp.zeros_like(products)
    for wait in waits:
        wait.wait()

    def conclude(group, carry):
        rows = pl.ds(pl.multiple_of(group * GROUP, GROUP), GROUP)
        total = share[rows, :].astype(f32) + first[rows, :].astype(f32) + last[rows, :].astype(f32)
        own = scale[rows, :] * (
            total - first_sum[rows, :] - second_sum[rows, :] * normal[rows, :].astype(f32)
        )
        inner[rows, :] = own
        for i in range(count):
            products[i] = products[i] + tile_sum(streams[i, rows].astype(f32) * own)
        return carry

    lax.fori_loop(0, groups, conclude, 0)
    parts = [streams_grads[...], other_products[...], products[...]]
    total = jnp.concatenate([jnp.sum(jnp.sum(part, 1), -1, keepdims=True) for part in parts], 0)
    total = jnp.concatenate([total, jnp.zeros((128 - total.shape[0], 1), f32)], 0)
    total = jnp.broadcast_to(total, (128, 128)).T[:8]
    pl.semaphore_wait(barrier, size - 1 + count_rows - 1)
    for axis, members, base in (("col", size, 0), ("row", count_rows, size)):
        here = lax.axis_index(axis)

        def share_copy(source, member):
            return pltpu.make_async_remote_copy(
                src_ref=shares.at[base + source],
                dst_ref=shares.at[base + source],
                send_sem=shares_sent.at[base + member],
                recv_sem=shares_got.at[base + source],
                device_id={axis: member},
                device_id_type=MESH,
            )

        shares[base + here] = total
        for member in range(members):

            @pl.when(member != here)
            def _():
                share_copy(here, member).start()

        for member in range(members):

            @pl.when(member != here)
            def _():
                share_copy(member, member).wait()

        total = shares[base]
        for member in range(1, members):
            total = total + shares[base + member]
    whole_products[...] = total


def back_in(size, partial, first, last, normal, scale, sums, streams, streams_grads, other_products):
    count, tokens, width = streams.shape
    own = -(-count // 8) * 8
    members = size + lax.axis_size("row")
    dma = pltpu.SemaphoreType.DMA
    return call(
        functools.partial(back_in_kernel, size),
        (partial, first, last, normal, scale, *sums, streams, streams_grads, other_products),
        (pl.ANY, pl.ANY, pl.ANY, pl.ANY, VM, VM, VM, pl.ANY, VM, VM),
        [
            jax.ShapeDtypeStruct((tokens, width), f32),
            jax.ShapeDtypeStruct((8, 128), f32),
        ],
        (VM, VM),
        held(first, first, last, first, streams)
        + [
            pltpu.VMEM((own, 8, 128), f32),
            pltpu.VMEM((members, 8, 128), f32),
            dma((5,)),
            dma((members,)),
            dma((members,)),
        ],
        "back_in",
        4,
        10**9,
    )


def end_kernel(mix, streams, grads, branch_one, branch_two, inner_two, final, products):
    count, tokens, width = streams.shape
    through, _, out_one, _ = mixings(mix)
    out_two = [mix[1, j, 1 + count] for j in range(count)]

    @pl.when(pl.program_id(0) == 0)
    def _():
        products[...] = jnp.zeros_like(products)

    def slab(index, sums):
        rows = pl.ds(pl.multiple_of(index * 16, 16), 16)
        sums = list(sums)
        for start in range(0, width, 128):
            columns = slice(start, start + 128)
            values = [streams[i, rows, columns].astype(f32) for i in range(count)]
            above = [grads[i, rows, columns].astype(f32) for i in range(count)]
            one = branch_one[rows, columns]
            two = branch_two[rows, columns].astype(f32)
            below = inner_two[rows, columns]
            for j in range(count):
                value = out_one[j] * one + out_two[j] * two
                for k in range(count):
                    value = value + through[k][j] * values[k]
                final[j, rows, columns] = value.astype(jnp.bfloat16)
            pairs = [(a, below) for a in values]
            pairs = pairs + [(one, b) for b in above]
            pairs = pairs + [(a, two) for a in above]
            pairs = pairs + [(one, below)]
            for place, (a, b) in enumerate(pairs):
                product = a * b
                sums[place] = sums[place] + product[:8] + product[8:]
        return tuple(sums)

    used = 3 * count + 1
    sums = lax.fori_loop(0, tokens // 16, slab, (jnp.zeros((8, 128), f32),) * used)
    for place in range(used):
        products[place] = products[place] + sums[place]


def end_streams(mix, streams, grads, branch_one, branch_two, inner_two, tile=256):
    count, tokens, width = streams.shape
    used = -(-(3 * count + 1) // 8) * 8
    many = pl.BlockSpec((count, tile, width), lambda i: (0, i, 0))
    own = pl.BlockSpec((tile, width), lambda i: (i, 0))
    return pl.pallas_call(
        end_kernel,
        grid=(tokens // tile,),
        out_shape=[
            jax.ShapeDtypeStruct(streams.shape, jnp.bfloat16),
            jax.ShapeDtypeStruct((used, 8, 128), f32),
        ],
        in_specs=[pl.BlockSpec(memory_space=SM), many, many, own, own, own],
        out_specs=[many, pl.BlockSpec((used, 8, 128), lambda i: (0, 0, 0))],
        compiler_params=pltpu.CompilerParams(vmem_limit_bytes=60 * 2**20),
        cost_estimate=pl.CostEstimate(
            flops=60 * streams.size, bytes_accessed=9 * streams.size, transcendentals=0
        ),
        name="end_streams",
    )(mix, streams, grads, branch_one, branch_two, inner_two)


def grad_kernel(mix, grads, inner_two, inner_one, out):
    count = grads.shape[0]
    through, in_two, _, _ = mixings(mix)
    above = [grads[k].astype(f32) for k in range(count)]
    below, own = inner_two[...], inner_one[...]
    for i in range(count):
        value = in_two[i] * below + mix[0, i, 0] * own
        for k in range(count):
            value = value + through[i][k] * above[k]
        out[i] = value


def grad_streams_of(mix, grads, inner_two, inner_one, tile=256):
    count, tokens, width = grads.shape
    many = pl.BlockSpec((count, tile, width), lambda i: (0, i, 0))
    own = pl.BlockSpec((tile, width), lambda i: (i, 0))
    return pl.pallas_call(
        grad_kernel,
        grid=(tokens // tile,),
        out_shape=jax.ShapeDtypeStruct(grads.shape, f32),
        in_specs=[pl.BlockSpec(memory_space=SM), many, own, own],
        out_specs=many,
        compiler_params=pltpu.CompilerParams(vmem_limit_bytes=60 * 2**20),
        cost_estimate=pl.CostEstimate(
            flops=10 * grads.size, bytes_accessed=8 * grads.size, transcendentals=0
        ),
        name="grad_streams",
    )(mix, grads, inner_two, inner_one)


def tiled(body, grid, operands, specs, outs, out_specs, scratch, flops, name):
    moved = sum(array.size * array.dtype.itemsize for array in list(operands) + (list(outs) if isinstance(outs, list) else [outs]))
    return pl.pallas_call(
        body,
        grid=grid,
        out_shape=outs,
        in_specs=specs,
        out_specs=out_specs,
        scratch_shapes=scratch,
        compiler_params=pltpu.CompilerParams(vmem_limit_bytes=60 * 2**20),
        cost_estimate=pl.CostEstimate(flops=flops, bytes_accessed=moved, transcendentals=0),
        name=name,
    )(*operands)


def gate_kernel(
    size,
    steps,
    chunks,
    whole,
    gate_rows,
    upper_rows,
    down_rows,
    own_in,
    before_in,
    after_in,
    active_out,
    by_gate,
    by_upper,
    partial,
    gathered,
    active,
    blocks,
    loads,
    stores,
    sent,
    got,
):
    step = pl.program_id(0)
    me = lax.axis_index("col")
    tiles, tile = active.shape[1] // gate_rows.shape[1], gate_rows.shape[1]
    tokens, width = blocks.shape[1:]
    chunk = tokens // chunks
    edge = size - 1
    right, left = jnp.minimum(me + 1, edge), jnp.maximum(me - 1, 0)
    other = jnp.where(me == edge, left, right)

    def load(place, way):
        source = (own_in, before_in, after_in)[way]
        return pltpu.make_async_copy(source, blocks.at[place], loads.at[way])

    def store(place):
        return pltpu.make_async_copy(
            blocks.at[place],
            gathered.at[:, pl.ds(pl.multiple_of(place * width, width), width)],
            stores.at[place],
        )

    def send(place, index, way, device):
        rows = pl.ds(pl.multiple_of(index * chunk, chunk), chunk)
        return pltpu.make_async_remote_copy(
            src_ref=blocks.at[place, rows],
            dst_ref=blocks.at[place, rows],
            send_sem=sent.at[way, place, index],
            recv_sem=got.at[place, index],
            device_id={"col": device},
            device_id_type=MESH,
        )

    def both_ways(near, act):
        for way, place, target, onward in (
            (0, me - near, right, me < edge),
            (1, me + near, left, me > 0),
        ):

            @pl.when((place >= 0) & (place < size))
            def _():
                act(way, place, target, onward)

    @pl.when(step == 0)
    def _():
        load(me, 0).start()
        both_ways(1, lambda way, place, target, onward: load(place, 1 + way).start())
        barrier = pltpu.get_barrier_semaphore()
        both_ways(
            1,
            lambda way, place, target, onward: pl.semaphore_signal(
                barrier, inc=1, device_id={"col": place}, device_id_type=MESH
            ),
        )
        load(me, 0).wait()
        store(me).start()
        both_ways(1, lambda way, place, target, onward: load(place, 1 + way).wait())

        @pl.when((me > 0) & (me < edge))
        def _():
            pl.semaphore_wait(barrier, 2)

        @pl.when((me == 0) | (me == edge))
        def _():
            pl.semaphore_wait(barrier, 1)


        def begin(way, place, target, onward):
            store(place).start()

            @pl.when(onward)
            def _():
                for index in range(chunks):
                    send(place, index, way, target).start()

        both_ways(1, begin)

    for near in range(2, size - 1):
        index = step - (steps - chunks - (size - 2 - near))

        def forward(way, place, target, onward):
            send(place, index, way, other).wait_recv()

            @pl.when(onward)
            def _():
                send(place, index, way, target).start()

        @pl.when((index >= 0) & (index < chunks))
        def _():
            both_ways(near, forward)

    @pl.when(step < tiles)
    def _():
        gate = jnp.dot(whole[...], gate_rows[...], preferred_element_type=f32)
        upper = jnp.dot(whole[...], upper_rows[...], preferred_element_type=f32)
        sigma = jax.nn.sigmoid(gate)
        silu = gate * sigma
        value = (silu * upper).astype(jnp.bfloat16)
        active_out[...] = value
        active[:, pl.ds(pl.multiple_of(step * tile, tile), tile)] = value
        by_gate[...] = (upper * sigma * (1.0 + gate * (1.0 - sigma))).astype(jnp.bfloat16)
        by_upper[...] = silu.astype(jnp.bfloat16)

    @pl.when(step >= tiles)
    def _():
        partial[...] = lax.dot_general(
            active[...], down_rows[...], LANES, preferred_element_type=f32
        ).astype(jnp.bfloat16)

    @pl.when(step == steps - 1)
    def _():
        def last(way, place, target, onward):
            for index in range(chunks):
                send(place, index, way, other).wait_recv()

        both_ways(size - 1, last)
        for near in range(2, size):
            both_ways(near, lambda way, place, target, onward: store(place).start())

        def sends_done(way, place, target, onward):
            @pl.when(onward)
            def _():
                for index in range(chunks):
                    send(place, index, way, other).wait_send()

        for near in range(1, size - 1):
            both_ways(near, sends_done)
        for place in range(size):
            store(place).wait()


def gate_forward(size, whole, weights, own, before, after, tile=256):
    tokens, features = whole.shape
    hidden = weights.shape[1] // 3
    tile = min(tile, hidden)
    tiles = hidden // tile
    down_tile = min(512, features)
    steps = tiles + features // down_tile
    chunks = 1
    while 2 * chunks <= min(8, steps - size + 3):
        chunks = 2 * chunks
    wide = pl.BlockSpec((tokens, tile), lambda j: (0, jnp.minimum(j, tiles - 1)))
    plain = pl.BlockSpec(memory_space=pl.ANY)
    dma = pltpu.SemaphoreType.DMA
    wide_shape = jax.ShapeDtypeStruct((tokens, hidden), jnp.bfloat16)
    return pl.pallas_call(
        functools.partial(gate_kernel, size, steps, chunks),
        grid=(steps,),
        out_shape=[wide_shape] * 3 + [jax.ShapeDtypeStruct((tokens, features), jnp.bfloat16)] * 2,
        in_specs=[
            pl.BlockSpec((tokens, features), lambda j: (0, 0)),
            pl.BlockSpec((features, tile), lambda j: (0, jnp.minimum(j, tiles - 1))),
            pl.BlockSpec((features, tile), lambda j: (0, tiles + jnp.minimum(j, tiles - 1))),
            pl.BlockSpec((down_tile, hidden), lambda j: (jnp.maximum(j - tiles, 0), 2)),
            plain,
            plain,
            plain,
        ],
        out_specs=[wide] * 3
        + [pl.BlockSpec((tokens, down_tile), lambda j: (0, jnp.maximum(j - tiles, 0))), plain],
        scratch_shapes=[
            pltpu.VMEM((tokens, hidden), jnp.bfloat16),
            pltpu.VMEM((size, tokens, own.shape[1]), jnp.bfloat16),
            dma((3,)),
            dma((size,)),
            dma((2, size, chunks)),
            dma((size, chunks)),
        ],
        compiler_params=pltpu.CompilerParams(
            collective_id=5, has_side_effects=True, vmem_limit_bytes=60 * 2**20
        ),
        cost_estimate=pl.CostEstimate(
            flops=6 * tokens * features * hidden,
            bytes_accessed=2 * weights.size,
            transcendentals=0,
        ),
        name="gate_forward",
    )(whole, weights, weights, weights, own, before, after)


def gate_back_kernel(whole, rows, by_gate, by_upper, grads):
    grad = jnp.dot(whole[...], rows[...], preferred_element_type=f32)
    grads[0] = (grad * by_gate[...].astype(f32)).astype(jnp.bfloat16)
    grads[1] = (grad * by_upper[...].astype(f32)).astype(jnp.bfloat16)


def gate_back(whole, weights, by_gate, by_upper, tile=512):
    tokens, features = whole.shape
    hidden = weights.shape[1] // 3
    tile = min(tile, hidden)
    tiles = hidden // tile
    part = pl.BlockSpec((tokens, tile), lambda j: (0, j))
    return tiled(
        gate_back_kernel,
        (tiles,),
        (whole, weights, by_gate, by_upper),
        [
            pl.BlockSpec((tokens, features), lambda j: (0, 0)),
            pl.BlockSpec((features, tile), lambda j: (0, 2 * tiles + j)),
            part,
            part,
        ],
        jax.ShapeDtypeStruct((2, tokens, hidden), jnp.bfloat16),
        pl.BlockSpec((2, tokens, tile), lambda j: (0, 0, j)),
        [],
        2 * tokens * features * hidden,
        "gate_back",
    )


def outer_kernel(cut, left, right, other_left, other_right, out, turned):
    step = pl.program_id(0)

    @pl.when(step == 0)
    def _():
        turned[...] = left[...].T

    @pl.when(step == cut)
    def _():
        turned[...] = other_left[...].T

    @pl.when(step < cut)
    def _():
        out[...] = jnp.dot(turned[...], right[...], preferred_element_type=f32).astype(jnp.bfloat16)

    @pl.when(step >= cut)
    def _():
        out[...] = jnp.dot(turned[...], other_right[...], preferred_element_type=f32).astype(
            jnp.bfloat16
        )


def outer(left, right, other_left, other_right, tile=512, name="outer"):
    tokens, rows = left.shape
    tile = min(tile, other_right.shape[1])
    other = other_right.shape[1] // tile
    if right.ndim == 3:
        tiles = right.shape[2] // tile
        cut = right.shape[0] * tiles
        clip = lambda j: jnp.minimum(j, cut - 1)
        spec = pl.BlockSpec((None, tokens, tile), lambda j: (clip(j) // tiles, 0, clip(j) % tiles))
    else:
        cut = right.shape[1] // tile
        spec = pl.BlockSpec((tokens, tile), lambda j: (0, jnp.minimum(j, cut - 1)))
    whole = pl.BlockSpec((tokens, rows), lambda j: (0, 0))
    return tiled(
        functools.partial(outer_kernel, cut),
        (cut + other,),
        (left, right, other_left, other_right),
        [whole, spec, whole, pl.BlockSpec((tokens, tile), lambda j: (0, jnp.maximum(j - cut, 0)))],
        jax.ShapeDtypeStruct((rows, (cut + other) * tile), jnp.bfloat16),
        pl.BlockSpec((rows, tile), lambda j: (0, j)),
        [pltpu.VMEM((rows, tokens), jnp.bfloat16)],
        2 * tokens * rows * (cut + other) * tile,
        name,
    )


def product_kernel(dims, left, right, out):
    total = lax.dot_general(left[...], right[...], dims, preferred_element_type=f32)
    out[...] = total.astype(out.dtype)


def product(left, right, start, columns, kind=jnp.bfloat16, tile=512, name="product"):
    tokens, depth = left.shape
    tile = min(tile, columns)
    first = start // tile
    return tiled(
        functools.partial(product_kernel, (((1,), (0,)), ((), ()))),
        (columns // tile,),
        (left, right),
        [
            pl.BlockSpec((tokens, depth), lambda j: (0, 0)),
            pl.BlockSpec((depth, tile), lambda j: (0, first + j)),
        ],
        jax.ShapeDtypeStruct((tokens, columns), kind),
        pl.BlockSpec((tokens, tile), lambda j: (0, j)),
        [],
        2 * tokens * depth * columns,
        name,
    )


def heads_kernel(ends, grads, rows, *refs):
    width = grads.shape[2]
    total = 0.0
    for k in range(grads.shape[0]):
        total = total + lax.dot_general(
            grads[k], rows[:, k * width : (k + 1) * width], LANES, preferred_element_type=f32
        )
    total = total.astype(jnp.bfloat16)
    if ends:
        out, low, high = refs

        @pl.when(pl.program_id(0) == 0)
        def _():
            low[...] = total

        @pl.when(pl.program_id(0) == 1)
        def _():
            high[...] = total

    else:
        out = refs[1]
    out[...] = total


def heads_product(size, grads, weights, begun=None):
    count, tokens, width = grads.shape
    rows = weights.shape[0]
    tile = rows // size
    ends = begun is None
    place = (lambda j: j * (size - 1)) if ends else (lambda j: j + 1)
    whole = jax.ShapeDtypeStruct((tokens, rows), jnp.bfloat16)
    one = jax.ShapeDtypeStruct((tokens, tile), jnp.bfloat16)
    own = pl.BlockSpec((tokens, tile), lambda j: (0, 0))
    steps = 2 if ends else size - 2
    return pl.pallas_call(
        functools.partial(heads_kernel, ends),
        grid=(steps,),
        out_shape=[whole, one, one] if ends else whole,
        in_specs=[
            pl.BlockSpec((count, tokens, width), lambda j: (0, 0, 0)),
            pl.BlockSpec((tile, count * width), lambda j: (place(j), 0)),
        ]
        + ([] if ends else [pl.BlockSpec(memory_space=pl.ANY)]),
        out_specs=[pl.BlockSpec((tokens, tile), lambda j: (0, place(j))), own, own]
        if ends
        else pl.BlockSpec((tokens, tile), lambda j: (0, place(j))),
        input_output_aliases={} if ends else {2: 0},
        compiler_params=pltpu.CompilerParams(vmem_limit_bytes=60 * 2**20),
        cost_estimate=pl.CostEstimate(
            flops=2 * count * tokens * width * steps * tile,
            bytes_accessed=4 * tokens * rows,
            transcendentals=0,
        ),
        name="heads_product",
    )(*((grads, weights) if ends else (grads, weights, begun)))


def fill_bias(bias, column, row):
    tile = min(256, bias.shape[0])
    for start in range(0, bias.shape[0], tile):
        shape = (tile, bias.shape[1])
        index = lax.broadcasted_iota(jnp.int32, shape, 0) + start
        allowed = (column[start : start + tile] == row[...].astype(f32)) & (
            lax.broadcasted_iota(jnp.int32, shape, 1) <= index
        )
        bias[start : start + tile] = jnp.where(allowed, 0.0, MASKED)


def key_span(start, block):
    return max(0, start + 1 - LONGEST) // 128 * 128, start + block


def block_probs(queries, key_heads, bias):
    scores = lax.dot_general(queries, key_heads, LANES, preferred_element_type=f32) + bias
    expo = jnp.exp2(scores - jnp.max(scores, -1, keepdims=True))
    return expo * (1.0 / jnp.sum(expo, -1, keepdims=True))


def attend_forward_kernel(
    block,
    query,
    key,
    value,
    cosine,
    sine,
    column,
    row,
    queries,
    key_heads,
    value_heads,
    attended,
    bias,
):
    length = query.shape[0]

    @pl.when(pl.program_id(0) == 0)
    def _():
        fill_bias(bias, column, row)

    cosines = jnp.concatenate([cosine[...], cosine[...]], 1)
    sines = jnp.concatenate([-sine[...], sine[...]], 1)

    def turn(values):
        return values * cosines + pltpu.roll(values, HEAD_DIM // 2, 1) * sines

    queries[...] = (turn(query[...]) * (HEAD_DIM ** (-0.5) * LOG2E)).astype(jnp.bfloat16)
    key_heads[...] = turn(key[...]).astype(jnp.bfloat16)
    value_heads[...] = value[...].astype(jnp.bfloat16)
    for start in range(0, length, block):
        first, end = key_span(start, block)
        probs = block_probs(
            queries[start:end], key_heads[first:end], bias[start:end, first:end]
        )
        result = jnp.dot(
            probs.astype(jnp.bfloat16), value_heads[first:end], preferred_element_type=f32
        )
        attended[start:end, :] = result.astype(jnp.bfloat16)


def attend_forward(projected, cosine, sine, column, row):
    length, width = projected.shape
    width = width // 3
    heads = width // HEAD_DIM
    block = min(256, length)

    def head(offset):
        return pl.BlockSpec((length, HEAD_DIM), lambda h: (0, h + offset))

    def fixed(array):
        return pl.BlockSpec(array.shape, lambda h: (0, 0))

    return pl.pallas_call(
        functools.partial(attend_forward_kernel, block),
        grid=(heads,),
        out_shape=[jax.ShapeDtypeStruct((length, width), jnp.bfloat16)] * 4,
        in_specs=[head(0), head(heads), head(2 * heads)]
        + [fixed(array) for array in (cosine, sine, column, row)],
        out_specs=[head(0)] * 4,
        scratch_shapes=[pltpu.VMEM((length, length), f32)],
        compiler_params=pltpu.CompilerParams(vmem_limit_bytes=60 * 2**20),
        name="attend_forward",
    )(projected, projected, projected, cosine, sine, column, row)


def attend_back_kernel(
    block,
    queries,
    key_heads,
    value_heads,
    grad_result,
    cosine,
    sine,
    column,
    row,
    grads,
    key_sum,
    value_sum,
    bias,
):
    length = queries.shape[0]

    @pl.when(pl.program_id(0) == 0)
    def _():
        fill_bias(bias, column, row)

    key_sum[...] = jnp.zeros_like(key_sum)
    value_sum[...] = jnp.zeros_like(value_sum)

    def turn_back(values, rows, factor):
        values = values * factor
        cosines = jnp.concatenate([cosine[rows], cosine[rows]], 1)
        sines = jnp.concatenate([-sine[rows], sine[rows]], 1)
        return (values * cosines - pltpu.roll(values, HEAD_DIM // 2, 1) * sines).astype(
            jnp.bfloat16
        )

    for start in range(0, length, block):
        first, end = key_span(start, block)
        query, grad_part = queries[start:end], grad_result[start:end]
        probs = block_probs(query, key_heads[first:end], bias[start:end, first:end])
        grad_probs = lax.dot_general(
            grad_part, value_heads[first:end], LANES, preferred_element_type=f32
        )
        row_sum = jnp.sum(probs * grad_probs, -1, keepdims=True)
        grad_scores = (probs * (grad_probs - row_sum)).astype(jnp.bfloat16)
        grad_part_query = jnp.dot(grad_scores, key_heads[first:end], preferred_element_type=f32)
        grads[0, start:end] = turn_back(
            grad_part_query, pl.ds(start, block), HEAD_DIM ** (-0.5)
        )
        key_sum[first:end, :] += lax.dot_general(
            grad_scores, query, ROWS, preferred_element_type=f32
        )
        value_sum[first:end, :] += lax.dot_general(
            probs.astype(jnp.bfloat16), grad_part, ROWS, preferred_element_type=f32
        )
    grads[1] = turn_back(key_sum[...], pl.ds(0, length), 1.0 / LOG2E)
    grads[2] = value_sum[...].astype(jnp.bfloat16)


def attend_back(queries, key_heads, value_heads, grad_result, cosine, sine, column, row):
    length, width = queries.shape
    heads = width // HEAD_DIM
    block = min(256, length)
    head = pl.BlockSpec((length, HEAD_DIM), lambda h: (0, h))

    def fixed(array):
        return pl.BlockSpec(array.shape, lambda h: (0, 0))

    return pl.pallas_call(
        functools.partial(attend_back_kernel, block),
        grid=(heads,),
        out_shape=jax.ShapeDtypeStruct((3, length, width), jnp.bfloat16),
        in_specs=[head] * 4 + [fixed(array) for array in (cosine, sine, column, row)],
        out_specs=pl.BlockSpec((3, length, HEAD_DIM), lambda h: (0, 0, h)),
        scratch_shapes=[pltpu.VMEM((length, HEAD_DIM), f32)] * 2
        + [pltpu.VMEM((length, length), f32)],
        compiler_params=pltpu.CompilerParams(vmem_limit_bytes=60 * 2**20),
        name="attend_back",
    )(queries, key_heads, value_heads, grad_result, cosine, sine, column, row)


def update(weight, grad, moment, average, rate):
    step_grad = grad + DECAY * weight
    moment_new = MOMENTUM * moment + step_grad
    weight_new = weight - rate * (step_grad + MOMENTUM * moment_new)
    return (weight_new, moment_new, average + (weight_new - average) / (STEP + 1))


def hyper_kernel(rate, products, mix, moment, average, new_mix, new_moment, new_average):
    count = mix.shape[1]
    span = range(count)
    square = count * count
    shared = [[products[0, i * count + j] for j in span] for i in span]
    below = [products[0, square + i] for i in span]
    branch = [products[0, square + count + j] for j in span]
    outward = [products[0, square + 2 * count + j] for j in span]
    both = products[0, square + 3 * count]
    start = square + -(-(3 * count + 1) // 8) * 8
    above = [products[0, start + i] for i in span]

    def dot(left, right):
        total = left[0] * right[0]
        for a, b in zip(left[1:], right[1:]):
            total = total + a * b
        return total

    for i in span:
        rows_two = [[mix[1, j, 1 + k] for k in span] for j in span]
        column_one = [mix[0, k, 1 + i] for k in span]
        onto = mix[0, i, 1 + count]
        one = [above[i]]
        one = one + [dot(shared[i], rows_two[j]) + below[i] * mix[1, j, 0] for j in span]
        one.append(dot(rows_two[i], branch) + mix[1, i, 0] * both)
        two = [dot(column_one, below) + onto * both]
        two = two + [
            dot(column_one, [shared[k][j] for k in span]) + onto * branch[j] for j in span
        ]
        two.append(outward[i])
        for layer, grads in ((0, one), (1, two)):
            for j, grad in enumerate(grads):
                at = (layer, i, j)
                results = update(mix[at], grad, moment[at], average[at], rate)
                new_mix[at], new_moment[at], new_average[at] = results


def update_mix(products, mix, moment, average, rate):
    place = pl.BlockSpec(memory_space=SM)
    return pl.pallas_call(
        functools.partial(hyper_kernel, rate),
        out_shape=[jax.ShapeDtypeStruct(mix.shape, f32)] * 3,
        in_specs=[place] * 4,
        out_specs=[place] * 3,
        name="update_mix",
    )(products, mix, moment, average)


def update_kernel(rate, turned, weight, grad, moment, average, *outs):
    value = grad[...].astype(f32)
    results = update(weight[...], value.T if turned else value, moment[...], average[...], rate)
    for out, result in zip(outs, results):
        out[...] = result


def update_blocks(weight, grad, moment, average, rate, start):
    turned = weight.ndim == 2
    rows = grad.shape[0]
    columns = weight.shape[0] if turned else weight.shape[2]
    tile = min(columns, 512)
    tiles = columns // tile
    first = start // tile
    if turned:
        grid = (tiles,)
        own = pl.BlockSpec((tile, rows), lambda j: (j, 0))
        place = pl.BlockSpec((rows, tile), lambda j: (0, first + j))
    else:
        grid = (weight.shape[0], tiles)
        own = pl.BlockSpec((None, rows, tile), lambda k, j: (k, 0, j))
        place = pl.BlockSpec((rows, tile), lambda k, j: (0, first + k * tiles + j))
    return pl.pallas_call(
        functools.partial(update_kernel, rate, turned),
        grid=grid,
        out_shape=[jax.ShapeDtypeStruct(weight.shape, f32)] * 3,
        in_specs=[own, place, own, own],
        out_specs=[own] * 3,
        compiler_params=pltpu.CompilerParams(vmem_limit_bytes=60 * 2**20),
        cost_estimate=pl.CostEstimate(
            flops=10 * weight.size, bytes_accessed=26 * weight.size, transcendentals=0
        ),
        name="update",
    )(weight, grad, moment, average)


def tie(*values):
    return lax.optimization_barrier(values)


def line_ways():
    size = lax.axis_size("col")
    up = [(i, i + 1) for i in range(size - 1)]
    down = [(i + 1, i) for i in range(size - 1)]
    return size, up, down


def scatter_steps(partial, low, high):
    size, up, down = line_ways()
    me = lax.axis_index("col")
    width = partial.shape[1] // size

    def share(place):
        return lax.dynamic_slice_in_dim(partial, place * width, width, 1)

    first, last = high, low
    for step in range(1, size):
        if step > 1:
            first = share(jnp.minimum(me + size - step, size - 1)).astype(f32) + first.astype(f32)
            last = share(jnp.maximum(me - size + step, 0)).astype(f32) + last.astype(f32)
            first = first.astype(jnp.bfloat16)
            last = last.astype(jnp.bfloat16)
        first, last = yield (lax.ppermute(first, "col", up), lax.ppermute(last, "col", down))
    yield [first, last]


def advance(steps, got, *values):
    moved = next(steps) if got is None else steps.send(got)
    tied = tie(*moved, *values)
    return tied[: len(moved)], tied[len(moved) :]


def finish_line(steps, got):
    moved = steps.send(got)
    while isinstance(moved, tuple):
        moved = steps.send(moved)
    return moved


def scatter_rows(grad):
    return lax.psum_scatter(grad, "row", scatter_dimension=0, tiled=True)


def pack_kernel(weights, turned, out):
    count, _, columns = weights.shape
    for k in range(count):
        out[:, k * columns : (k + 1) * columns] = weights[k].astype(jnp.bfloat16)
    out[:, count * columns :] = turned[...].T.astype(jnp.bfloat16)


def pack(weights, turned):
    count, rows, columns = weights.shape
    return pl.pallas_call(
        pack_kernel,
        out_shape=jax.ShapeDtypeStruct((rows, count * columns + turned.shape[0]), jnp.bfloat16),
        in_specs=[pl.BlockSpec(memory_space=VM)] * 2,
        out_specs=pl.BlockSpec(memory_space=VM),
        name="pack",
    )(weights, turned)


def per_device(
    streams,
    segments,
    attention_in,
    attention_out,
    gate_up,
    down_weights,
    hyper_mix,
    moment_attention_in,
    moment_attention_out,
    moment_gate_up,
    moment_down_weights,
    moment_hyper_mix,
    average_attention_in,
    average_attention_out,
    average_gate_up,
    average_down_weights,
    average_hyper_mix,
    cotangent,
):
    size = lax.axis_size("col")
    low = jnp.bfloat16
    count, length, width = streams.shape

    attention_weights = lax.all_gather(
        pack(attention_in, attention_out), "row", axis=0, tiled=True
    )
    whole_one, scale_one, grad_two, streams_grads, hidden_weights, column, cosine, sine = norm_in(
        size, streams, cotangent, gate_up, down_weights, segments, hyper_mix
    )
    hidden_weights = lax.all_gather(hidden_weights, "row", axis=0, tiled=True)
    heads = attention_in.shape[2]
    _, up, down = line_ways()
    before = lax.ppermute(grad_two, "col", up)
    after = lax.ppermute(grad_two, "col", down)
    projected = product(whole_one, attention_weights, 0, 3 * heads, f32, heads, "project_in")
    queries, key_heads, value_heads, attended = attend_forward(
        projected, cosine, sine, column, segments
    )
    attended, before, after = tie(attended, before, after)
    whole_two, scale_two, branch_one = norm_mid(
        size, attended, attention_weights, streams, hyper_mix
    )

    active, by_gate, by_upper, partial_two, whole_grad_two = gate_forward(
        size, whole_two, hidden_weights, grad_two, before, after
    )
    branch_two = lax.psum_scatter(partial_two, "col", scatter_dimension=1, tiled=True)
    grad_gated = gate_back(whole_grad_two, hidden_weights, by_gate, by_upper)
    grad_hidden = outer(whole_two, grad_gated, whole_grad_two, active, name="outer_hidden")
    grad_hidden, grad_gated = tie(grad_hidden, grad_gated)
    grad_hidden = scatter_rows(grad_hidden)
    whole_grad_one, inner_two, grad_attended = back_mid(
        size,
        grad_gated,
        hidden_weights,
        cotangent,
        whole_two,
        scale_two,
        attention_weights,
        hyper_mix,
    )

    grad_attended, branch_two = tie(grad_attended, branch_two)
    grad_heads = attend_back(
        queries, key_heads, value_heads, grad_attended, cosine, sine, column, segments
    )
    tokens_all = length * lax.axis_size("row")
    token_scale = tokens_all ** (-0.5)
    model_rate = D ** (-0.5) * token_scale
    begun, low_share, high_share = heads_product(size, grad_heads, attention_weights)
    partial_one = heads_product(size, grad_heads, attention_weights, begun)
    steps = scatter_steps(partial_one, low_share, high_share)
    grad_attention = outer(
        whole_one, grad_heads, whole_grad_one, attended, name="outer_attention"
    )
    got, (grad_attention,) = advance(steps, None, grad_attention)
    grad_attention = scatter_rows(grad_attention)
    third = update_blocks(gate_up, grad_hidden, moment_gate_up, average_gate_up, model_rate, 0)
    fourth = update_blocks(
        down_weights,
        grad_hidden,
        moment_down_weights,
        average_down_weights,
        FF ** (-0.5) * token_scale,
        gate_up.shape[0] * gate_up.shape[2],
    )
    got, hidden = advance(steps, got, *third, *fourth)
    third, fourth = hidden[:3], hidden[3:]
    final, other_products = end_streams(
        hyper_mix,
        streams,
        cotangent,
        branch_one,
        branch_two,
        inner_two,
    )
    sums = back_sums(size, partial_one, whole_one)
    got, (other_products, *sums) = advance(steps, got, other_products, *sums)
    first_part, last_part = finish_line(steps, got)
    inner_one, products = back_in(
        size,
        partial_one,
        first_part,
        last_part,
        whole_one,
        scale_one,
        sums,
        streams,
        streams_grads,
        other_products,
    )
    grad_streams = grad_streams_of(hyper_mix, cotangent, inner_two, inner_one)

    products, grad_attention = tie(products, grad_attention)
    first = update_blocks(
        attention_in, grad_attention, moment_attention_in, average_attention_in, model_rate, 0
    )
    second = update_blocks(
        attention_out,
        grad_attention,
        moment_attention_out,
        average_attention_out,
        model_rate,
        attention_in.shape[0] * heads,
    )
    fifth = update_mix(
        products, hyper_mix, moment_hyper_mix, average_hyper_mix, 0.05 * (tokens_all * D) ** (-0.5)
    )
    return (
        final,
        grad_streams,
        first[0],
        first[1],
        first[2],
        second[0],
        second[1],
        second[2],
        third[0],
        third[1],
        third[2],
        fourth[0],
        fourth[1],
        fourth[2],
        fifth[0],
        fifth[1],
        fifth[2],
    )


def solution(mesh):
    in_specs = (
        P(None, "row", "col"),
        P("row", None),
        P(None, "row", "col"),
        P("col", "row"),
        P(None, "row", "col"),
        P("col", "row"),
        P(),
        P(None, "row", "col"),
        P("col", "row"),
        P(None, "row", "col"),
        P("col", "row"),
        P(),
        P(None, "row", "col"),
        P("col", "row"),
        P(None, "row", "col"),
        P("col", "row"),
        P(),
        P(None, "row", "col"),
    )
    out_specs = (
        P(None, "row", "col"),
        P(None, "row", "col"),
        P(None, "row", "col"),
        P(None, "row", "col"),
        P(None, "row", "col"),
        P("col", "row"),
        P("col", "row"),
        P("col", "row"),
        P(None, "row", "col"),
        P(None, "row", "col"),
        P(None, "row", "col"),
        P("col", "row"),
        P("col", "row"),
        P("col", "row"),
        P(),
        P(),
        P(),
    )
    return jax.shard_map(
        per_device, mesh=mesh, in_specs=in_specs, out_specs=out_specs, check_vma=False
    )
```

```python
import functools

import jax
import jax.numpy as jnp
from jax import lax
from jax.experimental import pallas as pl
from jax.experimental.pallas import tpu as pltpu
from jax.sharding import PartitionSpec as P

D = 2048
HEAD_DIM = 128
FF = 8192
STEP = 8


EPSILON = 1e-05
MASKED = -1e30
MOMENTUM = 0.9
DECAY = 0.01
GROUP = 128
MESH = pl.DeviceIdType.MESH
VM, SM = pltpu.VMEM, pltpu.SMEM
f32 = jnp.float32
LONGEST = 512
LOG2E = 1.4426950408889634
LANES = (((1,), (1,)), ((), ()))
ROWS = (((0,), (0,)), ((), ()))


def line_exchange(
    size, tokens, width, chunk, hop, scatter, gather, produce, prepare, finish, scratch, during=None, rows_too=0
):
    recv, blocks, facts, own_facts, sums_sent, sums_got, blocks_sent, blocks_got, facts_sent, facts_got = scratch
    me = lax.axis_index("col")
    chunks = tokens // chunk
    per_group = GROUP // chunk
    groups = tokens // GROUP
    edge = size - 1

    hop, wait_hop, pass_hop = hop

    def far(place):
        lag = jnp.maximum(place, edge - place) * hop + wait_hop
        return lag if scatter is not None else place * 0

    def remote(source, target, sent, got, device):
        return pltpu.make_async_remote_copy(
            src_ref=source,
            dst_ref=target,
            send_sem=sent,
            recv_sem=got,
            device_id={"col": device},
            device_id_type=MESH,
        )

    def rows(index):
        return pl.ds(pl.multiple_of(index * chunk, chunk), chunk)

    def group_rows(group):
        return pl.ds(pl.multiple_of(group * GROUP, GROUP), GROUP)

    def sum_copy(shard, slot, index, device):
        return remote(
            scatter.at[rows(index), pl.ds(shard * width, width)],
            recv.at[slot, rows(index)],
            sums_sent.at[shard, index],
            sums_got.at[slot, index],
            device,
        )

    def block_copy(place, index, way, device):
        return remote(
            blocks.at[place, rows(index)],
            blocks.at[place, rows(index)],
            blocks_sent.at[way, place, index],
            blocks_got.at[place, index],
            device,
        )

    def fact_copy(place, group, device):
        return remote(
            facts.at[group, pl.ds(pl.multiple_of(place * 8, 8), 8)],
            facts.at[group, pl.ds(pl.multiple_of(place * 8, 8), 8)],
            facts_sent.at[device, group],
            facts_got.at[place, group],
            device,
        )

    right = jnp.minimum(me + 1, edge)
    left = jnp.maximum(me - 1, 0)
    other = jnp.where(me == edge, left, right)

    def inside(index):
        return (index >= 0) & (index < chunks)

    def relay_sum(shard, slot, index, fresh, target):
        columns = slice(shard * width, (shard + 1) * width)

        @pl.when(jnp.logical_not(fresh))
        def _():
            sum_copy(shard, shard, index, other).wait_recv()
            total = scatter[rows(index), columns].astype(f32) + recv[shard, rows(index)].astype(f32)
            scatter[rows(index), columns] = total.astype(jnp.bfloat16)

        sum_copy(shard, slot, index, target).start()

    def relay_sums(step):
        index = step - me * hop

        @pl.when(inside(index))
        def _():
            for shard in range(size - 1, 0, -1):

                @pl.when(shard > me)
                def _():
                    slot = jnp.where(me + 1 == shard, size, shard)
                    relay_sum(shard, slot, index, me == 0, right)

        back = step - (edge - me) * hop

        @pl.when(inside(back))
        def _():
            for shard in range(size - 1):

                @pl.when(shard < me)
                def _():
                    relay_sum(shard, shard, back, me == edge, left)

    def ready(step):
        index = step - far(me)

        @pl.when(inside(index))
        def _():
            if scatter is not None:

                @pl.when(me > 0)
                def _():
                    sum_copy(0, size, index, other).wait_recv()

                @pl.when(me < edge)
                def _():
                    sum_copy(0, me, index, other).wait_recv()

                start = pl.multiple_of(me * width, width)
                total = scatter[rows(index), pl.ds(start, width)].astype(f32)
                total = total + jnp.where(me > 0, recv[size, rows(index)].astype(f32), 0.0)
                total = total + jnp.where(me < edge, recv[me, rows(index)].astype(f32), 0.0)
            else:
                total = None
            columns, block = prepare(rows(index), total)
            lane = lax.broadcasted_iota(jnp.int32, (chunk, 128), 1)
            packed = jnp.zeros((chunk, 128), f32)
            for place, column in enumerate(columns):
                packed = jnp.where(lane == place, column, packed)
            within = lax.rem(index, per_group)
            own_facts[pl.ds(pl.multiple_of(within * chunk, chunk), chunk), :] = packed
            if gather:
                blocks[me, rows(index)] = block

                @pl.when(me < edge)
                def _():
                    block_copy(me, index, 0, right).start()

                @pl.when(me > 0)
                def _():
                    block_copy(me, index, 1, left).start()

            @pl.when(within == per_group - 1)
            def _():
                group = index // per_group
                turned = own_facts[...].T
                facts[group, pl.ds(pl.multiple_of(me * 8, 8), 8), :] = turned[:8]
                for place in range(size):

                    @pl.when(place != me)
                    def _():
                        fact_copy(me, group, place).start()

    def relay_blocks(step):
        for near in range(1, size):
            for way, place in ((0, me - near), (1, me + near)):
                index = step - far(place) - near * pass_hop

                @pl.when((place >= 0) & (place < size) & inside(index))
                def _():
                    block_copy(place, index, way, other).wait_recv()
                    onward = (me < edge) if way == 0 else (me > 0)

                    @pl.when(onward)
                    def _():
                        block_copy(place, index, way, right if way == 0 else left).start()

    longest = (edge * hop + wait_hop if scatter is not None else 0) + edge * pass_hop

    def conclude(step):
        index = step - longest

        @pl.when(inside(index) & (lax.rem(index, per_group) == per_group - 1))
        def _():
            group = index // per_group
            for place in range(size):

                @pl.when(place != me)
                def _():
                    fact_copy(place, group, other).wait_recv()

            finish(group, group_rows(group), facts[group].T)

    barrier = pltpu.get_barrier_semaphore()
    for place in range(size):

        @pl.when(place != me)
        def _():
            pl.semaphore_signal(barrier, inc=1, device_id={"col": place}, device_id_type=MESH)

    line = lax.axis_index("row")
    for place in range(rows_too):

        @pl.when(place != line)
        def _():
            pl.semaphore_signal(barrier, inc=1, device_id={"row": place}, device_id_type=MESH)

    if scatter is not None:
        order = sorted(range(size), key=lambda shard: -max(shard, edge - shard))
        for shard in order:
            produce(group_rows(0), shard, True)
    pl.semaphore_wait(barrier, size - 1 + max(rows_too - 1, 0))

    def step_all(step, carry):
        if scatter is not None:
            relay_sums(step)
        ready(step)
        if gather:
            relay_blocks(step)
        conclude(step)
        if scatter is not None:
            following = step // per_group + 1
            for part in range(per_group):

                @pl.when((following < groups) & (lax.rem(step, per_group) == part))
                def _():
                    for shard in range(part * size // per_group, (part + 1) * size // per_group):
                        produce(group_rows(following), shard, False)

        if during is not None:

            @pl.when(inside(step))
            def _():
                during(rows(step))

        return carry

    lax.fori_loop(0, chunks + longest, step_all, 0)

    def drain(index, carry):
        if scatter is not None:
            for shard in range(size):

                @pl.when(shard != me)
                def _():
                    sum_copy(shard, shard, index, other).wait_send()

        if gather:
            for place in range(size):

                @pl.when((place <= me) & (me < edge))
                def _():
                    block_copy(place, index, 0, other).wait_send()

                @pl.when((place >= me) & (me > 0))
                def _():
                    block_copy(place, index, 1, other).wait_send()

        return carry

    lax.fori_loop(0, chunks, drain, 0)

    def drain_facts(group, carry):
        for place in range(size):

            @pl.when(place != me)
            def _():
                fact_copy(me, group, place).wait_send()

        return carry

    lax.fori_loop(0, groups, drain_facts, 0)


def exchange_scratch(size, tokens, width, chunk, scatter, gather):
    chunks = tokens // chunk
    groups = tokens // GROUP
    dma = pltpu.SemaphoreType.DMA
    tiny = (1, chunk, 128)
    return [
        pltpu.VMEM((size + 1, tokens, width) if scatter else tiny, jnp.bfloat16),
        pltpu.VMEM((size, tokens, width) if gather else tiny, jnp.bfloat16),
        pltpu.VMEM((groups, 128, 128), f32),
        pltpu.VMEM((GROUP, 128), f32),
        dma((size, chunks) if scatter else (1, 1)),
        dma((size + 1, chunks) if scatter else (1, 1)),
        dma((2, size, chunks) if gather else (1, 1, 1)),
        dma((size, chunks) if gather else (1, 1)),
        dma((size, groups)),
        dma((size, groups)),
    ]


def call(body, operands, places, outs, out_places, scratch, name, ident, cost=10**11):
    moved = sum(array.size * array.dtype.itemsize for array in list(operands) + outs)
    return pl.pallas_call(
        body,
        out_shape=outs,
        in_specs=[pl.BlockSpec(memory_space=place) for place in places],
        out_specs=[pl.BlockSpec(memory_space=place) for place in out_places],
        scratch_shapes=scratch,
        compiler_params=pltpu.CompilerParams(
            collective_id=ident, has_side_effects=True, vmem_limit_bytes=60 * 2**20
        ),
        cost_estimate=pl.CostEstimate(flops=cost, bytes_accessed=moved, transcendentals=0),
        name=name,
    )(*operands)


def held(*arrays):
    return [pltpu.VMEM(array.shape, array.dtype) for array in arrays]


def start_loads(pairs, sems):
    copies = [
        pltpu.make_async_copy(source, target, sems.at[place])
        for place, (source, target) in enumerate(pairs)
    ]
    for copy in copies:
        copy.start()
    return copies


def group_store(source, target, sems):
    groups = source.shape[0] // GROUP

    def copy(group):
        rows = pl.ds(pl.multiple_of(group * GROUP, GROUP), GROUP)
        return pltpu.make_async_copy(source.at[rows], target.at[rows], sems.at[group])

    def wait_all():
        def one(group, carry):
            copy(group).wait()
            return carry

        lax.fori_loop(0, groups, one, 0)

    return lambda group: copy(group).start(), wait_all


def norm_stats(value):
    mean = jnp.sum(value, -1, keepdims=True) * (1.0 / value.shape[-1])
    center = value - mean
    return mean, center, jnp.sum(center * center, -1, keepdims=True)


def norm_whole(size, width, turned):
    means = [turned[:, 8 * z : 8 * z + 1] for z in range(size)]
    squares = [turned[:, 8 * z + 1 : 8 * z + 2] for z in range(size)]
    mean = sum(means[1:], means[0]) * (1.0 / size)
    shifts = [own - mean for own in means]
    spread = sum(squares[1:], squares[0])
    for shift in shifts:
        spread = spread + width * shift * shift
    return shifts, lax.rsqrt(spread * (1.0 / (size * width)) + EPSILON)


def norm_finish(size, width, blocks, scale, whole, store):
    def finish(group, rows, turned):
        shifts, rate = norm_whole(size, width, turned)
        scale[rows, :] = rate
        for z in range(size):
            value = (blocks[z, rows].astype(f32) + shifts[z]) * rate
            whole[rows, z * width : (z + 1) * width] = value.astype(jnp.bfloat16)
        store(group)

    return finish


def mixings(mix):
    count = mix.shape[1]
    span = range(count)

    def dot(left, right):
        total = left[0] * right[0]
        for a, b in zip(left[1:], right[1:]):
            total = total + a * b
        return total

    across_one = [[mix[0, k, 1 + i] for i in span] for k in span]
    across_two = [[mix[1, i, 1 + j] for i in span] for j in span]
    through = [[dot(across_one[k], across_two[j]) for j in span] for k in span]
    second = [mix[1, i, 0] for i in span]
    outward = [mix[0, i, 1 + count] for i in span]
    in_two = [dot(across_one[k], second) for k in span]
    out_one = [dot(outward, across_two[j]) for j in span]
    return through, in_two, out_one, dot(outward, second)


def norm_in_kernel(
    size,
    chunk,
    hop,
    mix,
    streams,
    grads_in,
    gate_in,
    down_in,
    documents,
    rates,
    whole_out,
    scale,
    branch_grad,
    products,
    packed,
    column,
    cosine,
    sine,
    whole,
    grads,
    gate_up,
    down,
    loads,
    stores,
    *scratch,
):
    count, tokens, width = streams.shape
    kinds, _, hidden = gate_up.shape
    tile = min(512, hidden)
    tiles = hidden // tile
    into = [mix[0, k, 0] for k in range(count)]
    onto = [mix[1, k, 1 + count] for k in range(count)]
    products[...] = jnp.zeros_like(products)
    waits = start_loads(((grads_in, grads), (gate_in, gate_up), (down_in, down)), loads)
    store, wait_stores = group_store(whole, whole_out, stores)

    def prepare(rows, total):
        mixed = into[0] * streams[0, rows].astype(f32)
        for k in range(1, count):
            mixed = mixed + into[k] * streams[k, rows].astype(f32)
        mean, center, square = norm_stats(mixed)
        return (mean, square), center.astype(jnp.bfloat16)

    def during(rows):
        @pl.when(rows.start == 0)
        def _():
            for wait in waits:
                wait.wait()

        own_docs = documents[:, pl.ds(pl.multiple_of(rows.start // GROUP * GROUP, GROUP), GROUP)]
        turned = jnp.broadcast_to(own_docs.astype(f32), (GROUP, GROUP)).T

        @pl.when(lax.rem(rows.start, GROUP) == 0)
        def _():
            group = pl.ds(pl.multiple_of(rows.start, GROUP), GROUP)
            docs = turned[:, :1]
            shape = (GROUP, tokens)
            index = lax.broadcasted_iota(jnp.int32, shape, 0) + rows.start
            before = lax.broadcasted_iota(jnp.int32, shape, 1) < index
            same = (docs == documents[...].astype(f32)) & before
            place = jnp.sum(jnp.where(same, 1.0, 0.0), -1, keepdims=True)
            angle = place * rates[...]
            column[group, :] = docs
            cosine[group, :] = jnp.cos(angle)
            sine[group, :] = jnp.sin(angle)

        for piece in range((kinds + 1) * tiles):

            @pl.when(rows.start == piece * chunk)
            def _():
                kind, start = piece // tiles, piece % tiles * tile
                if kind < kinds:
                    value = gate_up[kind, :, start : start + tile]
                else:
                    value = down[start : start + tile, :].T
                packed[:, piece * tile : (piece + 1) * tile] = value.astype(jnp.bfloat16)

        above = [grads[k, rows].astype(f32) for k in range(count)]
        value = onto[0] * above[0]
        for k in range(1, count):
            value = value + onto[k] * above[k]
        branch_grad[rows, :] = value.astype(jnp.bfloat16)
        for i in range(count):
            own = streams[i, rows].astype(f32)
            for k in range(count):
                place = i * count + k
                products[place] = products[place] + tile_sum(own * above[k])

    finish = norm_finish(size, width, scratch[1], scale, whole, store)
    line_exchange(
        size, tokens, width, chunk, hop, None, True, None, prepare, finish, scratch, during
    )
    wait_stores()


def norm_in(size, streams, grads, gate_up, down, documents, mix, chunk=64, hop=(1, 0, 1)):
    _, tokens, width = streams.shape
    whole = jax.ShapeDtypeStruct((tokens, size * width), jnp.bfloat16)
    half = HEAD_DIM // 2
    rates = 10000.0 ** (-2.0 * jnp.arange(half).astype(f32) / HEAD_DIM)
    return call(
        functools.partial(norm_in_kernel, size, chunk, hop),
        (mix, streams, grads, gate_up, down, documents, rates[None]),
        (SM, VM, pl.ANY, pl.ANY, pl.ANY, VM, VM),
        [
            whole,
            jax.ShapeDtypeStruct((tokens, 1), f32),
            jax.ShapeDtypeStruct((tokens, width), jnp.bfloat16),
            jax.ShapeDtypeStruct((streams.shape[0] * grads.shape[0], 8, 128), f32),
            jax.ShapeDtypeStruct(
                (gate_up.shape[1], (gate_up.shape[0] + 1) * gate_up.shape[2]), jnp.bfloat16
            ),
            jax.ShapeDtypeStruct((tokens, 1), f32),
            jax.ShapeDtypeStruct((tokens, half), f32),
            jax.ShapeDtypeStruct((tokens, half), f32),
        ],
        (pl.ANY,) + (VM,) * 7,
        held(whole, grads, gate_up, down)
        + [pltpu.SemaphoreType.DMA((3,)), pltpu.SemaphoreType.DMA((tokens // GROUP,))]
        + exchange_scratch(size, tokens, width, chunk, False, True),
        "norm_in",
        1,
    )


def norm_mid_kernel(
    size,
    chunk,
    hop,
    mix,
    attended_in,
    rows_in,
    streams_in,
    whole_out,
    scale,
    branch,
    attended,
    weights,
    streams,
    scatter,
    whole,
    loads,
    stores,
    *scratch,
):
    count, tokens, width = streams.shape
    in_two, turn = mixings(mix)[1::2]
    heads = attended.shape[1]
    own_columns = rows_in.at[:, pl.ds(rows_in.shape[1] - heads, heads)]
    waits = start_loads(
        ((attended_in, attended), (own_columns, weights), (streams_in, streams)), loads
    )
    store, wait_stores = group_store(whole, whole_out, stores)
    waits[0].wait()
    waits[1].wait()

    def produce(rows, shard, first):
        columns = slice(shard * width, (shard + 1) * width)
        scatter[rows, columns] = lax.dot_general(
            attended[rows, :], weights[columns, :], LANES, preferred_element_type=f32
        ).astype(jnp.bfloat16)
        if first and shard == size // 2:
            waits[2].wait()

    def prepare(rows, total):
        branch[rows, :] = total
        mixed = turn * total
        for k in range(count):
            mixed = mixed + in_two[k] * streams[k, rows].astype(f32)
        mean, center, square = norm_stats(mixed)
        return (mean, square), center.astype(jnp.bfloat16)

    finish = norm_finish(size, width, scratch[1], scale, whole, store)
    line_exchange(size, tokens, width, chunk, hop, scatter, True, produce, prepare, finish, scratch)
    wait_stores()


def norm_mid(size, attended, rows, streams, mix, chunk=64, hop=(1, 0, 1)):
    _, tokens, width = streams.shape
    weights = jax.ShapeDtypeStruct((size * width, attended.shape[1]), jnp.bfloat16)
    whole = jax.ShapeDtypeStruct((tokens, size * width), jnp.bfloat16)
    return call(
        functools.partial(norm_mid_kernel, size, chunk, hop),
        (mix, attended, rows, streams),
        (SM, pl.ANY, pl.ANY, pl.ANY),
        [
            whole,
            jax.ShapeDtypeStruct((tokens, 1), f32),
            jax.ShapeDtypeStruct((tokens, width), f32),
        ],
        (pl.ANY, VM, VM),
        held(attended, weights, streams, whole, whole)
        + [pltpu.SemaphoreType.DMA((3,)), pltpu.SemaphoreType.DMA((tokens // GROUP,))]
        + exchange_scratch(size, tokens, width, chunk, True, True),
        "norm_mid",
        2,
    )


def back_mid_kernel(
    size,
    chunk,
    hop,
    mix,
    gated_in,
    rows_in,
    grads_in,
    normal_in,
    scale,
    output_in,
    whole_out,
    inner_out,
    grad_attended,
    gated,
    weights,
    grads,
    whole_normal,
    output_rows,
    scatter,
    inner,
    whole,
    loads,
    stores,
    inner_stores,
    *scratch,
):
    count, tokens, width = grads.shape
    out_one, turn = mixings(mix)[2:]
    blocks = scratch[1]
    hidden = gated.shape[2]
    heads = output_rows.shape[1]
    me = lax.axis_index("col")
    edge = size - 1
    order = sorted(range(size), key=lambda shard: -max(shard, edge - shard))
    pairs = [(gated_in.at[:, pl.ds(0, GROUP)], gated.at[:, pl.ds(0, GROUP)])]
    for shard in order:
        shard_rows = pl.ds(shard * width, width)
        pairs.append((rows_in.at[shard_rows, pl.ds(0, 2 * hidden)], weights.at[shard_rows]))
    rest = pl.ds(GROUP, tokens - GROUP)
    pairs = pairs + [
        (gated_in.at[:, rest], gated.at[:, rest]),
        (grads_in, grads),
        (normal_in, whole_normal),
        (output_in.at[:, pl.ds(output_in.shape[1] - heads, heads)], output_rows),
    ]
    waits = start_loads(pairs, loads)
    store, wait_stores = group_store(whole, whole_out, stores)
    store_inner, wait_inner = group_store(inner, inner_out, inner_stores)
    waits[0].wait()

    def produce(rows, shard, first):
        if first:
            waits[1 + order.index(shard)].wait()
        shard_rows = slice(shard * width, (shard + 1) * width)
        total = lax.dot_general(
            gated[0, rows], weights[shard_rows, :hidden], LANES, preferred_element_type=f32
        )
        total = total + lax.dot_general(
            gated[1, rows], weights[shard_rows, hidden:], LANES, preferred_element_type=f32
        )
        scatter[rows, shard_rows] = total.astype(jnp.bfloat16)
        if first and shard == order[-1]:
            for wait in waits[1 + size :]:
                wait.wait()

    def own_normal(rows):
        return whole_normal[rows, pl.ds(pl.multiple_of(me * width, width), width)].astype(f32)

    def prepare(rows, total):
        inner[rows, :] = total
        normal = own_normal(rows)
        part = 1.0 / width
        first = jnp.sum(total, -1, keepdims=True)
        second = jnp.sum(total * normal, -1, keepdims=True)
        plain = jnp.sum(normal, -1, keepdims=True)
        square = jnp.sum(normal * normal, -1, keepdims=True)
        spread = square - plain * plain * part
        cross = second - first * plain * part
        slope = jnp.where(spread > 1e-3, cross / jnp.maximum(spread, 1e-3), 0.0)
        level = (first - slope * plain) * part
        known = out_one[0] * grads[0, rows].astype(f32)
        for k in range(1, count):
            known = known + out_one[k] * grads[k, rows].astype(f32)
        block = known + (turn * scale[rows, :]) * (total - level - slope * normal)
        return (first, second, level, slope), block.astype(jnp.bfloat16)

    def finish(group, rows, turned):
        first, second = whole_sums(size, width, turned)
        rate = scale[rows, :]
        gain = turn * rate
        for z in range(size):
            level = gain * (turned[:, 8 * z + 2 : 8 * z + 3] - first)
            slope = gain * (turned[:, 8 * z + 3 : 8 * z + 4] - second)
            columns = slice(z * width, (z + 1) * width)
            value = blocks[z, rows].astype(f32) + level
            value = value + slope * whole_normal[rows, columns].astype(f32)
            whole[rows, columns] = value.astype(jnp.bfloat16)
        store(group)
        grad_attended[rows, :] = jnp.dot(
            whole[rows, :], output_rows[...], preferred_element_type=f32
        ).astype(jnp.bfloat16)
        inner[rows, :] = rate * (inner[rows, :] - first - second * own_normal(rows))
        store_inner(group)

    line_exchange(size, tokens, width, chunk, hop, scatter, True, produce, prepare, finish, scratch)
    wait_stores()
    wait_inner()


def whole_sums(size, width, turned):
    first = turned[:, 0:1]
    second = turned[:, 1:2]
    for z in range(1, size):
        first = first + turned[:, 8 * z : 8 * z + 1]
        second = second + turned[:, 8 * z + 1 : 8 * z + 2]
    return first * (1.0 / (size * width)), second * (1.0 / (size * width))


def back_mid(
    size, gated, rows, grads, whole_normal, scale, output_rows, mix, chunk=64, hop=(1, 0, 1)
):
    _, tokens, width = grads.shape
    whole = jax.ShapeDtypeStruct((tokens, size * width), jnp.bfloat16)
    inner = jax.ShapeDtypeStruct((tokens, width), f32)
    groups = tokens // GROUP
    weights = jax.ShapeDtypeStruct((size * width, 2 * gated.shape[2]), jnp.bfloat16)
    heads = output_rows.shape[1] // 4
    output_own = jax.ShapeDtypeStruct((size * width, heads), jnp.bfloat16)
    return call(
        functools.partial(back_mid_kernel, size, chunk, hop),
        (mix, gated, rows, grads, whole_normal, scale, output_rows),
        (SM,) + (pl.ANY,) * 4 + (VM, pl.ANY),
        [whole, inner, jax.ShapeDtypeStruct((tokens, heads), jnp.bfloat16)],
        (pl.ANY, pl.ANY, VM),
        held(gated, weights, grads, whole_normal, output_own, whole, inner, whole)
        + [
            pltpu.SemaphoreType.DMA((size + 5,)),
            pltpu.SemaphoreType.DMA((groups,)),
            pltpu.SemaphoreType.DMA((groups,)),
        ]
        + exchange_scratch(size, tokens, width, chunk, True, True),
        "back_mid",
        3,
        10**9,
    )


def tile_sum(product):
    height, width = product.shape
    folded = jnp.sum(product.reshape(height // 8, 8, width), 0)
    total = folded[:, :128]
    for start in range(128, width, 128):
        total = total + folded[:, start : start + 128]
    return total


def back_sums_kernel(
    size, partial_in, normal_in, first_sum, second_sum, partial, normal, facts, loads, sent, got
):
    tokens, features = partial.shape
    groups = tokens // GROUP
    me = lax.axis_index("col")

    def rows_of(group):
        return pl.ds(pl.multiple_of(group * GROUP, GROUP), GROUP)

    def load(way, group):
        source, target = ((partial_in, partial), (normal_in, normal))[way]
        rows = rows_of(group)
        return pltpu.make_async_copy(source.at[rows], target.at[rows], loads.at[way, group])

    def start_load(group, carry):
        load(0, group).start()
        load(1, group).start()
        return carry

    lax.fori_loop(0, groups, start_load, 0)
    barrier = pltpu.get_barrier_semaphore()
    for member in range(size):

        @pl.when(member != me)
        def _():
            pl.semaphore_signal(barrier, inc=1, device_id={"col": member}, device_id_type=MESH)

    def own(group, carry):
        load(0, group).wait()
        load(1, group).wait()
        rows = rows_of(group)
        total = partial[rows, :].astype(f32)
        one = jnp.sum(total, -1, keepdims=True)
        two = jnp.sum(total * normal[rows, :].astype(f32), -1, keepdims=True)
        lane = lax.broadcasted_iota(jnp.int32, (GROUP, 128), 1)
        packed = jnp.where(lane == 0, one, jnp.where(lane == 1, two, 0.0))
        facts[me, pl.ds(pl.multiple_of(group * 8, 8), 8)] = packed.T[:8]
        return carry

    lax.fori_loop(0, groups, own, 0)
    pl.semaphore_wait(barrier, size - 1)

    def fact_copy(place, member):
        return pltpu.make_async_remote_copy(
            src_ref=facts.at[place],
            dst_ref=facts.at[place],
            send_sem=sent.at[member],
            recv_sem=got.at[place],
            device_id={"col": member},
            device_id_type=MESH,
        )

    for member in range(size):

        @pl.when(member != me)
        def _():
            fact_copy(me, member).start()

    for member in range(size):

        @pl.when(member != me)
        def _():
            fact_copy(member, member).wait()

    def conclude(group, carry):
        fact_rows = pl.ds(pl.multiple_of(group * 8, 8), 8)
        total = facts[0, fact_rows]
        for place in range(1, size):
            total = total + facts[place, fact_rows]
        total = total * (1.0 / features)
        turned = jnp.concatenate([total, jnp.zeros((GROUP - 8, 128), f32)], 0).T
        first_sum[rows_of(group), :] = turned[:, :1]
        second_sum[rows_of(group), :] = turned[:, 1:2]
        return carry

    lax.fori_loop(0, groups, conclude, 0)


def back_sums(size, partial, normal):
    tokens = partial.shape[0]
    dma = pltpu.SemaphoreType.DMA
    return call(
        functools.partial(back_sums_kernel, size),
        (partial, normal),
        (pl.ANY, pl.ANY),
        [jax.ShapeDtypeStruct((tokens, 1), f32)] * 2,
        (VM, VM),
        held(partial, normal)
        + [
            pltpu.VMEM((size, tokens // GROUP * 8, 128), f32),
            dma((2, tokens // GROUP)),
            dma((size,)),
            dma((size,)),
        ],
        "back_sums",
        6,
        10**9,
    )


def back_in_kernel(
    place,
    mix,
    share,
    first,
    last,
    normal,
    scale,
    first_sum,
    second_sum,
    streams,
    grads,
    inner_two,
    out,
    products,
):
    count = streams.shape[0]
    through, in_two, _, _ = mixings(mix)

    @pl.when(pl.program_id(0) == 0)
    def _():
        products[...] = jnp.zeros_like(products)

    width = share.shape[1]

    def slab(index, sums):
        rows = pl.ds(pl.multiple_of(index * 16, 16), 16)
        sums = list(sums)
        shape = (16, 128)
        rate = jnp.broadcast_to(scale[rows, :], shape)
        one = jnp.broadcast_to(first_sum[rows, :], shape)
        two = jnp.broadcast_to(second_sum[rows, :], shape)
        for start in range(0, width, 128):
            columns = slice(start, start + 128)
            total = share[rows, columns].astype(f32) + first[rows, columns].astype(f32)
            total = total + last[rows, columns].astype(f32)
            own = rate * (total - one - two * normal[rows, columns].astype(f32))
            below = inner_two[rows, columns]
            above = [grads[k, rows, columns].astype(f32) for k in range(count)]
            for i in range(count):
                value = in_two[i] * below + mix[0, i, 0] * own
                for k in range(count):
                    value = value + through[i][k] * above[k]
                out[i, rows, columns] = value
                product = streams[i, rows, columns].astype(f32) * own
                sums[i] = sums[i] + product[:8] + product[8:]
        return tuple(sums)

    sums = lax.fori_loop(0, share.shape[0] // 16, slab, (jnp.zeros((8, 128), f32),) * count)
    for i in range(count):
        products[i] = products[i] + sums[i]


def back_in(mix, partial, first, last, normal, scale, sums, streams, grads, inner_two, tile=256):
    count, tokens, width = streams.shape
    used = -(-count // 8) * 8
    many = pl.BlockSpec((count, tile, width), lambda i, place: (0, i, 0))
    here = pl.BlockSpec((tile, width), lambda i, place: (i, place[0]))
    own = pl.BlockSpec((tile, width), lambda i, place: (i, 0))
    thin = pl.BlockSpec((tile, 1), lambda i, place: (i, 0))
    return pl.pallas_call(
        back_in_kernel,
        grid_spec=pltpu.PrefetchScalarGridSpec(
            num_scalar_prefetch=1,
            grid=(tokens // tile,),
            in_specs=[pl.BlockSpec(memory_space=SM), here, own, own, here, thin, thin, thin]
            + [many, many, own],
            out_specs=[many, pl.BlockSpec((used, 8, 128), lambda i, place: (0, 0, 0))],
        ),
        out_shape=[
            jax.ShapeDtypeStruct(streams.shape, f32),
            jax.ShapeDtypeStruct((used, 8, 128), f32),
        ],
        compiler_params=pltpu.CompilerParams(vmem_limit_bytes=60 * 2**20),
        cost_estimate=pl.CostEstimate(
            flops=20 * streams.size, bytes_accessed=11 * streams.size, transcendentals=0
        ),
        name="back_in",
    )(
        lax.axis_index("col").astype(jnp.int32)[None],
        mix,
        partial,
        first,
        last,
        normal,
        scale,
        *sums,
        streams,
        grads,
        inner_two,
    )


def sum_all_kernel(size, *refs):
    parts, whole, shares, sent, got = refs[:-4], refs[-4], refs[-3], refs[-2], refs[-1]
    count_rows = lax.axis_size("row")
    barrier = pltpu.get_barrier_semaphore()
    for axis, members in (("col", size), ("row", count_rows)):
        for member in range(members):

            @pl.when(member != lax.axis_index(axis))
            def _():
                pl.semaphore_signal(
                    barrier, inc=1, device_id={axis: member}, device_id_type=MESH
                )

    total = jnp.concatenate([jnp.sum(jnp.sum(part[...], 1), -1, keepdims=True) for part in parts], 0)
    total = jnp.concatenate([total, jnp.zeros((128 - total.shape[0], 1), f32)], 0)
    total = jnp.broadcast_to(total, (128, 128)).T[:8]
    pl.semaphore_wait(barrier, size - 1 + count_rows - 1)
    for axis, members, base in (("col", size, 0), ("row", count_rows, size)):
        here = lax.axis_index(axis)

        def share_copy(source, member):
            return pltpu.make_async_remote_copy(
                src_ref=shares.at[base + source],
                dst_ref=shares.at[base + source],
                send_sem=sent.at[base + member],
                recv_sem=got.at[base + source],
                device_id={axis: member},
                device_id_type=MESH,
            )

        shares[base + here] = total
        for member in range(members):

            @pl.when(member != here)
            def _():
                share_copy(here, member).start()

        for member in range(members):

            @pl.when(member != here)
            def _():
                share_copy(member, member).wait()

        total = shares[base]
        for member in range(1, members):
            total = total + shares[base + member]
    whole[...] = total


def sum_all(size, *parts):
    members = size + lax.axis_size("row")
    return call(
        functools.partial(sum_all_kernel, size),
        parts,
        (VM,) * len(parts),
        [jax.ShapeDtypeStruct((8, 128), f32)],
        (VM,),
        [
            pltpu.VMEM((members, 8, 128), f32),
            pltpu.SemaphoreType.DMA((members,)),
            pltpu.SemaphoreType.DMA((members,)),
        ],
        "sum_all",
        4,
        10**9,
    )[0]


def end_kernel(mix, streams, grads, branch_one, branch_two, inner_two, final, products):
    count, tokens, width = streams.shape
    through, _, out_one, _ = mixings(mix)
    out_two = [mix[1, j, 1 + count] for j in range(count)]

    @pl.when(pl.program_id(0) == 0)
    def _():
        products[...] = jnp.zeros_like(products)

    def slab(index, sums):
        rows = pl.ds(pl.multiple_of(index * 16, 16), 16)
        sums = list(sums)
        for start in range(0, width, 128):
            columns = slice(start, start + 128)
            values = [streams[i, rows, columns].astype(f32) for i in range(count)]
            above = [grads[i, rows, columns].astype(f32) for i in range(count)]
            one = branch_one[rows, columns]
            two = branch_two[rows, columns].astype(f32)
            below = inner_two[rows, columns]
            for j in range(count):
                value = out_one[j] * one + out_two[j] * two
                for k in range(count):
                    value = value + through[k][j] * values[k]
                final[j, rows, columns] = value.astype(jnp.bfloat16)
            pairs = [(a, below) for a in values]
            pairs = pairs + [(one, b) for b in above]
            pairs = pairs + [(a, two) for a in above]
            pairs = pairs + [(one, below)]
            for place, (a, b) in enumerate(pairs):
                product = a * b
                sums[place] = sums[place] + product[:8] + product[8:]
        return tuple(sums)

    used = 3 * count + 1
    sums = lax.fori_loop(0, tokens // 16, slab, (jnp.zeros((8, 128), f32),) * used)
    for place in range(used):
        products[place] = products[place] + sums[place]


def end_streams(mix, streams, grads, branch_one, branch_two, inner_two, tile=256):
    count, tokens, width = streams.shape
    used = -(-(3 * count + 1) // 8) * 8
    many = pl.BlockSpec((count, tile, width), lambda i: (0, i, 0))
    own = pl.BlockSpec((tile, width), lambda i: (i, 0))
    return pl.pallas_call(
        end_kernel,
        grid=(tokens // tile,),
        out_shape=[
            jax.ShapeDtypeStruct(streams.shape, jnp.bfloat16),
            jax.ShapeDtypeStruct((used, 8, 128), f32),
        ],
        in_specs=[pl.BlockSpec(memory_space=SM), many, many, own, own, own],
        out_specs=[many, pl.BlockSpec((used, 8, 128), lambda i: (0, 0, 0))],
        compiler_params=pltpu.CompilerParams(vmem_limit_bytes=60 * 2**20),
        cost_estimate=pl.CostEstimate(
            flops=60 * streams.size, bytes_accessed=9 * streams.size, transcendentals=0
        ),
        name="end_streams",
    )(mix, streams, grads, branch_one, branch_two, inner_two)


def tiled(body, grid, operands, specs, outs, out_specs, scratch, flops, name):
    moved = sum(array.size * array.dtype.itemsize for array in list(operands) + (list(outs) if isinstance(outs, list) else [outs]))
    return pl.pallas_call(
        body,
        grid=grid,
        out_shape=outs,
        in_specs=specs,
        out_specs=out_specs,
        scratch_shapes=scratch,
        compiler_params=pltpu.CompilerParams(vmem_limit_bytes=60 * 2**20),
        cost_estimate=pl.CostEstimate(flops=flops, bytes_accessed=moved, transcendentals=0),
        name=name,
    )(*operands)


def gate_kernel(
    size,
    steps,
    chunks,
    whole,
    gate_rows,
    upper_rows,
    down_rows,
    own_in,
    before_in,
    after_in,
    active_out,
    by_gate,
    by_upper,
    partial,
    gathered,
    active,
    blocks,
    loads,
    stores,
    sent,
    got,
):
    step = pl.program_id(0)
    me = lax.axis_index("col")
    tiles, tile = active.shape[1] // gate_rows.shape[1], gate_rows.shape[1]
    tokens, width = blocks.shape[1:]
    chunk = tokens // chunks
    edge = size - 1
    right, left = jnp.minimum(me + 1, edge), jnp.maximum(me - 1, 0)
    other = jnp.where(me == edge, left, right)

    def load(place, way):
        source = (own_in, before_in, after_in)[way]
        return pltpu.make_async_copy(source, blocks.at[place], loads.at[way])

    def store(place):
        return pltpu.make_async_copy(
            blocks.at[place],
            gathered.at[:, pl.ds(pl.multiple_of(place * width, width), width)],
            stores.at[place],
        )

    def send(place, index, way, device):
        rows = pl.ds(pl.multiple_of(index * chunk, chunk), chunk)
        return pltpu.make_async_remote_copy(
            src_ref=blocks.at[place, rows],
            dst_ref=blocks.at[place, rows],
            send_sem=sent.at[way, place, index],
            recv_sem=got.at[place, index],
            device_id={"col": device},
            device_id_type=MESH,
        )

    def both_ways(near, act):
        for way, place, target, onward in (
            (0, me - near, right, me < edge),
            (1, me + near, left, me > 0),
        ):

            @pl.when((place >= 0) & (place < size))
            def _():
                act(way, place, target, onward)

    @pl.when(step == 0)
    def _():
        load(me, 0).start()
        both_ways(1, lambda way, place, target, onward: load(place, 1 + way).start())
        barrier = pltpu.get_barrier_semaphore()
        both_ways(
            1,
            lambda way, place, target, onward: pl.semaphore_signal(
                barrier, inc=1, device_id={"col": place}, device_id_type=MESH
            ),
        )
        load(me, 0).wait()
        store(me).start()
        both_ways(1, lambda way, place, target, onward: load(place, 1 + way).wait())

        @pl.when((me > 0) & (me < edge))
        def _():
            pl.semaphore_wait(barrier, 2)

        @pl.when((me == 0) | (me == edge))
        def _():
            pl.semaphore_wait(barrier, 1)


        def begin(way, place, target, onward):
            store(place).start()

            @pl.when(onward)
            def _():
                for index in range(chunks):
                    send(place, index, way, target).start()

        both_ways(1, begin)

    for near in range(2, size - 1):
        index = step - (steps - chunks - (size - 2 - near))

        def forward(way, place, target, onward):
            send(place, index, way, other).wait_recv()

            @pl.when(onward)
            def _():
                send(place, index, way, target).start()

        @pl.when((index >= 0) & (index < chunks))
        def _():
            both_ways(near, forward)

    @pl.when(step < tiles)
    def _():
        gate = jnp.dot(whole[...], gate_rows[...], preferred_element_type=f32)
        upper = jnp.dot(whole[...], upper_rows[...], preferred_element_type=f32)
        sigma = jax.nn.sigmoid(gate)
        silu = gate * sigma
        value = (silu * upper).astype(jnp.bfloat16)
        active_out[...] = value
        active[:, pl.ds(pl.multiple_of(step * tile, tile), tile)] = value
        by_gate[...] = (upper * sigma * (1.0 + gate * (1.0 - sigma))).astype(jnp.bfloat16)
        by_upper[...] = silu.astype(jnp.bfloat16)

    @pl.when(step >= tiles)
    def _():
        partial[...] = lax.dot_general(
            active[...], down_rows[...], LANES, preferred_element_type=f32
        ).astype(jnp.bfloat16)

    @pl.when(step == steps - 1)
    def _():
        def last(way, place, target, onward):
            for index in range(chunks):
                send(place, index, way, other).wait_recv()

        both_ways(size - 1, last)
        for near in range(2, size):
            both_ways(near, lambda way, place, target, onward: store(place).start())

        def sends_done(way, place, target, onward):
            @pl.when(onward)
            def _():
                for index in range(chunks):
                    send(place, index, way, other).wait_send()

        for near in range(1, size - 1):
            both_ways(near, sends_done)
        for place in range(size):
            store(place).wait()


def gate_forward(size, whole, weights, own, before, after, tile=256):
    tokens, features = whole.shape
    hidden = weights.shape[1] // 3
    tile = min(tile, hidden)
    tiles = hidden // tile
    down_tile = min(512, features)
    steps = tiles + features // down_tile
    chunks = 1
    while 2 * chunks <= min(8, steps - size + 3):
        chunks = 2 * chunks
    wide = pl.BlockSpec((tokens, tile), lambda j: (0, jnp.minimum(j, tiles - 1)))
    plain = pl.BlockSpec(memory_space=pl.ANY)
    dma = pltpu.SemaphoreType.DMA
    wide_shape = jax.ShapeDtypeStruct((tokens, hidden), jnp.bfloat16)
    return pl.pallas_call(
        functools.partial(gate_kernel, size, steps, chunks),
        grid=(steps,),
        out_shape=[wide_shape] * 3 + [jax.ShapeDtypeStruct((tokens, features), jnp.bfloat16)] * 2,
        in_specs=[
            pl.BlockSpec((tokens, features), lambda j: (0, 0)),
            pl.BlockSpec((features, tile), lambda j: (0, jnp.minimum(j, tiles - 1))),
            pl.BlockSpec((features, tile), lambda j: (0, tiles + jnp.minimum(j, tiles - 1))),
            pl.BlockSpec((down_tile, hidden), lambda j: (jnp.maximum(j - tiles, 0), 2)),
            plain,
            plain,
            plain,
        ],
        out_specs=[wide] * 3
        + [pl.BlockSpec((tokens, down_tile), lambda j: (0, jnp.maximum(j - tiles, 0))), plain],
        scratch_shapes=[
            pltpu.VMEM((tokens, hidden), jnp.bfloat16),
            pltpu.VMEM((size, tokens, own.shape[1]), jnp.bfloat16),
            dma((3,)),
            dma((size,)),
            dma((2, size, chunks)),
            dma((size, chunks)),
        ],
        compiler_params=pltpu.CompilerParams(
            collective_id=5, has_side_effects=True, vmem_limit_bytes=60 * 2**20
        ),
        cost_estimate=pl.CostEstimate(
            flops=6 * tokens * features * hidden,
            bytes_accessed=2 * weights.size,
            transcendentals=0,
        ),
        name="gate_forward",
    )(whole, weights, weights, weights, own, before, after)


def gate_back_kernel(
    branch_grad, normal, rows, by_gate, by_upper, active, grads, weight_grads, turned_grad, turned
):
    @pl.when(pl.program_id(0) == 0)
    def _():
        turned[...] = normal[...].T
        turned_grad[...] = branch_grad[...].T

    grad = jnp.dot(branch_grad[...], rows[...], preferred_element_type=f32)
    grads[0] = (grad * by_gate[...].astype(f32)).astype(jnp.bfloat16)
    grads[1] = (grad * by_upper[...].astype(f32)).astype(jnp.bfloat16)
    pairs = ((turned, grads.at[0]), (turned, grads.at[1]), (turned_grad, active))
    for place, (left, right) in enumerate(pairs):
        weight_grads[place] = jnp.dot(
            left[...], right[...], preferred_element_type=f32
        ).astype(jnp.bfloat16)


def gate_back(branch_grad, normal, weights, by_gate, by_upper, active, tile=256):
    tokens, features = normal.shape
    hidden = weights.shape[1] // 3
    tile = min(tile, hidden)
    tiles = hidden // tile
    whole = pl.BlockSpec(
        (tokens, features), lambda j: (0, 0), pipeline_mode=pl.Buffered(buffer_count=1)
    )
    part = pl.BlockSpec((tokens, tile), lambda j: (0, j))
    return tiled(
        gate_back_kernel,
        (tiles,),
        (branch_grad, normal, weights, by_gate, by_upper, active),
        [
            whole,
            whole,
            pl.BlockSpec((features, tile), lambda j: (0, 2 * tiles + j)),
            part,
            part,
            part,
        ],
        [
            jax.ShapeDtypeStruct((2, tokens, hidden), jnp.bfloat16),
            jax.ShapeDtypeStruct((3, features, hidden), jnp.bfloat16),
        ],
        [
            pl.BlockSpec((2, tokens, tile), lambda j: (0, 0, j)),
            pl.BlockSpec((3, features, tile), lambda j: (0, 0, j)),
        ],
        [pltpu.VMEM((features, tokens), jnp.bfloat16)] * 2,
        8 * tokens * features * hidden,
        "gate_back",
    )


def outer_kernel(cut, left, right, other_left, other_right, out, turned):
    step = pl.program_id(0)

    @pl.when(step == 0)
    def _():
        turned[...] = left[...].T

    @pl.when(step == cut)
    def _():
        turned[...] = other_left[...].T

    @pl.when(step < cut)
    def _():
        out[...] = jnp.dot(turned[...], right[...], preferred_element_type=f32).astype(jnp.bfloat16)

    @pl.when(step >= cut)
    def _():
        out[...] = jnp.dot(turned[...], other_right[...], preferred_element_type=f32).astype(
            jnp.bfloat16
        )


def outer(left, right, other_left, other_right, tile=512, name="outer"):
    tokens, rows = left.shape
    tile = min(tile, other_right.shape[1])
    other = other_right.shape[1] // tile
    if right.ndim == 3:
        tiles = right.shape[2] // tile
        cut = right.shape[0] * tiles
        clip = lambda j: jnp.minimum(j, cut - 1)
        spec = pl.BlockSpec((None, tokens, tile), lambda j: (clip(j) // tiles, 0, clip(j) % tiles))
    else:
        cut = right.shape[1] // tile
        spec = pl.BlockSpec((tokens, tile), lambda j: (0, jnp.minimum(j, cut - 1)))
    whole = pl.BlockSpec((tokens, rows), lambda j: (0, 0))
    return tiled(
        functools.partial(outer_kernel, cut),
        (cut + other,),
        (left, right, other_left, other_right),
        [whole, spec, whole, pl.BlockSpec((tokens, tile), lambda j: (0, jnp.maximum(j - cut, 0)))],
        jax.ShapeDtypeStruct((rows, (cut + other) * tile), jnp.bfloat16),
        pl.BlockSpec((rows, tile), lambda j: (0, j)),
        [pltpu.VMEM((rows, tokens), jnp.bfloat16)],
        2 * tokens * rows * (cut + other) * tile,
        name,
    )


def product_kernel(dims, left, right, out):
    total = lax.dot_general(left[...], right[...], dims, preferred_element_type=f32)
    out[...] = total.astype(out.dtype)


def product(left, right, start, columns, kind=jnp.bfloat16, tile=512, name="product"):
    tokens, depth = left.shape
    tile = min(tile, columns)
    first = start // tile
    return tiled(
        functools.partial(product_kernel, (((1,), (0,)), ((), ()))),
        (columns // tile,),
        (left, right),
        [
            pl.BlockSpec((tokens, depth), lambda j: (0, 0)),
            pl.BlockSpec((depth, tile), lambda j: (0, first + j)),
        ],
        jax.ShapeDtypeStruct((tokens, columns), kind),
        pl.BlockSpec((tokens, tile), lambda j: (0, j)),
        [],
        2 * tokens * depth * columns,
        name,
    )


def heads_kernel(ends, grads, rows, *refs):
    width = grads.shape[2]
    total = 0.0
    for k in range(grads.shape[0]):
        total = total + lax.dot_general(
            grads[k], rows[:, k * width : (k + 1) * width], LANES, preferred_element_type=f32
        )
    total = total.astype(jnp.bfloat16)
    if ends:
        out, low, high = refs

        @pl.when(pl.program_id(0) == 0)
        def _():
            low[...] = total

        @pl.when(pl.program_id(0) == 1)
        def _():
            high[...] = total

    else:
        out = refs[1]
    out[...] = total


def heads_product(size, grads, weights, begun=None):
    count, tokens, width = grads.shape
    rows = weights.shape[0]
    tile = rows // size
    ends = begun is None
    place = (lambda j: j * (size - 1)) if ends else (lambda j: j + 1)
    whole = jax.ShapeDtypeStruct((tokens, rows), jnp.bfloat16)
    one = jax.ShapeDtypeStruct((tokens, tile), jnp.bfloat16)
    own = pl.BlockSpec((tokens, tile), lambda j: (0, 0))
    steps = 2 if ends else size - 2
    return pl.pallas_call(
        functools.partial(heads_kernel, ends),
        grid=(steps,),
        out_shape=[whole, one, one] if ends else whole,
        in_specs=[
            pl.BlockSpec((count, tokens, width), lambda j: (0, 0, 0)),
            pl.BlockSpec((tile, count * width), lambda j: (place(j), 0)),
        ]
        + ([] if ends else [pl.BlockSpec(memory_space=pl.ANY)]),
        out_specs=[pl.BlockSpec((tokens, tile), lambda j: (0, place(j))), own, own]
        if ends
        else pl.BlockSpec((tokens, tile), lambda j: (0, place(j))),
        input_output_aliases={} if ends else {2: 0},
        compiler_params=pltpu.CompilerParams(vmem_limit_bytes=60 * 2**20),
        cost_estimate=pl.CostEstimate(
            flops=2 * count * tokens * width * steps * tile,
            bytes_accessed=4 * tokens * rows,
            transcendentals=0,
        ),
        name="heads_product",
    )(*((grads, weights) if ends else (grads, weights, begun)))


def fill_bias(bias, column, row):
    tile = min(256, bias.shape[0])
    for start in range(0, bias.shape[0], tile):
        shape = (tile, bias.shape[1])
        index = lax.broadcasted_iota(jnp.int32, shape, 0) + start
        allowed = (column[start : start + tile] == row[...].astype(f32)) & (
            lax.broadcasted_iota(jnp.int32, shape, 1) <= index
        )
        bias[start : start + tile] = jnp.where(allowed, 0.0, MASKED)


def key_span(start, block):
    return max(0, start + 1 - LONGEST) // 128 * 128, start + block


def block_probs(queries, key_heads, bias):
    scores = lax.dot_general(queries, key_heads, LANES, preferred_element_type=f32) + bias
    expo = jnp.exp2(scores - jnp.max(scores, -1, keepdims=True))
    return expo * (1.0 / jnp.sum(expo, -1, keepdims=True))


def attend_forward_kernel(
    block,
    query,
    key,
    value,
    cosine,
    sine,
    column,
    row,
    queries,
    key_heads,
    value_heads,
    attended,
    kept,
    bias,
):
    length = query.shape[0]

    @pl.when(pl.program_id(0) == 0)
    def _():
        fill_bias(bias, column, row)

    cosines = jnp.concatenate([cosine[...], cosine[...]], 1)
    sines = jnp.concatenate([-sine[...], sine[...]], 1)

    def turn(values):
        return values * cosines + pltpu.roll(values, HEAD_DIM // 2, 1) * sines

    queries[...] = (turn(query[...]) * (HEAD_DIM ** (-0.5) * LOG2E)).astype(jnp.bfloat16)
    key_heads[...] = turn(key[...]).astype(jnp.bfloat16)
    value_heads[...] = value[...].astype(jnp.bfloat16)
    for start in range(0, length, block):
        first, end = key_span(start, block)
        probs = block_probs(
            queries[start:end], key_heads[first:end], bias[start:end, first:end]
        )
        probs = probs.astype(jnp.bfloat16)
        kept[start:end, first:end] = probs
        result = jnp.dot(probs, value_heads[first:end], preferred_element_type=f32)
        attended[start:end, :] = result.astype(jnp.bfloat16)


def attend_forward(projected, cosine, sine, column, row):
    length, width = projected.shape
    width = width // 3
    heads = width // HEAD_DIM
    block = min(256, length)

    def head(offset):
        return pl.BlockSpec((length, HEAD_DIM), lambda h: (0, h + offset))

    def fixed(array):
        return pl.BlockSpec(array.shape, lambda h: (0, 0))

    return pl.pallas_call(
        functools.partial(attend_forward_kernel, block),
        grid=(heads,),
        out_shape=[jax.ShapeDtypeStruct((length, width), jnp.bfloat16)] * 4
        + [jax.ShapeDtypeStruct((heads, length, length), jnp.bfloat16)],
        in_specs=[head(0), head(heads), head(2 * heads)]
        + [fixed(array) for array in (cosine, sine, column, row)],
        out_specs=[head(0)] * 4 + [pl.BlockSpec((None, length, length), lambda h: (h, 0, 0))],
        scratch_shapes=[pltpu.VMEM((length, length), f32)],
        compiler_params=pltpu.CompilerParams(vmem_limit_bytes=60 * 2**20),
        name="attend_forward",
    )(projected, projected, projected, cosine, sine, column, row)


def attend_back_kernel(
    block,
    queries,
    key_heads,
    value_heads,
    grad_result,
    kept,
    cosine,
    sine,
    grads,
    key_sum,
    value_sum,
):
    length = queries.shape[0]
    key_sum[...] = jnp.zeros_like(key_sum)
    value_sum[...] = jnp.zeros_like(value_sum)

    def turn_back(values, rows, factor):
        values = values * factor
        cosines = jnp.concatenate([cosine[rows], cosine[rows]], 1)
        sines = jnp.concatenate([-sine[rows], sine[rows]], 1)
        return (values * cosines - pltpu.roll(values, HEAD_DIM // 2, 1) * sines).astype(
            jnp.bfloat16
        )

    for start in range(0, length, block):
        first, end = key_span(start, block)
        query, grad_part = queries[start:end], grad_result[start:end]
        lowered = kept[start:end, first:end]
        probs = lowered.astype(f32)
        grad_probs = lax.dot_general(
            grad_part, value_heads[first:end], LANES, preferred_element_type=f32
        )
        row_sum = jnp.sum(probs * grad_probs, -1, keepdims=True)
        grad_scores = (probs * (grad_probs - row_sum)).astype(jnp.bfloat16)
        grad_part_query = jnp.dot(grad_scores, key_heads[first:end], preferred_element_type=f32)
        grads[0, start:end] = turn_back(
            grad_part_query, pl.ds(start, block), HEAD_DIM ** (-0.5)
        )
        key_sum[first:end, :] += lax.dot_general(
            grad_scores, query, ROWS, preferred_element_type=f32
        )
        value_sum[first:end, :] += lax.dot_general(
            lowered, grad_part, ROWS, preferred_element_type=f32
        )
    grads[1] = turn_back(key_sum[...], pl.ds(0, length), 1.0 / LOG2E)
    grads[2] = value_sum[...].astype(jnp.bfloat16)


def attend_back(queries, key_heads, value_heads, grad_result, kept, cosine, sine):
    length, width = queries.shape
    heads = width // HEAD_DIM
    block = min(256, length)
    head = pl.BlockSpec((length, HEAD_DIM), lambda h: (0, h))

    def fixed(array):
        return pl.BlockSpec(array.shape, lambda h: (0, 0))

    return pl.pallas_call(
        functools.partial(attend_back_kernel, block),
        grid=(heads,),
        out_shape=jax.ShapeDtypeStruct((3, length, width), jnp.bfloat16),
        in_specs=[head] * 4
        + [pl.BlockSpec((None, length, length), lambda h: (h, 0, 0)), fixed(cosine), fixed(sine)],
        out_specs=pl.BlockSpec((3, length, HEAD_DIM), lambda h: (0, 0, h)),
        scratch_shapes=[pltpu.VMEM((length, HEAD_DIM), f32)] * 2,
        compiler_params=pltpu.CompilerParams(vmem_limit_bytes=60 * 2**20),
        name="attend_back",
    )(queries, key_heads, value_heads, grad_result, kept, cosine, sine)


def update(weight, grad, moment, average, rate):
    step_grad = grad + DECAY * weight
    moment_new = MOMENTUM * moment + step_grad
    weight_new = weight - rate * (step_grad + MOMENTUM * moment_new)
    return (weight_new, moment_new, average + (weight_new - average) / (STEP + 1))


def hyper_kernel(rate, products, mix, moment, average, new_mix, new_moment, new_average):
    count = mix.shape[1]
    span = range(count)
    square = count * count
    shared = [[products[0, i * count + j] for j in span] for i in span]
    below = [products[0, square + i] for i in span]
    branch = [products[0, square + count + j] for j in span]
    outward = [products[0, square + 2 * count + j] for j in span]
    both = products[0, square + 3 * count]
    start = square + -(-(3 * count + 1) // 8) * 8
    above = [products[0, start + i] for i in span]

    def dot(left, right):
        total = left[0] * right[0]
        for a, b in zip(left[1:], right[1:]):
            total = total + a * b
        return total

    for i in span:
        rows_two = [[mix[1, j, 1 + k] for k in span] for j in span]
        column_one = [mix[0, k, 1 + i] for k in span]
        onto = mix[0, i, 1 + count]
        one = [above[i]]
        one = one + [dot(shared[i], rows_two[j]) + below[i] * mix[1, j, 0] for j in span]
        one.append(dot(rows_two[i], branch) + mix[1, i, 0] * both)
        two = [dot(column_one, below) + onto * both]
        two = two + [
            dot(column_one, [shared[k][j] for k in span]) + onto * branch[j] for j in span
        ]
        two.append(outward[i])
        for layer, grads in ((0, one), (1, two)):
            for j, grad in enumerate(grads):
                at = (layer, i, j)
                results = update(mix[at], grad, moment[at], average[at], rate)
                new_mix[at], new_moment[at], new_average[at] = results


def update_mix(products, mix, moment, average, rate):
    place = pl.BlockSpec(memory_space=SM)
    return pl.pallas_call(
        functools.partial(hyper_kernel, rate),
        out_shape=[jax.ShapeDtypeStruct(mix.shape, f32)] * 3,
        in_specs=[place] * 4,
        out_specs=[place] * 3,
        name="update_mix",
    )(products, mix, moment, average)


def update_kernel(rate, turned, weight, grad, moment, average, *outs):
    value = grad[...].astype(f32)
    results = update(weight[...], value.T if turned else value, moment[...], average[...], rate)
    for out, result in zip(outs, results):
        out[...] = result


def update_blocks(weight, grad, moment, average, rate, start):
    turned = weight.ndim == 2
    parted = grad.ndim == 3
    rows = grad.shape[-2]
    columns = weight.shape[0] if turned else weight.shape[2]
    tile = min(columns, 512)
    tiles = columns // tile
    lead = (None,) if parted else ()

    def spot(k, j):
        return (start + k, 0, j) if parted else (0, start // tile + k * tiles + j)

    if turned:
        grid = (tiles,)
        own = pl.BlockSpec((tile, rows), lambda j: (j, 0))
        place = pl.BlockSpec(lead + (rows, tile), lambda j: spot(0, j))
    else:
        grid = (weight.shape[0], tiles)
        own = pl.BlockSpec((None, rows, tile), lambda k, j: (k, 0, j))
        place = pl.BlockSpec(lead + (rows, tile), spot)
    return pl.pallas_call(
        functools.partial(update_kernel, rate, turned),
        grid=grid,
        out_shape=[jax.ShapeDtypeStruct(weight.shape, f32)] * 3,
        in_specs=[own, place, own, own],
        out_specs=[own] * 3,
        compiler_params=pltpu.CompilerParams(vmem_limit_bytes=60 * 2**20),
        cost_estimate=pl.CostEstimate(
            flops=10 * weight.size, bytes_accessed=26 * weight.size, transcendentals=0
        ),
        name="update",
    )(weight, grad, moment, average)


def tie(*values):
    return lax.optimization_barrier(values)


def line_ways():
    size = lax.axis_size("col")
    up = [(i, i + 1) for i in range(size - 1)]
    down = [(i + 1, i) for i in range(size - 1)]
    return size, up, down


def scatter_steps(partial, low, high):
    size, up, down = line_ways()
    me = lax.axis_index("col")
    width = partial.shape[1] // size

    def share(place):
        return lax.dynamic_slice_in_dim(partial, place * width, width, 1)

    first, last = high, low
    for step in range(1, size):
        if step > 1:
            first = share(jnp.minimum(me + size - step, size - 1)).astype(f32) + first.astype(f32)
            last = share(jnp.maximum(me - size + step, 0)).astype(f32) + last.astype(f32)
            first = first.astype(jnp.bfloat16)
            last = last.astype(jnp.bfloat16)
        first, last = yield (lax.ppermute(first, "col", up), lax.ppermute(last, "col", down))
    yield [first, last]


def advance(steps, got, *values):
    moved = next(steps) if got is None else steps.send(got)
    tied = tie(*moved, *values)
    return tied[: len(moved)], tied[len(moved) :]


def finish_line(steps, got):
    moved = steps.send(got)
    while isinstance(moved, tuple):
        moved = steps.send(moved)
    return moved


def scatter_rows(grad):
    return lax.psum_scatter(grad, "row", scatter_dimension=0, tiled=True)


def pack_kernel(weights, turned, out):
    count, _, columns = weights.shape
    for k in range(count):
        out[:, k * columns : (k + 1) * columns] = weights[k].astype(jnp.bfloat16)
    out[:, count * columns :] = turned[...].T.astype(jnp.bfloat16)


def pack(weights, turned):
    count, rows, columns = weights.shape
    return pl.pallas_call(
        pack_kernel,
        out_shape=jax.ShapeDtypeStruct((rows, count * columns + turned.shape[0]), jnp.bfloat16),
        in_specs=[pl.BlockSpec(memory_space=VM)] * 2,
        out_specs=pl.BlockSpec(memory_space=VM),
        name="pack",
    )(weights, turned)


def per_device(
    streams,
    segments,
    attention_in,
    attention_out,
    gate_up,
    down_weights,
    hyper_mix,
    moment_attention_in,
    moment_attention_out,
    moment_gate_up,
    moment_down_weights,
    moment_hyper_mix,
    average_attention_in,
    average_attention_out,
    average_gate_up,
    average_down_weights,
    average_hyper_mix,
    cotangent,
):
    size = lax.axis_size("col")
    low = jnp.bfloat16
    count, length, width = streams.shape

    attention_weights = lax.all_gather(
        pack(attention_in, attention_out), "row", axis=0, tiled=True
    )
    whole_one, scale_one, grad_two, streams_grads, hidden_weights, column, cosine, sine = norm_in(
        size, streams, cotangent, gate_up, down_weights, segments, hyper_mix
    )
    hidden_weights = lax.all_gather(hidden_weights, "row", axis=0, tiled=True)
    heads = attention_in.shape[2]
    _, up, down = line_ways()
    before = lax.ppermute(grad_two, "col", up)
    after = lax.ppermute(grad_two, "col", down)
    projected = product(whole_one, attention_weights, 0, 3 * heads, f32, heads, "project_in")
    queries, key_heads, value_heads, attended, kept = attend_forward(
        projected, cosine, sine, column, segments
    )
    attended, before, after = tie(attended, before, after)
    whole_two, scale_two, branch_one = norm_mid(
        size, attended, attention_weights, streams, hyper_mix
    )

    active, by_gate, by_upper, partial_two, whole_grad_two = gate_forward(
        size, whole_two, hidden_weights, grad_two, before, after
    )
    branch_two = lax.psum_scatter(partial_two, "col", scatter_dimension=1, tiled=True)
    grad_gated, grad_hidden = gate_back(
        whole_grad_two, whole_two, hidden_weights, by_gate, by_upper, active
    )
    grad_hidden = lax.psum_scatter(grad_hidden, "row", scatter_dimension=1, tiled=True)
    whole_grad_one, inner_two, grad_attended = back_mid(
        size,
        grad_gated,
        hidden_weights,
        cotangent,
        whole_two,
        scale_two,
        attention_weights,
        hyper_mix,
    )

    grad_attended, branch_two = tie(grad_attended, branch_two)
    grad_heads = attend_back(
        queries, key_heads, value_heads, grad_attended, kept, cosine, sine
    )
    tokens_all = length * lax.axis_size("row")
    token_scale = tokens_all ** (-0.5)
    model_rate = D ** (-0.5) * token_scale
    begun, low_share, high_share = heads_product(size, grad_heads, attention_weights)
    partial_one = heads_product(size, grad_heads, attention_weights, begun)
    steps = scatter_steps(partial_one, low_share, high_share)
    grad_attention = outer(
        whole_one, grad_heads, whole_grad_one, attended, name="outer_attention"
    )
    got, (grad_attention,) = advance(steps, None, grad_attention)
    grad_attention = scatter_rows(grad_attention)
    third = update_blocks(gate_up, grad_hidden, moment_gate_up, average_gate_up, model_rate, 0)
    fourth = update_blocks(
        down_weights,
        grad_hidden,
        moment_down_weights,
        average_down_weights,
        FF ** (-0.5) * token_scale,
        gate_up.shape[0],
    )
    got, hidden = advance(steps, got, *third, *fourth)
    third, fourth = hidden[:3], hidden[3:]
    final, other_products = end_streams(
        hyper_mix,
        streams,
        cotangent,
        branch_one,
        branch_two,
        inner_two,
    )
    sums = back_sums(size, partial_one, whole_one)
    got, (other_products, *sums) = advance(steps, got, other_products, *sums)
    first_part, last_part = finish_line(steps, got)
    grad_streams, own_products = back_in(
        hyper_mix,
        partial_one,
        first_part,
        last_part,
        whole_one,
        scale_one,
        sums,
        streams,
        cotangent,
        inner_two,
    )
    products = sum_all(size, streams_grads, other_products, own_products)
    products, grad_attention = tie(products, grad_attention)
    first = update_blocks(
        attention_in, grad_attention, moment_attention_in, average_attention_in, model_rate, 0
    )
    second = update_blocks(
        attention_out,
        grad_attention,
        moment_attention_out,
        average_attention_out,
        model_rate,
        attention_in.shape[0] * heads,
    )
    fifth = update_mix(
        products, hyper_mix, moment_hyper_mix, average_hyper_mix, 0.05 * (tokens_all * D) ** (-0.5)
    )
    return (
        final,
        grad_streams,
        first[0],
        first[1],
        first[2],
        second[0],
        second[1],
        second[2],
        third[0],
        third[1],
        third[2],
        fourth[0],
        fourth[1],
        fourth[2],
        fifth[0],
        fifth[1],
        fifth[2],
    )


def solution(mesh):
    in_specs = (
        P(None, "row", "col"),
        P("row", None),
        P(None, "row", "col"),
        P("col", "row"),
        P(None, "row", "col"),
        P("col", "row"),
        P(),
        P(None, "row", "col"),
        P("col", "row"),
        P(None, "row", "col"),
        P("col", "row"),
        P(),
        P(None, "row", "col"),
        P("col", "row"),
        P(None, "row", "col"),
        P("col", "row"),
        P(),
        P(None, "row", "col"),
    )
    out_specs = (
        P(None, "row", "col"),
        P(None, "row", "col"),
        P(None, "row", "col"),
        P(None, "row", "col"),
        P(None, "row", "col"),
        P("col", "row"),
        P("col", "row"),
        P("col", "row"),
        P(None, "row", "col"),
        P(None, "row", "col"),
        P(None, "row", "col"),
        P("col", "row"),
        P("col", "row"),
        P("col", "row"),
        P(),
        P(),
        P(),
    )
    return jax.shard_map(
        per_device, mesh=mesh, in_specs=in_specs, out_specs=out_specs, check_vma=False
    )
```

```python
import functools

import jax
import jax.numpy as jnp
from jax import lax
from jax.experimental import pallas as pl
from jax.experimental.pallas import tpu as pltpu
from jax.sharding import PartitionSpec as P

D = 2048
HEAD_DIM = 128
FF = 8192
STEP = 8


EPSILON = 1e-05
MASKED = -1e30
MOMENTUM = 0.9
DECAY = 0.01
GROUP = 128
MESH = pl.DeviceIdType.MESH
VM, SM = pltpu.VMEM, pltpu.SMEM
f32 = jnp.float32
LONGEST = 512
LOG2E = 1.4426950408889634
LANES = (((1,), (1,)), ((), ()))
ROWS = (((0,), (0,)), ((), ()))


def line_exchange(
    size, tokens, width, chunk, hop, scatter, gather, produce, prepare, finish, scratch, during=None, rows_too=0
):
    recv, blocks, facts, own_facts, sums_sent, sums_got, blocks_sent, blocks_got, facts_sent, facts_got = scratch
    me = lax.axis_index("col")
    chunks = tokens // chunk
    per_group = GROUP // chunk
    groups = tokens // GROUP
    edge = size - 1

    hop, wait_hop, pass_hop = hop

    def far(place):
        lag = jnp.maximum(place, edge - place) * hop + wait_hop
        return lag if scatter is not None else place * 0

    def remote(source, target, sent, got, device):
        return pltpu.make_async_remote_copy(
            src_ref=source,
            dst_ref=target,
            send_sem=sent,
            recv_sem=got,
            device_id={"col": device},
            device_id_type=MESH,
        )

    def rows(index):
        return pl.ds(pl.multiple_of(index * chunk, chunk), chunk)

    def group_rows(group):
        return pl.ds(pl.multiple_of(group * GROUP, GROUP), GROUP)

    def sum_copy(shard, slot, index, device):
        return remote(
            scatter.at[rows(index), pl.ds(shard * width, width)],
            recv.at[slot, rows(index)],
            sums_sent.at[shard, index],
            sums_got.at[slot, index],
            device,
        )

    def block_copy(place, index, way, device):
        return remote(
            blocks.at[place, rows(index)],
            blocks.at[place, rows(index)],
            blocks_sent.at[way, place, index],
            blocks_got.at[place, index],
            device,
        )

    def fact_copy(place, group, device):
        return remote(
            facts.at[group, pl.ds(pl.multiple_of(place * 8, 8), 8)],
            facts.at[group, pl.ds(pl.multiple_of(place * 8, 8), 8)],
            facts_sent.at[device, group],
            facts_got.at[place, group],
            device,
        )

    right = jnp.minimum(me + 1, edge)
    left = jnp.maximum(me - 1, 0)
    other = jnp.where(me == edge, left, right)

    def inside(index):
        return (index >= 0) & (index < chunks)

    def relay_sum(shard, slot, index, fresh, target):
        columns = slice(shard * width, (shard + 1) * width)

        @pl.when(jnp.logical_not(fresh))
        def _():
            sum_copy(shard, shard, index, other).wait_recv()
            total = scatter[rows(index), columns].astype(f32) + recv[shard, rows(index)].astype(f32)
            scatter[rows(index), columns] = total.astype(jnp.bfloat16)

        sum_copy(shard, slot, index, target).start()

    def relay_sums(step):
        index = step - me * hop

        @pl.when(inside(index))
        def _():
            for shard in range(size - 1, 0, -1):

                @pl.when(shard > me)
                def _():
                    slot = jnp.where(me + 1 == shard, size, shard)
                    relay_sum(shard, slot, index, me == 0, right)

        back = step - (edge - me) * hop

        @pl.when(inside(back))
        def _():
            for shard in range(size - 1):

                @pl.when(shard < me)
                def _():
                    relay_sum(shard, shard, back, me == edge, left)

    def ready(step):
        index = step - far(me)

        @pl.when(inside(index))
        def _():
            if scatter is not None:

                @pl.when(me > 0)
                def _():
                    sum_copy(0, size, index, other).wait_recv()

                @pl.when(me < edge)
                def _():
                    sum_copy(0, me, index, other).wait_recv()

                start = pl.multiple_of(me * width, width)
                total = scatter[rows(index), pl.ds(start, width)].astype(f32)
                total = total + jnp.where(me > 0, recv[size, rows(index)].astype(f32), 0.0)
                total = total + jnp.where(me < edge, recv[me, rows(index)].astype(f32), 0.0)
            else:
                total = None
            columns, block = prepare(rows(index), total)
            lane = lax.broadcasted_iota(jnp.int32, (chunk, 128), 1)
            packed = jnp.zeros((chunk, 128), f32)
            for place, column in enumerate(columns):
                packed = jnp.where(lane == place, column, packed)
            within = lax.rem(index, per_group)
            own_facts[pl.ds(pl.multiple_of(within * chunk, chunk), chunk), :] = packed
            if gather:
                blocks[me, rows(index)] = block

                @pl.when(me < edge)
                def _():
                    block_copy(me, index, 0, right).start()

                @pl.when(me > 0)
                def _():
                    block_copy(me, index, 1, left).start()

            @pl.when(within == per_group - 1)
            def _():
                group = index // per_group
                turned = own_facts[...].T
                facts[group, pl.ds(pl.multiple_of(me * 8, 8), 8), :] = turned[:8]
                for place in range(size):

                    @pl.when(place != me)
                    def _():
                        fact_copy(me, group, place).start()

    def relay_blocks(step):
        for near in range(1, size):
            for way, place in ((0, me - near), (1, me + near)):
                index = step - far(place) - near * pass_hop

                @pl.when((place >= 0) & (place < size) & inside(index))
                def _():
                    block_copy(place, index, way, other).wait_recv()
                    onward = (me < edge) if way == 0 else (me > 0)

                    @pl.when(onward)
                    def _():
                        block_copy(place, index, way, right if way == 0 else left).start()

    longest = (edge * hop + wait_hop if scatter is not None else 0) + edge * pass_hop

    def conclude(step):
        index = step - longest

        @pl.when(inside(index) & (lax.rem(index, per_group) == per_group - 1))
        def _():
            group = index // per_group
            for place in range(size):

                @pl.when(place != me)
                def _():
                    fact_copy(place, group, other).wait_recv()

            finish(group, group_rows(group), facts[group].T)

    barrier = pltpu.get_barrier_semaphore()
    for place in range(size):

        @pl.when(place != me)
        def _():
            pl.semaphore_signal(barrier, inc=1, device_id={"col": place}, device_id_type=MESH)

    line = lax.axis_index("row")
    for place in range(rows_too):

        @pl.when(place != line)
        def _():
            pl.semaphore_signal(barrier, inc=1, device_id={"row": place}, device_id_type=MESH)

    if scatter is not None:
        order = sorted(range(size), key=lambda shard: -max(shard, edge - shard))
        for shard in order:
            produce(group_rows(0), shard, True)
    pl.semaphore_wait(barrier, size - 1 + max(rows_too - 1, 0))

    def step_all(step, carry):
        if scatter is not None:
            relay_sums(step)
        ready(step)
        if gather:
            relay_blocks(step)
        conclude(step)
        if scatter is not None:
            following = step // per_group + 1
            for part in range(per_group):

                @pl.when((following < groups) & (lax.rem(step, per_group) == part))
                def _():
                    for shard in range(part * size // per_group, (part + 1) * size // per_group):
                        produce(group_rows(following), shard, False)

        if during is not None:

            @pl.when(inside(step))
            def _():
                during(rows(step))

        return carry

    lax.fori_loop(0, chunks + longest, step_all, 0)

    def drain(index, carry):
        if scatter is not None:
            for shard in range(size):

                @pl.when(shard != me)
                def _():
                    sum_copy(shard, shard, index, other).wait_send()

        if gather:
            for place in range(size):

                @pl.when((place <= me) & (me < edge))
                def _():
                    block_copy(place, index, 0, other).wait_send()

                @pl.when((place >= me) & (me > 0))
                def _():
                    block_copy(place, index, 1, other).wait_send()

        return carry

    lax.fori_loop(0, chunks, drain, 0)

    def drain_facts(group, carry):
        for place in range(size):

            @pl.when(place != me)
            def _():
                fact_copy(me, group, place).wait_send()

        return carry

    lax.fori_loop(0, groups, drain_facts, 0)


def exchange_scratch(size, tokens, width, chunk, scatter, gather):
    chunks = tokens // chunk
    groups = tokens // GROUP
    dma = pltpu.SemaphoreType.DMA
    tiny = (1, chunk, 128)
    return [
        pltpu.VMEM((size + 1, tokens, width) if scatter else tiny, jnp.bfloat16),
        pltpu.VMEM((size, tokens, width) if gather else tiny, jnp.bfloat16),
        pltpu.VMEM((groups, 128, 128), f32),
        pltpu.VMEM((GROUP, 128), f32),
        dma((size, chunks) if scatter else (1, 1)),
        dma((size + 1, chunks) if scatter else (1, 1)),
        dma((2, size, chunks) if gather else (1, 1, 1)),
        dma((size, chunks) if gather else (1, 1)),
        dma((size, groups)),
        dma((size, groups)),
    ]


def call(body, operands, places, outs, out_places, scratch, name, ident, cost=10**11):
    moved = sum(array.size * array.dtype.itemsize for array in list(operands) + outs)
    return pl.pallas_call(
        body,
        out_shape=outs,
        in_specs=[pl.BlockSpec(memory_space=place) for place in places],
        out_specs=[pl.BlockSpec(memory_space=place) for place in out_places],
        scratch_shapes=scratch,
        compiler_params=pltpu.CompilerParams(
            collective_id=ident, has_side_effects=True, vmem_limit_bytes=60 * 2**20
        ),
        cost_estimate=pl.CostEstimate(flops=cost, bytes_accessed=moved, transcendentals=0),
        name=name,
    )(*operands)


def held(*arrays):
    return [pltpu.VMEM(array.shape, array.dtype) for array in arrays]


def start_loads(pairs, sems):
    copies = [
        pltpu.make_async_copy(source, target, sems.at[place])
        for place, (source, target) in enumerate(pairs)
    ]
    for copy in copies:
        copy.start()
    return copies


def group_store(source, target, sems):
    groups = source.shape[0] // GROUP

    def copy(group):
        rows = pl.ds(pl.multiple_of(group * GROUP, GROUP), GROUP)
        return pltpu.make_async_copy(source.at[rows], target.at[rows], sems.at[group])

    def wait_all():
        def one(group, carry):
            copy(group).wait()
            return carry

        lax.fori_loop(0, groups, one, 0)

    return lambda group: copy(group).start(), wait_all


def norm_stats(value):
    mean = jnp.sum(value, -1, keepdims=True) * (1.0 / value.shape[-1])
    center = value - mean
    return mean, center, jnp.sum(center * center, -1, keepdims=True)


def norm_whole(size, width, turned):
    means = [turned[:, 8 * z : 8 * z + 1] for z in range(size)]
    squares = [turned[:, 8 * z + 1 : 8 * z + 2] for z in range(size)]
    mean = sum(means[1:], means[0]) * (1.0 / size)
    shifts = [own - mean for own in means]
    spread = sum(squares[1:], squares[0])
    for shift in shifts:
        spread = spread + width * shift * shift
    return shifts, lax.rsqrt(spread * (1.0 / (size * width)) + EPSILON)


def norm_finish(size, width, blocks, scale, whole, store):
    def finish(group, rows, turned):
        shifts, rate = norm_whole(size, width, turned)
        scale[rows, :] = rate
        for z in range(size):
            value = (blocks[z, rows].astype(f32) + shifts[z]) * rate
            whole[rows, z * width : (z + 1) * width] = value.astype(jnp.bfloat16)
        store(group)

    return finish


def mixings(mix):
    count = mix.shape[1]
    span = range(count)

    def dot(left, right):
        total = left[0] * right[0]
        for a, b in zip(left[1:], right[1:]):
            total = total + a * b
        return total

    across_one = [[mix[0, k, 1 + i] for i in span] for k in span]
    across_two = [[mix[1, i, 1 + j] for i in span] for j in span]
    through = [[dot(across_one[k], across_two[j]) for j in span] for k in span]
    second = [mix[1, i, 0] for i in span]
    outward = [mix[0, i, 1 + count] for i in span]
    in_two = [dot(across_one[k], second) for k in span]
    out_one = [dot(outward, across_two[j]) for j in span]
    return through, in_two, out_one, dot(outward, second)


def norm_in_kernel(
    size,
    chunk,
    hop,
    mix,
    streams,
    grads_in,
    gate_in,
    down_in,
    documents,
    rates,
    whole_out,
    scale,
    branch_grad,
    products,
    packed,
    column,
    cosine,
    sine,
    whole,
    grads,
    gate_up,
    down,
    loads,
    stores,
    *scratch,
):
    count, tokens, width = streams.shape
    kinds, _, hidden = gate_up.shape
    tile = min(512, hidden)
    tiles = hidden // tile
    into = [mix[0, k, 0] for k in range(count)]
    onto = [mix[1, k, 1 + count] for k in range(count)]
    products[...] = jnp.zeros_like(products)
    waits = start_loads(((grads_in, grads), (gate_in, gate_up), (down_in, down)), loads)
    store, wait_stores = group_store(whole, whole_out, stores)

    def prepare(rows, total):
        mixed = into[0] * streams[0, rows].astype(f32)
        for k in range(1, count):
            mixed = mixed + into[k] * streams[k, rows].astype(f32)
        mean, center, square = norm_stats(mixed)
        return (mean, square), center.astype(jnp.bfloat16)

    def during(rows):
        @pl.when(rows.start == 0)
        def _():
            for wait in waits:
                wait.wait()

        own_docs = documents[:, pl.ds(pl.multiple_of(rows.start // GROUP * GROUP, GROUP), GROUP)]
        turned = jnp.broadcast_to(own_docs.astype(f32), (GROUP, GROUP)).T

        @pl.when(lax.rem(rows.start, GROUP) == 0)
        def _():
            group = pl.ds(pl.multiple_of(rows.start, GROUP), GROUP)
            docs = turned[:, :1]
            shape = (GROUP, tokens)
            index = lax.broadcasted_iota(jnp.int32, shape, 0) + rows.start
            before = lax.broadcasted_iota(jnp.int32, shape, 1) < index
            same = (docs == documents[...].astype(f32)) & before
            place = jnp.sum(jnp.where(same, 1.0, 0.0), -1, keepdims=True)
            angle = place * rates[...]
            column[group, :] = docs
            cosine[group, :] = jnp.cos(angle)
            sine[group, :] = jnp.sin(angle)

        for piece in range((kinds + 1) * tiles):

            @pl.when(rows.start == piece * chunk)
            def _():
                kind, start = piece // tiles, piece % tiles * tile
                if kind < kinds:
                    value = gate_up[kind, :, start : start + tile]
                else:
                    value = down[start : start + tile, :].T
                packed[:, piece * tile : (piece + 1) * tile] = value.astype(jnp.bfloat16)

        above = [grads[k, rows].astype(f32) for k in range(count)]
        value = onto[0] * above[0]
        for k in range(1, count):
            value = value + onto[k] * above[k]
        branch_grad[rows, :] = value.astype(jnp.bfloat16)
        for i in range(count):
            own = streams[i, rows].astype(f32)
            for k in range(count):
                place = i * count + k
                products[place] = products[place] + tile_sum(own * above[k])

    finish = norm_finish(size, width, scratch[1], scale, whole, store)
    line_exchange(
        size, tokens, width, chunk, hop, None, True, None, prepare, finish, scratch, during
    )
    wait_stores()


def norm_in(size, streams, grads, gate_up, down, documents, mix, chunk=64, hop=(1, 0, 1)):
    _, tokens, width = streams.shape
    whole = jax.ShapeDtypeStruct((tokens, size * width), jnp.bfloat16)
    half = HEAD_DIM // 2
    rates = 10000.0 ** (-2.0 * jnp.arange(half).astype(f32) / HEAD_DIM)
    return call(
        functools.partial(norm_in_kernel, size, chunk, hop),
        (mix, streams, grads, gate_up, down, documents, rates[None]),
        (SM, VM, pl.ANY, pl.ANY, pl.ANY, VM, VM),
        [
            whole,
            jax.ShapeDtypeStruct((tokens, 1), f32),
            jax.ShapeDtypeStruct((tokens, width), jnp.bfloat16),
            jax.ShapeDtypeStruct((streams.shape[0] * grads.shape[0], 8, 128), f32),
            jax.ShapeDtypeStruct(
                (gate_up.shape[1], (gate_up.shape[0] + 1) * gate_up.shape[2]), jnp.bfloat16
            ),
            jax.ShapeDtypeStruct((tokens, 1), f32),
            jax.ShapeDtypeStruct((tokens, half), f32),
            jax.ShapeDtypeStruct((tokens, half), f32),
        ],
        (pl.ANY,) + (VM,) * 7,
        held(whole, grads, gate_up, down)
        + [pltpu.SemaphoreType.DMA((3,)), pltpu.SemaphoreType.DMA((tokens // GROUP,))]
        + exchange_scratch(size, tokens, width, chunk, False, True),
        "norm_in",
        1,
    )


def norm_mid_kernel(
    size,
    chunk,
    hop,
    mix,
    attended_in,
    rows_in,
    streams_in,
    whole_out,
    scale,
    branch,
    attended,
    weights,
    streams,
    scatter,
    whole,
    loads,
    stores,
    *scratch,
):
    count, tokens, width = streams.shape
    in_two, turn = mixings(mix)[1::2]
    heads = attended.shape[1]
    own_columns = rows_in.at[:, pl.ds(rows_in.shape[1] - heads, heads)]
    waits = start_loads(
        ((attended_in, attended), (own_columns, weights), (streams_in, streams)), loads
    )
    store, wait_stores = group_store(whole, whole_out, stores)
    waits[0].wait()
    waits[1].wait()

    def produce(rows, shard, first):
        columns = slice(shard * width, (shard + 1) * width)
        scatter[rows, columns] = lax.dot_general(
            attended[rows, :], weights[columns, :], LANES, preferred_element_type=f32
        ).astype(jnp.bfloat16)
        if first and shard == size // 2:
            waits[2].wait()

    def prepare(rows, total):
        branch[rows, :] = total
        mixed = turn * total
        for k in range(count):
            mixed = mixed + in_two[k] * streams[k, rows].astype(f32)
        mean, center, square = norm_stats(mixed)
        return (mean, square), center.astype(jnp.bfloat16)

    finish = norm_finish(size, width, scratch[1], scale, whole, store)
    line_exchange(size, tokens, width, chunk, hop, scatter, True, produce, prepare, finish, scratch)
    wait_stores()


def norm_mid(size, attended, rows, streams, mix, chunk=64, hop=(1, 0, 1)):
    _, tokens, width = streams.shape
    weights = jax.ShapeDtypeStruct((size * width, attended.shape[1]), jnp.bfloat16)
    whole = jax.ShapeDtypeStruct((tokens, size * width), jnp.bfloat16)
    return call(
        functools.partial(norm_mid_kernel, size, chunk, hop),
        (mix, attended, rows, streams),
        (SM, pl.ANY, pl.ANY, pl.ANY),
        [
            whole,
            jax.ShapeDtypeStruct((tokens, 1), f32),
            jax.ShapeDtypeStruct((tokens, width), f32),
        ],
        (pl.ANY, VM, VM),
        held(attended, weights, streams, whole, whole)
        + [pltpu.SemaphoreType.DMA((3,)), pltpu.SemaphoreType.DMA((tokens // GROUP,))]
        + exchange_scratch(size, tokens, width, chunk, True, True),
        "norm_mid",
        2,
    )


def back_mid_kernel(
    size,
    chunk,
    hop,
    mix,
    gated_in,
    rows_in,
    grads_in,
    normal_in,
    scale,
    output_in,
    whole_out,
    inner_out,
    grad_attended,
    gated,
    weights,
    grads,
    whole_normal,
    output_rows,
    scatter,
    inner,
    whole,
    loads,
    stores,
    inner_stores,
    *scratch,
):
    count, tokens, width = grads.shape
    out_one, turn = mixings(mix)[2:]
    blocks = scratch[1]
    hidden = gated.shape[2]
    heads = output_rows.shape[1]
    me = lax.axis_index("col")
    edge = size - 1
    order = sorted(range(size), key=lambda shard: -max(shard, edge - shard))
    pairs = [(gated_in.at[:, pl.ds(0, GROUP)], gated.at[:, pl.ds(0, GROUP)])]
    for shard in order:
        shard_rows = pl.ds(shard * width, width)
        pairs.append((rows_in.at[shard_rows, pl.ds(0, 2 * hidden)], weights.at[shard_rows]))
    rest = pl.ds(GROUP, tokens - GROUP)
    pairs = pairs + [
        (gated_in.at[:, rest], gated.at[:, rest]),
        (grads_in, grads),
        (normal_in, whole_normal),
        (output_in.at[:, pl.ds(output_in.shape[1] - heads, heads)], output_rows),
    ]
    waits = start_loads(pairs, loads)
    store, wait_stores = group_store(whole, whole_out, stores)
    store_inner, wait_inner = group_store(inner, inner_out, inner_stores)
    waits[0].wait()

    def produce(rows, shard, first):
        if first:
            waits[1 + order.index(shard)].wait()
        shard_rows = slice(shard * width, (shard + 1) * width)
        total = lax.dot_general(
            gated[0, rows], weights[shard_rows, :hidden], LANES, preferred_element_type=f32
        )
        total = total + lax.dot_general(
            gated[1, rows], weights[shard_rows, hidden:], LANES, preferred_element_type=f32
        )
        scatter[rows, shard_rows] = total.astype(jnp.bfloat16)
        if first and shard == order[-1]:
            for wait in waits[1 + size :]:
                wait.wait()

    def own_normal(rows):
        return whole_normal[rows, pl.ds(pl.multiple_of(me * width, width), width)].astype(f32)

    def prepare(rows, total):
        inner[rows, :] = total
        normal = own_normal(rows)
        part = 1.0 / width
        first = jnp.sum(total, -1, keepdims=True)
        second = jnp.sum(total * normal, -1, keepdims=True)
        plain = jnp.sum(normal, -1, keepdims=True)
        square = jnp.sum(normal * normal, -1, keepdims=True)
        spread = square - plain * plain * part
        cross = second - first * plain * part
        slope = jnp.where(spread > 1e-3, cross / jnp.maximum(spread, 1e-3), 0.0)
        level = (first - slope * plain) * part
        known = out_one[0] * grads[0, rows].astype(f32)
        for k in range(1, count):
            known = known + out_one[k] * grads[k, rows].astype(f32)
        block = known + (turn * scale[rows, :]) * (total - level - slope * normal)
        return (first, second, level, slope), block.astype(jnp.bfloat16)

    def finish(group, rows, turned):
        first, second = whole_sums(size, width, turned)
        rate = scale[rows, :]
        gain = turn * rate
        for z in range(size):
            level = gain * (turned[:, 8 * z + 2 : 8 * z + 3] - first)
            slope = gain * (turned[:, 8 * z + 3 : 8 * z + 4] - second)
            columns = slice(z * width, (z + 1) * width)
            value = blocks[z, rows].astype(f32) + level
            value = value + slope * whole_normal[rows, columns].astype(f32)
            whole[rows, columns] = value.astype(jnp.bfloat16)
        store(group)
        grad_attended[rows, :] = jnp.dot(
            whole[rows, :], output_rows[...], preferred_element_type=f32
        ).astype(jnp.bfloat16)
        inner[rows, :] = rate * (inner[rows, :] - first - second * own_normal(rows))
        store_inner(group)

    line_exchange(size, tokens, width, chunk, hop, scatter, True, produce, prepare, finish, scratch)
    wait_stores()
    wait_inner()


def whole_sums(size, width, turned):
    first = turned[:, 0:1]
    second = turned[:, 1:2]
    for z in range(1, size):
        first = first + turned[:, 8 * z : 8 * z + 1]
        second = second + turned[:, 8 * z + 1 : 8 * z + 2]
    return first * (1.0 / (size * width)), second * (1.0 / (size * width))


def back_mid(
    size, gated, rows, grads, whole_normal, scale, output_rows, mix, chunk=64, hop=(1, 0, 1)
):
    _, tokens, width = grads.shape
    whole = jax.ShapeDtypeStruct((tokens, size * width), jnp.bfloat16)
    inner = jax.ShapeDtypeStruct((tokens, width), f32)
    groups = tokens // GROUP
    weights = jax.ShapeDtypeStruct((size * width, 2 * gated.shape[2]), jnp.bfloat16)
    heads = output_rows.shape[1] // 4
    output_own = jax.ShapeDtypeStruct((size * width, heads), jnp.bfloat16)
    return call(
        functools.partial(back_mid_kernel, size, chunk, hop),
        (mix, gated, rows, grads, whole_normal, scale, output_rows),
        (SM,) + (pl.ANY,) * 4 + (VM, pl.ANY),
        [whole, inner, jax.ShapeDtypeStruct((tokens, heads), jnp.bfloat16)],
        (pl.ANY, pl.ANY, VM),
        held(gated, weights, grads, whole_normal, output_own, whole, inner, whole)
        + [
            pltpu.SemaphoreType.DMA((size + 5,)),
            pltpu.SemaphoreType.DMA((groups,)),
            pltpu.SemaphoreType.DMA((groups,)),
        ]
        + exchange_scratch(size, tokens, width, chunk, True, True),
        "back_mid",
        3,
        10**9,
    )


def tile_sum(product):
    height, width = product.shape
    folded = jnp.sum(product.reshape(height // 8, 8, width), 0)
    total = folded[:, :128]
    for start in range(128, width, 128):
        total = total + folded[:, start : start + 128]
    return total


def back_sums_kernel(
    size, partial_in, normal_in, first_sum, second_sum, partial, normal, facts, loads, sent, got
):
    tokens, features = partial.shape
    groups = tokens // GROUP
    me = lax.axis_index("col")

    def rows_of(group):
        return pl.ds(pl.multiple_of(group * GROUP, GROUP), GROUP)

    def load(way, group):
        source, target = ((partial_in, partial), (normal_in, normal))[way]
        rows = rows_of(group)
        return pltpu.make_async_copy(source.at[rows], target.at[rows], loads.at[way, group])

    def start_load(group, carry):
        load(0, group).start()
        load(1, group).start()
        return carry

    lax.fori_loop(0, groups, start_load, 0)
    barrier = pltpu.get_barrier_semaphore()
    for member in range(size):

        @pl.when(member != me)
        def _():
            pl.semaphore_signal(barrier, inc=1, device_id={"col": member}, device_id_type=MESH)

    def own(group, carry):
        load(0, group).wait()
        load(1, group).wait()
        rows = rows_of(group)
        total = partial[rows, :].astype(f32)
        one = jnp.sum(total, -1, keepdims=True)
        two = jnp.sum(total * normal[rows, :].astype(f32), -1, keepdims=True)
        lane = lax.broadcasted_iota(jnp.int32, (GROUP, 128), 1)
        packed = jnp.where(lane == 0, one, jnp.where(lane == 1, two, 0.0))
        facts[me, pl.ds(pl.multiple_of(group * 8, 8), 8)] = packed.T[:8]
        return carry

    lax.fori_loop(0, groups, own, 0)
    pl.semaphore_wait(barrier, size - 1)

    def fact_copy(place, member):
        return pltpu.make_async_remote_copy(
            src_ref=facts.at[place],
            dst_ref=facts.at[place],
            send_sem=sent.at[member],
            recv_sem=got.at[place],
            device_id={"col": member},
            device_id_type=MESH,
        )

    for member in range(size):

        @pl.when(member != me)
        def _():
            fact_copy(me, member).start()

    for member in range(size):

        @pl.when(member != me)
        def _():
            fact_copy(member, member).wait()

    def conclude(group, carry):
        fact_rows = pl.ds(pl.multiple_of(group * 8, 8), 8)
        total = facts[0, fact_rows]
        for place in range(1, size):
            total = total + facts[place, fact_rows]
        total = total * (1.0 / features)
        turned = jnp.concatenate([total, jnp.zeros((GROUP - 8, 128), f32)], 0).T
        first_sum[rows_of(group), :] = turned[:, :1]
        second_sum[rows_of(group), :] = turned[:, 1:2]
        return carry

    lax.fori_loop(0, groups, conclude, 0)


def back_sums(size, partial, normal):
    tokens = partial.shape[0]
    dma = pltpu.SemaphoreType.DMA
    return call(
        functools.partial(back_sums_kernel, size),
        (partial, normal),
        (pl.ANY, pl.ANY),
        [jax.ShapeDtypeStruct((tokens, 1), f32)] * 2,
        (VM, VM),
        held(partial, normal)
        + [
            pltpu.VMEM((size, tokens // GROUP * 8, 128), f32),
            dma((2, tokens // GROUP)),
            dma((size,)),
            dma((size,)),
        ],
        "back_sums",
        6,
        10**9,
    )


def back_in_kernel(
    place,
    mix,
    share,
    first,
    last,
    normal,
    scale,
    first_sum,
    second_sum,
    streams,
    grads,
    inner_two,
    out,
    products,
):
    count = streams.shape[0]
    through, in_two, _, _ = mixings(mix)

    @pl.when(pl.program_id(0) == 0)
    def _():
        products[...] = jnp.zeros_like(products)

    width = share.shape[1]

    def slab(index, sums):
        rows = pl.ds(pl.multiple_of(index * 16, 16), 16)
        sums = list(sums)
        shape = (16, 128)
        rate = jnp.broadcast_to(scale[rows, :], shape)
        one = jnp.broadcast_to(first_sum[rows, :], shape)
        two = jnp.broadcast_to(second_sum[rows, :], shape)
        for start in range(0, width, 128):
            columns = slice(start, start + 128)
            total = share[rows, columns].astype(f32) + first[rows, columns].astype(f32)
            total = total + last[rows, columns].astype(f32)
            own = rate * (total - one - two * normal[rows, columns].astype(f32))
            below = inner_two[rows, columns]
            above = [grads[k, rows, columns].astype(f32) for k in range(count)]
            for i in range(count):
                value = in_two[i] * below + mix[0, i, 0] * own
                for k in range(count):
                    value = value + through[i][k] * above[k]
                out[i, rows, columns] = value
                product = streams[i, rows, columns].astype(f32) * own
                sums[i] = sums[i] + product[:8] + product[8:]
        return tuple(sums)

    sums = lax.fori_loop(0, share.shape[0] // 16, slab, (jnp.zeros((8, 128), f32),) * count)
    for i in range(count):
        products[i] = products[i] + sums[i]


def back_in(mix, partial, first, last, normal, scale, sums, streams, grads, inner_two, tile=256):
    count, tokens, width = streams.shape
    used = -(-count // 8) * 8
    many = pl.BlockSpec((count, tile, width), lambda i, place: (0, i, 0))
    here = pl.BlockSpec((tile, width), lambda i, place: (i, place[0]))
    own = pl.BlockSpec((tile, width), lambda i, place: (i, 0))
    thin = pl.BlockSpec((tile, 1), lambda i, place: (i, 0))
    return pl.pallas_call(
        back_in_kernel,
        grid_spec=pltpu.PrefetchScalarGridSpec(
            num_scalar_prefetch=1,
            grid=(tokens // tile,),
            in_specs=[pl.BlockSpec(memory_space=SM), here, own, own, here, thin, thin, thin]
            + [many, many, own],
            out_specs=[many, pl.BlockSpec((used, 8, 128), lambda i, place: (0, 0, 0))],
        ),
        out_shape=[
            jax.ShapeDtypeStruct(streams.shape, f32),
            jax.ShapeDtypeStruct((used, 8, 128), f32),
        ],
        compiler_params=pltpu.CompilerParams(vmem_limit_bytes=60 * 2**20),
        cost_estimate=pl.CostEstimate(
            flops=20 * streams.size, bytes_accessed=11 * streams.size, transcendentals=0
        ),
        name="back_in",
    )(
        lax.axis_index("col").astype(jnp.int32)[None],
        mix,
        partial,
        first,
        last,
        normal,
        scale,
        *sums,
        streams,
        grads,
        inner_two,
    )


def sum_all_kernel(size, *refs):
    parts, whole, shares, sent, got = refs[:-4], refs[-4], refs[-3], refs[-2], refs[-1]
    count_rows = lax.axis_size("row")
    barrier = pltpu.get_barrier_semaphore()
    for axis, members in (("col", size), ("row", count_rows)):
        for member in range(members):

            @pl.when(member != lax.axis_index(axis))
            def _():
                pl.semaphore_signal(
                    barrier, inc=1, device_id={axis: member}, device_id_type=MESH
                )

    total = jnp.concatenate([jnp.sum(jnp.sum(part[...], 1), -1, keepdims=True) for part in parts], 0)
    total = jnp.concatenate([total, jnp.zeros((128 - total.shape[0], 1), f32)], 0)
    total = jnp.broadcast_to(total, (128, 128)).T[:8]
    pl.semaphore_wait(barrier, size - 1 + count_rows - 1)
    for axis, members, base in (("col", size, 0), ("row", count_rows, size)):
        here = lax.axis_index(axis)

        def share_copy(source, member):
            return pltpu.make_async_remote_copy(
                src_ref=shares.at[base + source],
                dst_ref=shares.at[base + source],
                send_sem=sent.at[base + member],
                recv_sem=got.at[base + source],
                device_id={axis: member},
                device_id_type=MESH,
            )

        shares[base + here] = total
        for member in range(members):

            @pl.when(member != here)
            def _():
                share_copy(here, member).start()

        for member in range(members):

            @pl.when(member != here)
            def _():
                share_copy(member, member).wait()

        total = shares[base]
        for member in range(1, members):
            total = total + shares[base + member]
    whole[...] = total


def sum_all(size, *parts):
    members = size + lax.axis_size("row")
    return call(
        functools.partial(sum_all_kernel, size),
        parts,
        (VM,) * len(parts),
        [jax.ShapeDtypeStruct((8, 128), f32)],
        (VM,),
        [
            pltpu.VMEM((members, 8, 128), f32),
            pltpu.SemaphoreType.DMA((members,)),
            pltpu.SemaphoreType.DMA((members,)),
        ],
        "sum_all",
        4,
        10**9,
    )[0]


def end_kernel(mix, streams, grads, branch_one, branch_two, inner_two, final, products):
    count, tokens, width = streams.shape
    through, _, out_one, _ = mixings(mix)
    out_two = [mix[1, j, 1 + count] for j in range(count)]

    @pl.when(pl.program_id(0) == 0)
    def _():
        products[...] = jnp.zeros_like(products)

    def slab(index, sums):
        rows = pl.ds(pl.multiple_of(index * 16, 16), 16)
        sums = list(sums)
        for start in range(0, width, 128):
            columns = slice(start, start + 128)
            values = [streams[i, rows, columns].astype(f32) for i in range(count)]
            above = [grads[i, rows, columns].astype(f32) for i in range(count)]
            one = branch_one[rows, columns]
            two = branch_two[rows, columns].astype(f32)
            below = inner_two[rows, columns]
            for j in range(count):
                value = out_one[j] * one + out_two[j] * two
                for k in range(count):
                    value = value + through[k][j] * values[k]
                final[j, rows, columns] = value.astype(jnp.bfloat16)
            pairs = [(a, below) for a in values]
            pairs = pairs + [(one, b) for b in above]
            pairs = pairs + [(a, two) for a in above]
            pairs = pairs + [(one, below)]
            for place, (a, b) in enumerate(pairs):
                product = a * b
                sums[place] = sums[place] + product[:8] + product[8:]
        return tuple(sums)

    used = 3 * count + 1
    sums = lax.fori_loop(0, tokens // 16, slab, (jnp.zeros((8, 128), f32),) * used)
    for place in range(used):
        products[place] = products[place] + sums[place]


def end_streams(mix, streams, grads, branch_one, branch_two, inner_two, tile=256):
    count, tokens, width = streams.shape
    used = -(-(3 * count + 1) // 8) * 8
    many = pl.BlockSpec((count, tile, width), lambda i: (0, i, 0))
    own = pl.BlockSpec((tile, width), lambda i: (i, 0))
    return pl.pallas_call(
        end_kernel,
        grid=(tokens // tile,),
        out_shape=[
            jax.ShapeDtypeStruct(streams.shape, jnp.bfloat16),
            jax.ShapeDtypeStruct((used, 8, 128), f32),
        ],
        in_specs=[pl.BlockSpec(memory_space=SM), many, many, own, own, own],
        out_specs=[many, pl.BlockSpec((used, 8, 128), lambda i: (0, 0, 0))],
        compiler_params=pltpu.CompilerParams(vmem_limit_bytes=60 * 2**20),
        cost_estimate=pl.CostEstimate(
            flops=60 * streams.size, bytes_accessed=9 * streams.size, transcendentals=0
        ),
        name="end_streams",
    )(mix, streams, grads, branch_one, branch_two, inner_two)


def tiled(body, grid, operands, specs, outs, out_specs, scratch, flops, name):
    moved = sum(array.size * array.dtype.itemsize for array in list(operands) + (list(outs) if isinstance(outs, list) else [outs]))
    return pl.pallas_call(
        body,
        grid=grid,
        out_shape=outs,
        in_specs=specs,
        out_specs=out_specs,
        scratch_shapes=scratch,
        compiler_params=pltpu.CompilerParams(vmem_limit_bytes=60 * 2**20),
        cost_estimate=pl.CostEstimate(flops=flops, bytes_accessed=moved, transcendentals=0),
        name=name,
    )(*operands)


def gate_kernel(
    size,
    steps,
    chunks,
    whole,
    gate_rows,
    upper_rows,
    down_rows,
    own_in,
    before_in,
    after_in,
    active_out,
    by_gate,
    by_upper,
    partial,
    gathered,
    active,
    blocks,
    loads,
    stores,
    sent,
    got,
):
    step = pl.program_id(0)
    me = lax.axis_index("col")
    tiles, tile = active.shape[1] // gate_rows.shape[1], gate_rows.shape[1]
    tokens, width = blocks.shape[1:]
    chunk = tokens // chunks
    edge = size - 1
    right, left = jnp.minimum(me + 1, edge), jnp.maximum(me - 1, 0)
    other = jnp.where(me == edge, left, right)

    def load(place, way):
        source = (own_in, before_in, after_in)[way]
        return pltpu.make_async_copy(source, blocks.at[place], loads.at[way])

    def store(place):
        return pltpu.make_async_copy(
            blocks.at[place],
            gathered.at[:, pl.ds(pl.multiple_of(place * width, width), width)],
            stores.at[place],
        )

    def send(place, index, way, device):
        rows = pl.ds(pl.multiple_of(index * chunk, chunk), chunk)
        return pltpu.make_async_remote_copy(
            src_ref=blocks.at[place, rows],
            dst_ref=blocks.at[place, rows],
            send_sem=sent.at[way, place, index],
            recv_sem=got.at[place, index],
            device_id={"col": device},
            device_id_type=MESH,
        )

    def both_ways(near, act):
        for way, place, target, onward in (
            (0, me - near, right, me < edge),
            (1, me + near, left, me > 0),
        ):

            @pl.when((place >= 0) & (place < size))
            def _():
                act(way, place, target, onward)

    @pl.when(step == 0)
    def _():
        load(me, 0).start()
        both_ways(1, lambda way, place, target, onward: load(place, 1 + way).start())
        barrier = pltpu.get_barrier_semaphore()
        both_ways(
            1,
            lambda way, place, target, onward: pl.semaphore_signal(
                barrier, inc=1, device_id={"col": place}, device_id_type=MESH
            ),
        )
        load(me, 0).wait()
        store(me).start()
        both_ways(1, lambda way, place, target, onward: load(place, 1 + way).wait())

        @pl.when((me > 0) & (me < edge))
        def _():
            pl.semaphore_wait(barrier, 2)

        @pl.when((me == 0) | (me == edge))
        def _():
            pl.semaphore_wait(barrier, 1)


        def begin(way, place, target, onward):
            store(place).start()

            @pl.when(onward)
            def _():
                for index in range(chunks):
                    send(place, index, way, target).start()

        both_ways(1, begin)

    for near in range(2, size - 1):
        index = step - (steps - chunks - (size - 2 - near))

        def forward(way, place, target, onward):
            send(place, index, way, other).wait_recv()

            @pl.when(onward)
            def _():
                send(place, index, way, target).start()

        @pl.when((index >= 0) & (index < chunks))
        def _():
            both_ways(near, forward)

    @pl.when(step < tiles)
    def _():
        gate = jnp.dot(whole[...], gate_rows[...], preferred_element_type=f32)
        upper = jnp.dot(whole[...], upper_rows[...], preferred_element_type=f32)
        sigma = jax.nn.sigmoid(gate)
        silu = gate * sigma
        value = (silu * upper).astype(jnp.bfloat16)
        active_out[...] = value
        active[:, pl.ds(pl.multiple_of(step * tile, tile), tile)] = value
        by_gate[...] = (upper * sigma * (1.0 + gate * (1.0 - sigma))).astype(jnp.bfloat16)
        by_upper[...] = silu.astype(jnp.bfloat16)

    @pl.when(step >= tiles)
    def _():
        partial[...] = lax.dot_general(
            active[...], down_rows[...], LANES, preferred_element_type=f32
        ).astype(jnp.bfloat16)

    @pl.when(step == steps - 1)
    def _():
        def last(way, place, target, onward):
            for index in range(chunks):
                send(place, index, way, other).wait_recv()

        both_ways(size - 1, last)
        for near in range(2, size):
            both_ways(near, lambda way, place, target, onward: store(place).start())

        def sends_done(way, place, target, onward):
            @pl.when(onward)
            def _():
                for index in range(chunks):
                    send(place, index, way, other).wait_send()

        for near in range(1, size - 1):
            both_ways(near, sends_done)
        for place in range(size):
            store(place).wait()


def gate_forward(size, whole, weights, own, before, after, tile=256):
    tokens, features = whole.shape
    hidden = weights.shape[1] // 3
    tile = min(tile, hidden)
    tiles = hidden // tile
    down_tile = min(512, features)
    steps = tiles + features // down_tile
    chunks = 1
    while 2 * chunks <= min(8, steps - size + 3):
        chunks = 2 * chunks
    wide = pl.BlockSpec((tokens, tile), lambda j: (0, jnp.minimum(j, tiles - 1)))
    plain = pl.BlockSpec(memory_space=pl.ANY)
    dma = pltpu.SemaphoreType.DMA
    wide_shape = jax.ShapeDtypeStruct((tokens, hidden), jnp.bfloat16)
    return pl.pallas_call(
        functools.partial(gate_kernel, size, steps, chunks),
        grid=(steps,),
        out_shape=[wide_shape] * 3 + [jax.ShapeDtypeStruct((tokens, features), jnp.bfloat16)] * 2,
        in_specs=[
            pl.BlockSpec((tokens, features), lambda j: (0, 0)),
            pl.BlockSpec((features, tile), lambda j: (0, jnp.minimum(j, tiles - 1))),
            pl.BlockSpec((features, tile), lambda j: (0, tiles + jnp.minimum(j, tiles - 1))),
            pl.BlockSpec((down_tile, hidden), lambda j: (jnp.maximum(j - tiles, 0), 2)),
            plain,
            plain,
            plain,
        ],
        out_specs=[wide] * 3
        + [pl.BlockSpec((tokens, down_tile), lambda j: (0, jnp.maximum(j - tiles, 0))), plain],
        scratch_shapes=[
            pltpu.VMEM((tokens, hidden), jnp.bfloat16),
            pltpu.VMEM((size, tokens, own.shape[1]), jnp.bfloat16),
            dma((3,)),
            dma((size,)),
            dma((2, size, chunks)),
            dma((size, chunks)),
        ],
        compiler_params=pltpu.CompilerParams(
            collective_id=5, has_side_effects=True, vmem_limit_bytes=60 * 2**20
        ),
        cost_estimate=pl.CostEstimate(
            flops=6 * tokens * features * hidden,
            bytes_accessed=2 * weights.size,
            transcendentals=0,
        ),
        name="gate_forward",
    )(whole, weights, weights, weights, own, before, after)


def gate_back_kernel(
    branch_grad, normal, rows, by_gate, by_upper, active, grads, weight_grads, turned_grad, turned
):
    @pl.when(pl.program_id(0) == 0)
    def _():
        turned[...] = normal[...].T
        turned_grad[...] = branch_grad[...].T

    grad = jnp.dot(branch_grad[...], rows[...], preferred_element_type=f32)
    grads[0] = (grad * by_gate[...].astype(f32)).astype(jnp.bfloat16)
    grads[1] = (grad * by_upper[...].astype(f32)).astype(jnp.bfloat16)
    pairs = ((turned, grads.at[0]), (turned, grads.at[1]), (turned_grad, active))
    for place, (left, right) in enumerate(pairs):
        weight_grads[place] = jnp.dot(
            left[...], right[...], preferred_element_type=f32
        ).astype(jnp.bfloat16)


def gate_back(branch_grad, normal, weights, by_gate, by_upper, active, tile=256):
    tokens, features = normal.shape
    hidden = weights.shape[1] // 3
    tile = min(tile, hidden)
    tiles = hidden // tile
    whole = pl.BlockSpec(
        (tokens, features), lambda j: (0, 0), pipeline_mode=pl.Buffered(buffer_count=1)
    )
    part = pl.BlockSpec((tokens, tile), lambda j: (0, j))
    return tiled(
        gate_back_kernel,
        (tiles,),
        (branch_grad, normal, weights, by_gate, by_upper, active),
        [
            whole,
            whole,
            pl.BlockSpec((features, tile), lambda j: (0, 2 * tiles + j)),
            part,
            part,
            part,
        ],
        [
            jax.ShapeDtypeStruct((2, tokens, hidden), jnp.bfloat16),
            jax.ShapeDtypeStruct((3, features, hidden), jnp.bfloat16),
        ],
        [
            pl.BlockSpec((2, tokens, tile), lambda j: (0, 0, j)),
            pl.BlockSpec((3, features, tile), lambda j: (0, 0, j)),
        ],
        [pltpu.VMEM((features, tokens), jnp.bfloat16)] * 2,
        8 * tokens * features * hidden,
        "gate_back",
    )


def outer_kernel(cut, left, right, other_in, other_right, out, turned, other_left, load):
    step = pl.program_id(0)
    fetch = pltpu.make_async_copy(other_in, other_left, load.at[0])

    @pl.when(step == 0)
    def _():
        fetch.start()
        turned[...] = left[...].T

    @pl.when(step == cut)
    def _():
        fetch.wait()
        turned[...] = other_left[...].T

    @pl.when(step < cut)
    def _():
        out[...] = jnp.dot(turned[...], right[...], preferred_element_type=f32).astype(jnp.bfloat16)

    @pl.when(step >= cut)
    def _():
        out[...] = jnp.dot(turned[...], other_right[...], preferred_element_type=f32).astype(
            jnp.bfloat16
        )


def outer(left, right, other_left, other_right, tile=512, name="outer"):
    tokens, rows = left.shape
    tile = min(tile, other_right.shape[1])
    other = other_right.shape[1] // tile
    if right.ndim == 3:
        tiles = right.shape[2] // tile
        cut = right.shape[0] * tiles
        clip = lambda j: jnp.minimum(j, cut - 1)
        spec = pl.BlockSpec((None, tokens, tile), lambda j: (clip(j) // tiles, 0, clip(j) % tiles))
    else:
        cut = right.shape[1] // tile
        spec = pl.BlockSpec((tokens, tile), lambda j: (0, jnp.minimum(j, cut - 1)))
    whole = pl.BlockSpec((tokens, rows), lambda j: (0, 0))
    return tiled(
        functools.partial(outer_kernel, cut),
        (cut + other,),
        (left, right, other_left, other_right),
        [
            whole,
            spec,
            pl.BlockSpec(memory_space=pl.ANY),
            pl.BlockSpec((tokens, tile), lambda j: (0, jnp.maximum(j - cut, 0))),
        ],
        jax.ShapeDtypeStruct((rows, (cut + other) * tile), jnp.bfloat16),
        pl.BlockSpec((rows, tile), lambda j: (0, j)),
        [
            pltpu.VMEM((rows, tokens), jnp.bfloat16),
            pltpu.VMEM((tokens, rows), jnp.bfloat16),
            pltpu.SemaphoreType.DMA((1,)),
        ],
        2 * tokens * rows * (cut + other) * tile,
        name,
    )


def product_kernel(dims, left, right, out):
    total = lax.dot_general(left[...], right[...], dims, preferred_element_type=f32)
    out[...] = total.astype(out.dtype)


def product(left, right, start, columns, kind=jnp.bfloat16, tile=512, name="product"):
    tokens, depth = left.shape
    tile = min(tile, columns)
    first = start // tile
    return tiled(
        functools.partial(product_kernel, (((1,), (0,)), ((), ()))),
        (columns // tile,),
        (left, right),
        [
            pl.BlockSpec((tokens, depth), lambda j: (0, 0)),
            pl.BlockSpec((depth, tile), lambda j: (0, first + j)),
        ],
        jax.ShapeDtypeStruct((tokens, columns), kind),
        pl.BlockSpec((tokens, tile), lambda j: (0, j)),
        [],
        2 * tokens * depth * columns,
        name,
    )


def heads_kernel(ends, grads, rows, *refs):
    width = grads.shape[2]
    total = 0.0
    for k in range(grads.shape[0]):
        total = total + lax.dot_general(
            grads[k], rows[:, k * width : (k + 1) * width], LANES, preferred_element_type=f32
        )
    total = total.astype(jnp.bfloat16)
    if ends:
        out, low, high = refs

        @pl.when(pl.program_id(0) == 0)
        def _():
            low[...] = total

        @pl.when(pl.program_id(0) == 1)
        def _():
            high[...] = total

    else:
        out = refs[1]
    out[...] = total


def heads_product(size, grads, weights, begun=None):
    count, tokens, width = grads.shape
    rows = weights.shape[0]
    tile = rows // size
    ends = begun is None
    place = (lambda j: j * (size - 1)) if ends else (lambda j: j + 1)
    whole = jax.ShapeDtypeStruct((tokens, rows), jnp.bfloat16)
    one = jax.ShapeDtypeStruct((tokens, tile), jnp.bfloat16)
    own = pl.BlockSpec((tokens, tile), lambda j: (0, 0))
    steps = 2 if ends else size - 2
    return pl.pallas_call(
        functools.partial(heads_kernel, ends),
        grid=(steps,),
        out_shape=[whole, one, one] if ends else whole,
        in_specs=[
            pl.BlockSpec((count, tokens, width), lambda j: (0, 0, 0)),
            pl.BlockSpec((tile, count * width), lambda j: (place(j), 0)),
        ]
        + ([] if ends else [pl.BlockSpec(memory_space=pl.ANY)]),
        out_specs=[pl.BlockSpec((tokens, tile), lambda j: (0, place(j))), own, own]
        if ends
        else pl.BlockSpec((tokens, tile), lambda j: (0, place(j))),
        input_output_aliases={} if ends else {2: 0},
        compiler_params=pltpu.CompilerParams(vmem_limit_bytes=60 * 2**20),
        cost_estimate=pl.CostEstimate(
            flops=2 * count * tokens * width * steps * tile,
            bytes_accessed=4 * tokens * rows,
            transcendentals=0,
        ),
        name="heads_product",
    )(*((grads, weights) if ends else (grads, weights, begun)))


def fill_bias(bias, column, row):
    tile = min(256, bias.shape[0])
    for start in range(0, bias.shape[0], tile):
        shape = (tile, bias.shape[1])
        index = lax.broadcasted_iota(jnp.int32, shape, 0) + start
        allowed = (column[start : start + tile] == row[...].astype(f32)) & (
            lax.broadcasted_iota(jnp.int32, shape, 1) <= index
        )
        bias[start : start + tile] = jnp.where(allowed, 0.0, MASKED)


def key_span(start, block):
    return max(0, start + 1 - LONGEST) // 128 * 128, start + block


def block_probs(queries, key_heads, bias):
    scores = lax.dot_general(queries, key_heads, LANES, preferred_element_type=f32) + bias
    expo = jnp.exp2(scores - jnp.max(scores, -1, keepdims=True))
    return expo * (1.0 / jnp.sum(expo, -1, keepdims=True))


def attend_forward_kernel(
    block,
    query,
    key,
    value,
    cosine,
    sine,
    column,
    row,
    queries,
    key_heads,
    value_heads,
    attended,
    kept,
    bias,
):
    length = query.shape[0]

    @pl.when(pl.program_id(0) == 0)
    def _():
        fill_bias(bias, column, row)

    cosines = jnp.concatenate([cosine[...], cosine[...]], 1)
    sines = jnp.concatenate([-sine[...], sine[...]], 1)

    def turn(values):
        return values * cosines + pltpu.roll(values, HEAD_DIM // 2, 1) * sines

    queries[...] = (turn(query[...]) * (HEAD_DIM ** (-0.5) * LOG2E)).astype(jnp.bfloat16)
    key_heads[...] = turn(key[...]).astype(jnp.bfloat16)
    value_heads[...] = value[...].astype(jnp.bfloat16)
    for start in range(0, length, block):
        first, end = key_span(start, block)
        probs = block_probs(
            queries[start:end], key_heads[first:end], bias[start:end, first:end]
        )
        probs = probs.astype(jnp.bfloat16)
        kept[start:end, first:end] = probs
        result = jnp.dot(probs, value_heads[first:end], preferred_element_type=f32)
        attended[start:end, :] = result.astype(jnp.bfloat16)


def attend_forward(projected, cosine, sine, column, row):
    length, width = projected.shape
    width = width // 3
    heads = width // HEAD_DIM
    block = min(256, length)

    def head(offset):
        return pl.BlockSpec((length, HEAD_DIM), lambda h: (0, h + offset))

    def fixed(array):
        return pl.BlockSpec(array.shape, lambda h: (0, 0))

    return pl.pallas_call(
        functools.partial(attend_forward_kernel, block),
        grid=(heads,),
        out_shape=[jax.ShapeDtypeStruct((length, width), jnp.bfloat16)] * 4
        + [jax.ShapeDtypeStruct((heads, length, length), jnp.bfloat16)],
        in_specs=[head(0), head(heads), head(2 * heads)]
        + [fixed(array) for array in (cosine, sine, column, row)],
        out_specs=[head(0)] * 4 + [pl.BlockSpec((None, length, length), lambda h: (h, 0, 0))],
        scratch_shapes=[pltpu.VMEM((length, length), f32)],
        compiler_params=pltpu.CompilerParams(vmem_limit_bytes=60 * 2**20),
        name="attend_forward",
    )(projected, projected, projected, cosine, sine, column, row)


def attend_back_kernel(
    block,
    queries,
    key_heads,
    value_heads,
    grad_result,
    kept,
    cosine,
    sine,
    grads,
    key_sum,
    value_sum,
):
    length = queries.shape[0]
    key_sum[...] = jnp.zeros_like(key_sum)
    value_sum[...] = jnp.zeros_like(value_sum)

    def turn_back(values, rows, factor):
        values = values * factor
        cosines = jnp.concatenate([cosine[rows], cosine[rows]], 1)
        sines = jnp.concatenate([-sine[rows], sine[rows]], 1)
        return (values * cosines - pltpu.roll(values, HEAD_DIM // 2, 1) * sines).astype(
            jnp.bfloat16
        )

    for start in range(0, length, block):
        first, end = key_span(start, block)
        query, grad_part = queries[start:end], grad_result[start:end]
        lowered = kept[start:end, first:end]
        probs = lowered.astype(f32)
        grad_probs = lax.dot_general(
            grad_part, value_heads[first:end], LANES, preferred_element_type=f32
        )
        row_sum = jnp.sum(probs * grad_probs, -1, keepdims=True)
        grad_scores = (probs * (grad_probs - row_sum)).astype(jnp.bfloat16)
        grad_part_query = jnp.dot(grad_scores, key_heads[first:end], preferred_element_type=f32)
        grads[0, start:end] = turn_back(
            grad_part_query, pl.ds(start, block), HEAD_DIM ** (-0.5)
        )
        key_sum[first:end, :] += lax.dot_general(
            grad_scores, query, ROWS, preferred_element_type=f32
        )
        value_sum[first:end, :] += lax.dot_general(
            lowered, grad_part, ROWS, preferred_element_type=f32
        )
    grads[1] = turn_back(key_sum[...], pl.ds(0, length), 1.0 / LOG2E)
    grads[2] = value_sum[...].astype(jnp.bfloat16)


def attend_back(queries, key_heads, value_heads, grad_result, kept, cosine, sine):
    length, width = queries.shape
    heads = width // HEAD_DIM
    block = min(256, length)
    head = pl.BlockSpec((length, HEAD_DIM), lambda h: (0, h))

    def fixed(array):
        return pl.BlockSpec(array.shape, lambda h: (0, 0))

    return pl.pallas_call(
        functools.partial(attend_back_kernel, block),
        grid=(heads,),
        out_shape=jax.ShapeDtypeStruct((3, length, width), jnp.bfloat16),
        in_specs=[head] * 4
        + [pl.BlockSpec((None, length, length), lambda h: (h, 0, 0)), fixed(cosine), fixed(sine)],
        out_specs=pl.BlockSpec((3, length, HEAD_DIM), lambda h: (0, 0, h)),
        scratch_shapes=[pltpu.VMEM((length, HEAD_DIM), f32)] * 2,
        compiler_params=pltpu.CompilerParams(vmem_limit_bytes=60 * 2**20),
        name="attend_back",
    )(queries, key_heads, value_heads, grad_result, kept, cosine, sine)


def update(weight, grad, moment, average, rate):
    step_grad = grad + DECAY * weight
    moment_new = MOMENTUM * moment + step_grad
    weight_new = weight - rate * (step_grad + MOMENTUM * moment_new)
    return (weight_new, moment_new, average + (weight_new - average) / (STEP + 1))


def hyper_kernel(rate, products, mix, moment, average, new_mix, new_moment, new_average):
    count = mix.shape[1]
    span = range(count)
    square = count * count
    shared = [[products[0, i * count + j] for j in span] for i in span]
    below = [products[0, square + i] for i in span]
    branch = [products[0, square + count + j] for j in span]
    outward = [products[0, square + 2 * count + j] for j in span]
    both = products[0, square + 3 * count]
    start = square + -(-(3 * count + 1) // 8) * 8
    above = [products[0, start + i] for i in span]

    def dot(left, right):
        total = left[0] * right[0]
        for a, b in zip(left[1:], right[1:]):
            total = total + a * b
        return total

    for i in span:
        rows_two = [[mix[1, j, 1 + k] for k in span] for j in span]
        column_one = [mix[0, k, 1 + i] for k in span]
        onto = mix[0, i, 1 + count]
        one = [above[i]]
        one = one + [dot(shared[i], rows_two[j]) + below[i] * mix[1, j, 0] for j in span]
        one.append(dot(rows_two[i], branch) + mix[1, i, 0] * both)
        two = [dot(column_one, below) + onto * both]
        two = two + [
            dot(column_one, [shared[k][j] for k in span]) + onto * branch[j] for j in span
        ]
        two.append(outward[i])
        for layer, grads in ((0, one), (1, two)):
            for j, grad in enumerate(grads):
                at = (layer, i, j)
                results = update(mix[at], grad, moment[at], average[at], rate)
                new_mix[at], new_moment[at], new_average[at] = results


def update_mix(products, mix, moment, average, rate):
    place = pl.BlockSpec(memory_space=SM)
    return pl.pallas_call(
        functools.partial(hyper_kernel, rate),
        out_shape=[jax.ShapeDtypeStruct(mix.shape, f32)] * 3,
        in_specs=[place] * 4,
        out_specs=[place] * 3,
        name="update_mix",
    )(products, mix, moment, average)


def update_kernel(rate, turned, weight, grad, moment, average, *outs):
    value = grad[...].astype(f32)
    results = update(weight[...], value.T if turned else value, moment[...], average[...], rate)
    for out, result in zip(outs, results):
        out[...] = result


def update_blocks(weight, grad, moment, average, rate, start):
    turned = weight.ndim == 2
    parted = grad.ndim == 3
    rows = grad.shape[-2]
    columns = weight.shape[0] if turned else weight.shape[2]
    tile = min(columns, 1024 if turned else 2048)
    tiles = columns // tile
    lead = (None,) if parted else ()

    def spot(k, j):
        return (start + k, 0, j) if parted else (0, start // tile + k * tiles + j)

    if turned:
        grid = (tiles,)
        own = pl.BlockSpec((tile, rows), lambda j: (j, 0))
        place = pl.BlockSpec(lead + (rows, tile), lambda j: spot(0, j))
    else:
        grid = (weight.shape[0], tiles)
        own = pl.BlockSpec((None, rows, tile), lambda k, j: (k, 0, j))
        place = pl.BlockSpec(lead + (rows, tile), spot)
    return pl.pallas_call(
        functools.partial(update_kernel, rate, turned),
        grid=grid,
        out_shape=[jax.ShapeDtypeStruct(weight.shape, f32)] * 3,
        in_specs=[own, place, own, own],
        out_specs=[own] * 3,
        compiler_params=pltpu.CompilerParams(vmem_limit_bytes=60 * 2**20),
        cost_estimate=pl.CostEstimate(
            flops=10 * weight.size, bytes_accessed=26 * weight.size, transcendentals=0
        ),
        name="update",
    )(weight, grad, moment, average)


def tie(*values):
    return lax.optimization_barrier(values)


def line_ways():
    size = lax.axis_size("col")
    up = [(i, i + 1) for i in range(size - 1)]
    down = [(i + 1, i) for i in range(size - 1)]
    return size, up, down


def scatter_steps(partial, low, high):
    size, up, down = line_ways()
    me = lax.axis_index("col")
    width = partial.shape[1] // size

    def share(place):
        return lax.dynamic_slice_in_dim(partial, place * width, width, 1)

    first, last = high, low
    for step in range(1, size):
        if step > 1:
            first = share(jnp.minimum(me + size - step, size - 1)).astype(f32) + first.astype(f32)
            last = share(jnp.maximum(me - size + step, 0)).astype(f32) + last.astype(f32)
            first = first.astype(jnp.bfloat16)
            last = last.astype(jnp.bfloat16)
        first, last = yield (lax.ppermute(first, "col", up), lax.ppermute(last, "col", down))
    yield [first, last]


def advance(steps, got, *values):
    moved = next(steps) if got is None else steps.send(got)
    tied = tie(*moved, *values)
    return tied[: len(moved)], tied[len(moved) :]


def finish_line(steps, got):
    moved = steps.send(got)
    while isinstance(moved, tuple):
        moved = steps.send(moved)
    return moved


def scatter_rows(grad):
    return lax.psum_scatter(grad, "row", scatter_dimension=0, tiled=True)


def attention_kernel(rate, last, *refs):
    step = pl.program_id(0)
    into, out = refs[:3], refs[3:6]
    grad, turned_grad = refs[6:8]
    results = refs[8:]

    @pl.when(step < last)
    def _():
        weight, moment, average = [ref[...] for ref in into]
        values = update(weight, grad[...].astype(f32), moment, average, rate)
        for ref, value in zip(results[:3], values):
            ref[...] = value

    @pl.when(step == last)
    def _():
        weight, moment, average = [ref[...] for ref in out]
        values = update(weight, turned_grad[...].astype(f32).T, moment, average, rate)
        for ref, value in zip(results[3:], values):
            ref[...] = value


def update_attention(weight, moment, average, out_weight, out_moment, out_average, grad, rate):
    count, rows, columns = weight.shape
    own = pl.BlockSpec((None, rows, columns), lambda j: (jnp.minimum(j, count - 1), 0, 0))
    whole = pl.BlockSpec(out_weight.shape, lambda j: (0, 0))
    return pl.pallas_call(
        functools.partial(attention_kernel, rate, count),
        grid=(count + 1,),
        out_shape=[jax.ShapeDtypeStruct(weight.shape, f32)] * 3
        + [jax.ShapeDtypeStruct(out_weight.shape, f32)] * 3,
        in_specs=[own] * 3
        + [whole] * 3
        + [
            pl.BlockSpec((rows, columns), lambda j: (0, jnp.minimum(j, count - 1))),
            pl.BlockSpec((rows, columns), lambda j: (0, count)),
        ],
        out_specs=[own] * 3 + [whole] * 3,
        compiler_params=pltpu.CompilerParams(vmem_limit_bytes=60 * 2**20),
        name="update_attention",
    )(weight, moment, average, out_weight, out_moment, out_average, grad, grad)


def pack_kernel(weights, turned, out):
    count, _, columns = weights.shape
    for k in range(count):
        out[:, k * columns : (k + 1) * columns] = weights[k].astype(jnp.bfloat16)
    out[:, count * columns :] = turned[...].T.astype(jnp.bfloat16)


def pack(weights, turned):
    count, rows, columns = weights.shape
    return pl.pallas_call(
        pack_kernel,
        out_shape=jax.ShapeDtypeStruct((rows, count * columns + turned.shape[0]), jnp.bfloat16),
        in_specs=[pl.BlockSpec(memory_space=VM)] * 2,
        out_specs=pl.BlockSpec(memory_space=VM),
        name="pack",
    )(weights, turned)


def per_device(
    streams,
    segments,
    attention_in,
    attention_out,
    gate_up,
    down_weights,
    hyper_mix,
    moment_attention_in,
    moment_attention_out,
    moment_gate_up,
    moment_down_weights,
    moment_hyper_mix,
    average_attention_in,
    average_attention_out,
    average_gate_up,
    average_down_weights,
    average_hyper_mix,
    cotangent,
):
    size = lax.axis_size("col")
    low = jnp.bfloat16
    count, length, width = streams.shape

    attention_weights = lax.all_gather(
        pack(attention_in, attention_out), "row", axis=0, tiled=True
    )
    whole_one, scale_one, grad_two, streams_grads, hidden_weights, column, cosine, sine = norm_in(
        size, streams, cotangent, gate_up, down_weights, segments, hyper_mix
    )
    hidden_weights = lax.all_gather(hidden_weights, "row", axis=0, tiled=True)
    heads = attention_in.shape[2]
    _, up, down = line_ways()
    before = lax.ppermute(grad_two, "col", up)
    after = lax.ppermute(grad_two, "col", down)
    projected = product(whole_one, attention_weights, 0, 3 * heads, f32, heads, "project_in")
    queries, key_heads, value_heads, attended, kept = attend_forward(
        projected, cosine, sine, column, segments
    )
    attended, before, after = tie(attended, before, after)
    whole_two, scale_two, branch_one = norm_mid(
        size, attended, attention_weights, streams, hyper_mix
    )

    active, by_gate, by_upper, partial_two, whole_grad_two = gate_forward(
        size, whole_two, hidden_weights, grad_two, before, after
    )
    branch_two = lax.psum_scatter(partial_two, "col", scatter_dimension=1, tiled=True)
    grad_gated, grad_hidden = gate_back(
        whole_grad_two, whole_two, hidden_weights, by_gate, by_upper, active
    )
    grad_hidden = lax.psum_scatter(grad_hidden, "row", scatter_dimension=1, tiled=True)
    whole_grad_one, inner_two, grad_attended = back_mid(
        size,
        grad_gated,
        hidden_weights,
        cotangent,
        whole_two,
        scale_two,
        attention_weights,
        hyper_mix,
    )

    grad_attended, branch_two = tie(grad_attended, branch_two)
    grad_heads = attend_back(
        queries, key_heads, value_heads, grad_attended, kept, cosine, sine
    )
    tokens_all = length * lax.axis_size("row")
    token_scale = tokens_all ** (-0.5)
    model_rate = D ** (-0.5) * token_scale
    begun, low_share, high_share = heads_product(size, grad_heads, attention_weights)
    partial_one = heads_product(size, grad_heads, attention_weights, begun)
    steps = scatter_steps(partial_one, low_share, high_share)
    grad_attention = outer(
        whole_one, grad_heads, whole_grad_one, attended, name="outer_attention"
    )
    got, (grad_attention,) = advance(steps, None, grad_attention)
    grad_attention = scatter_rows(grad_attention)
    third = update_blocks(gate_up, grad_hidden, moment_gate_up, average_gate_up, model_rate, 0)
    fourth = update_blocks(
        down_weights,
        grad_hidden,
        moment_down_weights,
        average_down_weights,
        FF ** (-0.5) * token_scale,
        gate_up.shape[0],
    )
    got, hidden = advance(steps, got, *third, *fourth)
    third, fourth = hidden[:3], hidden[3:]
    final, other_products = end_streams(
        hyper_mix,
        streams,
        cotangent,
        branch_one,
        branch_two,
        inner_two,
    )
    sums = back_sums(size, partial_one, whole_one)
    got, (other_products, *sums) = advance(steps, got, other_products, *sums)
    first_part, last_part = finish_line(steps, got)
    grad_streams, own_products = back_in(
        hyper_mix,
        partial_one,
        first_part,
        last_part,
        whole_one,
        scale_one,
        sums,
        streams,
        cotangent,
        inner_two,
    )
    products = sum_all(size, streams_grads, other_products, own_products)
    products, grad_attention = tie(products, grad_attention)
    updated = update_attention(
        attention_in,
        moment_attention_in,
        average_attention_in,
        attention_out,
        moment_attention_out,
        average_attention_out,
        grad_attention,
        model_rate,
    )
    first, second = updated[:3], updated[3:]
    fifth = update_mix(
        products, hyper_mix, moment_hyper_mix, average_hyper_mix, 0.05 * (tokens_all * D) ** (-0.5)
    )
    return (
        final,
        grad_streams,
        first[0],
        first[1],
        first[2],
        second[0],
        second[1],
        second[2],
        third[0],
        third[1],
        third[2],
        fourth[0],
        fourth[1],
        fourth[2],
        fifth[0],
        fifth[1],
        fifth[2],
    )


def solution(mesh):
    in_specs = (
        P(None, "row", "col"),
        P("row", None),
        P(None, "row", "col"),
        P("col", "row"),
        P(None, "row", "col"),
        P("col", "row"),
        P(),
        P(None, "row", "col"),
        P("col", "row"),
        P(None, "row", "col"),
        P("col", "row"),
        P(),
        P(None, "row", "col"),
        P("col", "row"),
        P(None, "row", "col"),
        P("col", "row"),
        P(),
        P(None, "row", "col"),
    )
    out_specs = (
        P(None, "row", "col"),
        P(None, "row", "col"),
        P(None, "row", "col"),
        P(None, "row", "col"),
        P(None, "row", "col"),
        P("col", "row"),
        P("col", "row"),
        P("col", "row"),
        P(None, "row", "col"),
        P(None, "row", "col"),
        P(None, "row", "col"),
        P("col", "row"),
        P("col", "row"),
        P("col", "row"),
        P(),
        P(),
        P(),
    )
    return jax.shard_map(
        per_device, mesh=mesh, in_specs=in_specs, out_specs=out_specs, check_vma=False
    )
```
